256 devices in a mesh: seq: 64 (over y, x_hi, z), grp: 4 (over x_lo, core).
Axes of the slice: x: 4 (x_hi: 2, x_lo: 2; x = x_hi * 2 + x_lo), y: 4, z: 8, core: 2. Of those that a mesh axis runs over, the one named last changes fastest.
Arguments:
- tokens: bfloat16 [768, 65536], P('grp', 'seq'), may hold values from -6 to 6
- in_weight: bfloat16 [3, 768, 768], P(None, 'grp'), may hold values from -0.21875 to 0.21875
- short_weight: float32 [3, 3, 768], P(None, None, 'grp'), may hold values from -3.5 to 3.5
- filter_bias: float32 [768], P('grp'), may hold values from -1 to 1
- spectra: float32 [2, 768, 512, 256], P(None, 'grp', 'seq'), may hold values from -12 to 12
- out_weight: bfloat16 [768, 768], P('grp'), may hold values from -0.21875 to 0.21875
Outputs:
- mixed: bfloat16 [768, 65536], P('grp', 'seq')
The draws below stay inside these ranges and needn't reach their ends.
All inputs are finite; a program needn't handle non-finite values.
Results may differ from the reference program's by a relative error of at most 0.019.
Values may be sent and summed in bfloat16 or wider, within the bound.
No kernel may reach another device: no remote copies, remote signals or barrier semaphores. Data moves between devices by JAX's collectives and lax.ppermute only.
A program may use at most 64 MiB of HBM per device.

```python
import jax
import jax.numpy as jnp
from jax import lax

D = 768
QCOLS = 256
TOKENS = 65536
NPAD = 131072
PROWS = 512


def steps_of(key, extent, cuts, least, top_value):
    factor_of = 1.0
    for position, parts in cuts:
        heights = jax.random.uniform(jax.random.fold_in(jax.random.fold_in(key, 6), position), (parts,), jnp.float32, least / len(cuts), top_value / len(cuts))
        factor_of = factor_of * jnp.repeat(jnp.exp(heights), extent[position] // parts).reshape((-1,) + (1,) * (len(extent) - 1 - position))
    return factor_of


def scatter_about(rng, shape, deviation, reach, shards=(), kind=jnp.bfloat16):
    factor_of = steps_of(rng, shape, shards, -0.22, 0.18) if shards else 1.0
    drawn = jax.random.normal(rng, shape, jnp.float32) * deviation * factor_of
    return jnp.minimum(jnp.maximum(drawn, -reach), reach).astype(kind)


def setup_inputs(seed: int = 0) -> dict:
    arg_keys = jax.random.split(jax.random.key(seed), 7)
    return {
        "tokens": scatter_about(arg_keys[0], (D, TOKENS), 1.0, 6.0, ((0, 4), (1, 64))),
        "in_weight": scatter_about(arg_keys[1], (3, D, D), D ** -0.5, 0.21875, ((1, 4),)),
        "short_weight": scatter_about(arg_keys[2], (3, 3, D), 3 ** -0.5, 3.5, ((2, 4),), jnp.float32),
        "filter_bias": jnp.clip(jax.random.uniform(arg_keys[3], (D,), jnp.float32, -1.0, 1.0) * steps_of(arg_keys[3], (D,), ((0, 4),), -0.4, 0.0), -1.0, 1.0),
        "spectra": scatter_about(arg_keys[4], (2, D, PROWS, QCOLS), 2.0, 12.0, ((1, 4), (2, 64)), jnp.float32),
        "out_weight": scatter_about(arg_keys[5], (D, D), D ** -0.5, 0.21875, ((0, 4),)),
    }


def reference(tokens, in_weight, short_weight, filter_bias, spectra, out_weight):
    rows_major = tokens.T
    weight_flat = jnp.transpose(in_weight, (2, 0, 1)).reshape(D, 3 * D)
    projected = jnp.dot(rows_major, weight_flat, preferred_element_type=jnp.float32)
    rounded = lax.optimization_barrier(projected.astype(jnp.bfloat16))
    streams = rounded.reshape(TOKENS, 3, D).astype(jnp.float32)
    padded = jnp.pad(streams, ((2, 0), (0, 0), (0, 0)))
    smooth = short_weight[0] * padded[2:] + short_weight[1] * padded[1:-1] + short_weight[2] * padded[:-2]
    gate_out = smooth[:, 0].astype(jnp.bfloat16)
    signal = (smooth[:, 2] * smooth[:, 1]).astype(jnp.bfloat16)
    signal_wide = signal.astype(jnp.float32)
    block_width = 64

    def conv_block(first_col):
        values = lax.dynamic_slice_in_dim(signal_wide, first_col, block_width, 1)
        response = lax.dynamic_slice_in_dim(spectra, first_col, block_width, 1)
        joined = lax.complex(response[0], response[1])
        joined = jnp.transpose(joined, (2, 1, 0)).reshape(NPAD, block_width)
        forward = jnp.fft.fft(values, n=NPAD, axis=0)
        return jnp.real(jnp.fft.ifft(forward * joined, axis=0))[:TOKENS]

    starts = jnp.arange(D // block_width, dtype=jnp.int32) * block_width
    pieces = lax.map(conv_block, starts)
    convolved = jnp.transpose(pieces, (1, 0, 2)).reshape(TOKENS, D)
    weighted = (gate_out.astype(jnp.float32) * (convolved + filter_bias * signal_wide)).astype(jnp.bfloat16)
    result = jnp.dot(weighted, out_weight, preferred_element_type=jnp.float32).astype(jnp.bfloat16)
    return result.T
```

```python
import math

import jax
import jax.numpy as jnp
import numpy as np
from jax import lax
from jax.experimental import pallas as pl
from jax.experimental.pallas import tpu as pltpu
from jax.sharding import PartitionSpec as P

COLS = 256
FREQS = 512
LANES = 128
BF16 = jnp.bfloat16
F32 = jnp.float32


def unit_circle(rows, cols, period):
    angle = (np.outer(rows, cols) % period) * (2.0 * math.pi / period)
    return np.cos(angle), np.sin(angle)


def transform_tables(shard_count, rows_dev):
    half = shard_count * rows_dev
    order = (np.arange(shard_count)[None, :] * rows_dev + np.arange(rows_dev)[:, None]).reshape(-1)
    freqs = np.arange(2 * half)
    cols = np.arange(COLS)
    padded = 2 * half * COLS
    cos1, sin1 = unit_circle(freqs, order, 2 * half)
    cos2, sin2 = unit_circle(cols, cols, COLS)
    cost, sint = unit_circle(freqs, cols, padded)
    first = np.concatenate([cos1, -sin1], 0)
    forward = np.block([[cos2, -sin2], [sin2, cos2]])
    backward = np.block([[cos2, sin2], [-sin2, cos2]])
    last = np.concatenate([cos1.T, -sin1.T], 1) / padded
    as_bf16 = [jnp.asarray(t, BF16) for t in (first, forward, backward, last)]
    return as_bf16 + [jnp.asarray(t, F32) for t in (cost, sint)]


def pack_spectra_body(spec_ref, out_ref):
    joined = jnp.concatenate([spec_ref[0], spec_ref[1]], axis=1)
    out_ref[...] = joined.reshape(out_ref.shape).astype(BF16)


def pack_spectra(spectra, shard_count):
    _, channels, rows, cols = spectra.shape
    per_dest = channels // shard_count
    steps = 8
    return pl.pallas_call(
        pack_spectra_body,
        grid=(steps,),
        in_specs=[pl.BlockSpec((2, channels // steps, rows, cols), lambda i: (0, i, 0, 0))],
        out_specs=pl.BlockSpec((shard_count // steps, per_dest, 2 * rows, cols), lambda i: (i, 0, 0, 0)),
        out_shape=jax.ShapeDtypeStruct((shard_count, per_dest, 2 * rows, cols), BF16),
        cost_estimate=pl.CostEstimate(flops=0, bytes_accessed=6 * spectra.size, transcendentals=0),
        name="pack_spectra",
    )(spectra)


def project_body(grp_ref, own_ref, far_ref, near_ref, diag_ref, weight_ref, taps_ref,
                 message_ref, signal_ref, gate_ref, token_ref, stream_ref, spread_ref):
    channels = own_ref.shape[0]
    width = own_ref.shape[1]
    grp = grp_ref[0]
    for mask, ref in ((0, own_ref), (2, far_ref), (1, near_ref), (3, diag_ref)):
        start = pl.multiple_of((grp ^ mask) * channels, 64)
        token_ref[pl.ds(start, channels), :] = ref[...]
    step = 384
    for col in range(0, width, step):
        stream_ref[:, col:col + step] = jnp.dot(
            weight_ref[...], token_ref[:, col:col + step], preferred_element_type=F32
        )
    rows = 16

    def chunk(index, carry):
        row = pl.multiple_of(index * rows, rows)
        smooth = []
        for s in range(3):
            x = stream_ref[pl.ds(s * channels + row, rows), :].astype(BF16).astype(F32)
            w = [taps_ref[pl.ds(row, rows), 3 * tap + s:3 * tap + s + 1] for tap in range(3)]
            y = w[0] * x + w[1] * pltpu.roll(x, 1, 1) + w[2] * pltpu.roll(x, 2, 1)
            smooth.append(y[:, LANES:])
        gate_ref[pl.ds(row, rows), :] = smooth[0].astype(BF16)
        signal = smooth[2] * smooth[1]
        signal_ref[pl.ds(row, rows), :] = signal.astype(BF16)
        for part in range(8):
            spread_ref[pl.ds(row * 8 + part, rows, stride=8), :] = signal[:, part * LANES:(part + 1) * LANES]
        return carry

    lax.fori_loop(0, channels // rows, chunk, 0)
    message_ref[...] = spread_ref[...].astype(BF16)


def project(grp, own, far, near, diag, weight, taps):
    channels, width = own.shape
    tok = width - LANES
    vmem = pl.BlockSpec(memory_space=pltpu.VMEM)
    return pl.pallas_call(
        project_body,
        in_specs=[pl.BlockSpec(memory_space=pltpu.SMEM)] + [vmem] * 6,
        out_specs=[vmem] * 3,
        out_shape=[
            jax.ShapeDtypeStruct((channels * 8, LANES), BF16),
            jax.ShapeDtypeStruct((channels, tok), BF16),
            jax.ShapeDtypeStruct((channels, tok), BF16),
        ],
        scratch_shapes=[
            pltpu.VMEM((4 * channels, width), BF16),
            pltpu.VMEM((3 * channels, width), F32),
            pltpu.VMEM((channels * 8, LANES), F32),
        ],
        compiler_params=pltpu.CompilerParams(vmem_limit_bytes=40 << 20),
        cost_estimate=pl.CostEstimate(flops=2 * 3 * channels * 4 * channels * width,
                                      bytes_accessed=6 << 20, transcendentals=0),
        name="project",
    )(grp, own, far, near, diag, weight, taps)


def convolve_body(x_ref, h_ref, first_ref, forward_ref, backward_ref, last_ref, cos_ref, sin_ref,
                  out_ref, spread_ref, grid_ref, mid_ref, tall_ref):
    shards, _, pieces, lanes = x_ref.shape
    rows_dev = pieces // 2
    freqs = cos_ref.shape[0]
    spread_ref[...] = x_ref[...].astype(F32).reshape(shards * pieces, lanes)
    for a in range(rows_dev):
        for h in range(2):
            grid_ref[a * shards:(a + 1) * shards, h * lanes:(h + 1) * lanes] = spread_ref[
                pl.ds(2 * a + h, shards, stride=pieces), :].astype(BF16)
    wave = jnp.dot(first_ref[...], grid_ref[...], preferred_element_type=F32)
    real, imag = wave[:freqs], wave[freqs:]
    cosine, sine = cos_ref[...], sin_ref[...]
    mid_ref[:, :COLS] = (real * cosine + imag * sine).astype(BF16)
    mid_ref[:, COLS:] = (imag * cosine - real * sine).astype(BF16)
    freq = jnp.dot(mid_ref[...], forward_ref[...], preferred_element_type=F32)
    real, imag = freq[:, :COLS], freq[:, COLS:]
    response = h_ref[...].astype(F32)
    half = h_ref.shape[2] // 2
    h_real = response[:, 0, :half].reshape(freqs, COLS)
    h_imag = response[:, 0, half:].reshape(freqs, COLS)
    mid_ref[:, :COLS] = (real * h_real - imag * h_imag).astype(BF16)
    mid_ref[:, COLS:] = (real * h_imag + imag * h_real).astype(BF16)
    back = jnp.dot(mid_ref[...], backward_ref[...], preferred_element_type=F32)
    real, imag = back[:, :COLS], back[:, COLS:]
    tall_ref[:freqs, :] = (real * cosine - imag * sine).astype(BF16)
    tall_ref[freqs:, :] = (imag * cosine + real * sine).astype(BF16)
    out = jnp.dot(last_ref[...], tall_ref[...], preferred_element_type=F32)
    for a in range(rows_dev):
        for h in range(2):
            spread_ref[pl.ds(2 * a + h, shards, stride=pieces), :] = out[
                a * shards:(a + 1) * shards, h * lanes:(h + 1) * lanes]
    out_ref[...] = spread_ref[...].reshape(out_ref.shape).astype(BF16)


def convolve(x, response):
    shards, channels, pieces, lanes = x.shape
    tables = transform_tables(shards, pieces // 2)
    freqs = shards * pieces
    block = pl.BlockSpec((shards, 1, pieces, lanes), lambda c: (0, c, 0, 0))
    whole = [pl.BlockSpec(t.shape, lambda c: (0, 0)) for t in tables]
    return pl.pallas_call(
        convolve_body,
        grid=(channels,),
        in_specs=[block, pl.BlockSpec((shards, 1, *response.shape[2:]), lambda c: (0, c, 0, 0)), *whole],
        out_specs=block,
        out_shape=jax.ShapeDtypeStruct(x.shape, BF16),
        scratch_shapes=[
            pltpu.VMEM((shards * pieces, lanes), F32),
            pltpu.VMEM((freqs // 2, COLS), BF16),
            pltpu.VMEM((freqs, 2 * COLS), BF16),
            pltpu.VMEM((2 * freqs, COLS), BF16),
        ],
        compiler_params=pltpu.CompilerParams(vmem_limit_bytes=40 << 20),
        cost_estimate=pl.CostEstimate(flops=3 << 30, bytes_accessed=6 << 20, transcendentals=0),
        name="convolve",
    )(x, response, *tables)


def gated_body(y_ref, signal_ref, gate_ref, bias_ref, out_ref, spread_ref):
    channels = out_ref.shape[0]
    spread_ref[...] = y_ref[...].astype(F32)
    bias = bias_ref[...]
    for part in range(8):
        cols = slice(part * LANES, (part + 1) * LANES)
        y = spread_ref[pl.ds(part, channels, stride=8), :]
        direct = bias * signal_ref[:, cols].astype(F32)
        out_ref[:, cols] = (gate_ref[:, cols].astype(F32) * (y + direct)).astype(BF16)


def gated(y, signal, gate, bias):
    vmem = pl.BlockSpec(memory_space=pltpu.VMEM)
    return pl.pallas_call(
        gated_body,
        in_specs=[vmem] * 4,
        out_specs=vmem,
        out_shape=jax.ShapeDtypeStruct(signal.shape, BF16),
        scratch_shapes=[pltpu.VMEM(y.shape, F32)],
        cost_estimate=pl.CostEstimate(flops=4 * y.size, bytes_accessed=8 * y.size, transcendentals=0),
        name="gated",
    )(y, signal, gate, bias)


def mixed_body(*refs):
    values, weights, out_ref = refs[:4], refs[4:8], refs[8]
    total = jnp.dot(weights[0][...], values[0][...], preferred_element_type=F32)
    for w, v in zip(weights[1:], values[1:]):
        total = total + jnp.dot(w[...], v[...], preferred_element_type=F32)
    out_ref[...] = total.astype(BF16)


def mixed(values, weights):
    vmem = pl.BlockSpec(memory_space=pltpu.VMEM)
    channels, tok = values[0].shape
    return pl.pallas_call(
        mixed_body,
        in_specs=[vmem] * 8,
        out_specs=vmem,
        out_shape=jax.ShapeDtypeStruct((weights[0].shape[0], tok), BF16),
        compiler_params=pltpu.CompilerParams(vmem_limit_bytes=32 << 20),
        cost_estimate=pl.CostEstimate(flops=8 * channels * channels * tok, bytes_accessed=3 << 20, transcendentals=0),
        name="mixed",
    )(*values, *weights)


def swapped(block, mask):
    return lax.ppermute(block, "grp", [(i, i ^ mask) for i in range(4)])


def gathered(block):
    far = swapped(block, 2)
    near = swapped(block, 1)
    return block, far, near, swapped(far, 1)


def shards(tokens, in_weight, short_weight, filter_bias, spectra, out_weight):
    shard_count = lax.axis_size("seq")
    grp = lax.axis_index("grp")
    channels, tok = tokens.shape
    per_dest = channels // shard_count

    packed = pack_spectra(spectra, shard_count)
    packed, tokens = lax.optimization_barrier((packed, tokens))
    response = lax.all_to_all(packed, "seq", 0, 0, tiled=True)

    route = [(i, i + 1) for i in range(shard_count - 1)]
    halo = lax.ppermute(tokens[:, -LANES:], "seq", route)
    extended = gathered(jnp.concatenate([halo, tokens], 1))
    taps = jnp.transpose(short_weight, (2, 0, 1)).reshape(channels, 9)
    message, signal, gate = project(
        grp.reshape(1).astype(jnp.int32), *extended, in_weight.reshape(3 * channels, -1), taps
    )
    turned = out_weight.T
    parts = [
        lax.dynamic_slice_in_dim(turned, (grp ^ mask) * channels, channels, 0) for mask in range(4)
    ]
    weights = [parts[0]] + [swapped(parts[m], m) for m in (2, 1, 3)]
    message, response, *weights = lax.optimization_barrier((message, response, *weights))
    columns = lax.all_to_all(
        message.reshape(shard_count, per_dest, 8, LANES), "seq", 0, 0, tiled=True
    )
    result = convolve(columns, response)
    back = lax.all_to_all(result, "seq", 0, 0, tiled=True).reshape(channels * 8, LANES)

    weighted = gated(back, signal, gate, filter_bias[:, None])
    return mixed(gathered(weighted), weights)


def solution(mesh):
    in_specs = (
        P("grp", "seq"),
        P(None, "grp", None),
        P(None, None, "grp"),
        P("grp"),
        P(None, "grp", "seq", None),
        P("grp", None),
    )
    out_specs = P("grp", "seq")
    return jax.shard_map(shards, mesh=mesh, in_specs=in_specs, out_specs=out_specs, check_vma=False)
```

```python
import math

import jax
import jax.numpy as jnp
import numpy as np
from jax import lax
from jax.experimental import pallas as pl
from jax.experimental.pallas import tpu as pltpu
from jax.sharding import PartitionSpec as P

COLS = 256
FREQS = 512
LANES = 128
BF16 = jnp.bfloat16
F32 = jnp.float32


def unit_circle(rows, cols, period):
    angle = (np.outer(rows, cols) % period) * (2.0 * math.pi / period)
    return np.cos(angle), np.sin(angle)


def transform_tables(shard_count, rows_dev):
    half = shard_count * rows_dev
    order = (np.arange(shard_count)[None, :] * rows_dev + np.arange(rows_dev)[:, None]).reshape(-1)
    freqs = np.arange(2 * half)
    cols = np.arange(COLS)
    padded = 2 * half * COLS
    cos1, sin1 = unit_circle(freqs, order, 2 * half)
    cos2, sin2 = unit_circle(cols, cols, COLS)
    cost, sint = unit_circle(freqs, cols, padded)
    first = np.concatenate([cos1, -sin1], 1)
    forward = np.block([[cos2, -sin2], [sin2, cos2]])
    backward = np.block([[cos2, sin2], [-sin2, cos2]])
    last = np.concatenate([cos1.T, -sin1.T], 0) / padded
    waves = np.concatenate([first, forward, backward, last], 0)
    return jnp.asarray(waves, BF16), jnp.asarray(np.concatenate([cost, sint], 1), F32)


def pack_spectra(spectra, shard_count):
    _, channels, rows, cols = spectra.shape
    grouped = spectra.reshape(2, shard_count, channels // shard_count, rows, cols)
    by_dest = jnp.transpose(grouped, (1, 2, 0, 3, 4)).astype(BF16)
    return by_dest.reshape(shard_count, channels // shard_count, 2 * rows, cols)


def project_body(grp_ref, own_ref, far_ref, near_ref, diag_ref, weight_ref, taps_ref,
                 message_ref, signal_ref, gate_ref, token_ref, stream_ref, spread_ref):
    channels = own_ref.shape[0]
    width = own_ref.shape[1]
    grp = grp_ref[0]
    for mask, ref in ((0, own_ref), (2, far_ref), (1, near_ref), (3, diag_ref)):
        start = pl.multiple_of((grp ^ mask) * channels, 64)
        token_ref[pl.ds(start, channels), :] = ref[...]
    step = 384
    for col in range(0, width, step):
        stream_ref[:, col:col + step] = jnp.dot(
            weight_ref[...], token_ref[:, col:col + step], preferred_element_type=F32
        )
    rows = 16

    def chunk(index, carry):
        row = pl.multiple_of(index * rows, rows)
        smooth = []
        for s in range(3):
            x = stream_ref[pl.ds(s * channels + row, rows), :].astype(BF16).astype(F32)
            w = [taps_ref[pl.ds(row, rows), 3 * tap + s:3 * tap + s + 1] for tap in range(3)]
            y = w[0] * x + w[1] * pltpu.roll(x, 1, 1) + w[2] * pltpu.roll(x, 2, 1)
            smooth.append(y[:, LANES:])
        gate_ref[pl.ds(row, rows), :] = smooth[0].astype(BF16)
        signal = smooth[2] * smooth[1]
        signal_ref[pl.ds(row, rows), :] = signal.astype(BF16)
        for part in range(8):
            spread_ref[pl.ds(row * 8 + part, rows, stride=8), :] = signal[:, part * LANES:(part + 1) * LANES]
        return carry

    lax.fori_loop(0, channels // rows, chunk, 0)
    message_ref[...] = spread_ref[...].astype(BF16)


def project(grp, own, far, near, diag, weight, taps):
    channels, width = own.shape
    tok = width - LANES
    vmem = pl.BlockSpec(memory_space=pltpu.VMEM)
    return pl.pallas_call(
        project_body,
        in_specs=[pl.BlockSpec(memory_space=pltpu.SMEM)] + [vmem] * 6,
        out_specs=[vmem] * 3,
        out_shape=[
            jax.ShapeDtypeStruct((channels * 8, LANES), BF16),
            jax.ShapeDtypeStruct((channels, tok), BF16),
            jax.ShapeDtypeStruct((channels, tok), BF16),
        ],
        scratch_shapes=[
            pltpu.VMEM((4 * channels, width), BF16),
            pltpu.VMEM((3 * channels, width), F32),
            pltpu.VMEM((channels * 8, LANES), F32),
        ],
        compiler_params=pltpu.CompilerParams(vmem_limit_bytes=20 << 20),
        cost_estimate=pl.CostEstimate(flops=2 * 3 * channels * 4 * channels * width,
                                      bytes_accessed=6 << 20, transcendentals=0),
        name="project",
    )(grp, own, far, near, diag, weight, taps)


def convolve_body(x_ref, h_ref, wave_ref, twist_ref, out_ref,
                  spread_ref, grid_ref, mid_ref, tall_ref, done_ref, sems):
    shards, channels, pieces, lanes = x_ref.shape
    rows_dev = pieces // 2
    freqs = twist_ref.shape[0]
    half = h_ref.shape[2] // 2
    first_ref, forward_ref, backward_ref = (wave_ref.at[pl.ds(i * freqs, freqs)] for i in range(3))
    last = 3 * freqs
    for c in range(channels):
        spread_ref[...] = x_ref[:, c].astype(F32).reshape(shards * pieces, lanes)
        for a in range(rows_dev):
            for h in range(2):
                grid_ref[a * shards:(a + 1) * shards, h * lanes:(h + 1) * lanes] = spread_ref[
                    pl.ds(2 * a + h, shards, stride=pieces), :].astype(BF16)
        real = jnp.dot(first_ref[:, :COLS], grid_ref[...], preferred_element_type=F32)
        imag = jnp.dot(first_ref[:, COLS:], grid_ref[...], preferred_element_type=F32)
        cosine, sine = twist_ref[:, :COLS], twist_ref[:, COLS:]
        mid_ref[:, :COLS] = (real * cosine + imag * sine).astype(BF16)
        mid_ref[:, COLS:] = (imag * cosine - real * sine).astype(BF16)
        freq = jnp.dot(mid_ref[...], forward_ref[...], preferred_element_type=F32)
        real, imag = freq[:, :COLS], freq[:, COLS:]
        response = h_ref[:, c].astype(F32)
        h_real = response[:, :half].reshape(freqs, COLS)
        h_imag = response[:, half:].reshape(freqs, COLS)
        mid_ref[:, :COLS] = (real * h_real - imag * h_imag).astype(BF16)
        mid_ref[:, COLS:] = (real * h_imag + imag * h_real).astype(BF16)
        back = jnp.dot(mid_ref[...], backward_ref[...], preferred_element_type=F32)
        real, imag = back[:, :COLS], back[:, COLS:]
        tall_ref[:freqs, :] = (real * cosine - imag * sine).astype(BF16)
        tall_ref[freqs:, :] = (imag * cosine + real * sine).astype(BF16)
        out = jnp.dot(wave_ref[last:last + COLS, :], tall_ref[:freqs], preferred_element_type=F32)
        out += jnp.dot(wave_ref[last + COLS:, :], tall_ref[freqs:], preferred_element_type=F32)
        for a in range(rows_dev):
            for h in range(2):
                spread_ref[pl.ds(2 * a + h, shards, stride=pieces), :] = out[
                    a * shards:(a + 1) * shards, h * lanes:(h + 1) * lanes]
        done_ref[c] = spread_ref[...].reshape(shards, pieces, lanes).astype(BF16)
        pltpu.make_async_copy(done_ref.at[c], out_ref.at[:, c], sems.at[c]).start()
    for c in range(channels):
        pltpu.make_async_copy(done_ref.at[c], out_ref.at[:, c], sems.at[c]).wait()


def convolve(x, response, tables):
    shards, channels, pieces, lanes = x.shape
    freqs = shards * pieces
    vmem = pl.BlockSpec(memory_space=pltpu.VMEM)
    return pl.pallas_call(
        convolve_body,
        in_specs=[vmem] * (2 + len(tables)),
        out_specs=pl.BlockSpec(memory_space=pl.ANY),
        out_shape=jax.ShapeDtypeStruct(x.shape, BF16),
        scratch_shapes=[
            pltpu.VMEM((shards * pieces, lanes), F32),
            pltpu.VMEM((freqs // 2, COLS), BF16),
            pltpu.VMEM((freqs, 2 * COLS), BF16),
            pltpu.VMEM((2 * freqs, COLS), BF16),
            pltpu.VMEM((channels, shards, pieces, lanes), BF16),
            pltpu.SemaphoreType.DMA((channels,)),
        ],
        compiler_params=pltpu.CompilerParams(vmem_limit_bytes=24 << 20),
        cost_estimate=pl.CostEstimate(flops=3 << 30, bytes_accessed=6 << 20, transcendentals=0),
        name="convolve",
    )(x, response, *tables)


def gated_body(y_ref, signal_ref, gate_ref, bias_ref, out_ref, spread_ref):
    channels = out_ref.shape[0]
    spread_ref[...] = y_ref[...].astype(F32)
    bias = bias_ref[...]
    for part in range(8):
        cols = slice(part * LANES, (part + 1) * LANES)
        y = spread_ref[pl.ds(part, channels, stride=8), :]
        direct = bias * signal_ref[:, cols].astype(F32)
        out_ref[:, cols] = (gate_ref[:, cols].astype(F32) * (y + direct)).astype(BF16)


def gated(y, signal, gate, bias):
    vmem = pl.BlockSpec(memory_space=pltpu.VMEM)
    return pl.pallas_call(
        gated_body,
        in_specs=[vmem] * 4,
        out_specs=vmem,
        out_shape=jax.ShapeDtypeStruct(signal.shape, BF16),
        scratch_shapes=[pltpu.VMEM(y.shape, F32)],
        compiler_params=pltpu.CompilerParams(vmem_limit_bytes=8 << 20),
        cost_estimate=pl.CostEstimate(flops=4 * y.size, bytes_accessed=8 * y.size, transcendentals=0),
        name="gated",
    )(y, signal, gate, bias)


def mixed_body(*refs):
    values, weights, out_ref = refs[:4], refs[4:8], refs[8]
    total = jnp.dot(weights[0][...], values[0][...], preferred_element_type=F32)
    for w, v in zip(weights[1:], values[1:]):
        total = total + jnp.dot(w[...], v[...], preferred_element_type=F32)
    out_ref[...] = total.astype(BF16)


def mixed(values, weights):
    vmem = pl.BlockSpec(memory_space=pltpu.VMEM)
    channels, tok = values[0].shape
    return pl.pallas_call(
        mixed_body,
        in_specs=[vmem] * 8,
        out_specs=vmem,
        out_shape=jax.ShapeDtypeStruct((weights[0].shape[0], tok), BF16),
        compiler_params=pltpu.CompilerParams(vmem_limit_bytes=12 << 20),
        cost_estimate=pl.CostEstimate(flops=8 * channels * channels * tok, bytes_accessed=3 << 20, transcendentals=0),
        name="mixed",
    )(*values, *weights)


def swapped(block, mask):
    return lax.ppermute(block, "grp", [(i, i ^ mask) for i in range(4)])


def gathered(block):
    far = swapped(block, 2)
    near = swapped(block, 1)
    return block, far, near, swapped(far, 1)


def shards(tokens, in_weight, short_weight, filter_bias, spectra, out_weight):
    shard_count = lax.axis_size("seq")
    grp = lax.axis_index("grp")
    channels, tok = tokens.shape
    per_dest = channels // shard_count

    route = [(i, i + 1) for i in range(shard_count - 1)]
    halo = lax.ppermute(tokens[:, -LANES:], "seq", route)
    packed = pack_spectra(spectra, shard_count)
    packed, halo = lax.optimization_barrier((packed, halo))
    response = lax.all_to_all(packed, "seq", 0, 0, tiled=True)

    extended = gathered(jnp.concatenate([halo, tokens], 1))
    taps = jnp.transpose(short_weight, (2, 0, 1)).reshape(channels, 9)
    message, signal, gate = project(
        grp.reshape(1).astype(jnp.int32), *extended, in_weight.reshape(3 * channels, -1), taps
    )
    turned = out_weight.T
    parts = [
        lax.dynamic_slice_in_dim(turned, (grp ^ mask) * channels, channels, 0) for mask in range(4)
    ]
    weights = [parts[0]] + [swapped(parts[m], m) for m in (2, 1, 3)]
    zero = jnp.minimum(grp, 0)
    tables = [t + zero.astype(t.dtype) for t in transform_tables(shard_count, tok // COLS)]
    bias = filter_bias[:, None] + zero.astype(F32)
    message, response, weights, tables, bias = lax.optimization_barrier(
        (message, response, weights, tables, bias)
    )
    columns = lax.all_to_all(
        message.reshape(shard_count, per_dest, 8, LANES), "seq", 0, 0, tiled=True
    )
    result = convolve(columns, response, tables)
    back = lax.all_to_all(result, "seq", 0, 0, tiled=True).reshape(channels * 8, LANES)

    weighted = gated(back, signal, gate, bias)
    return mixed(gathered(weighted), weights)


def solution(mesh):
    in_specs = (
        P("grp", "seq"),
        P(None, "grp", None),
        P(None, None, "grp"),
        P("grp"),
        P(None, "grp", "seq", None),
        P("grp", None),
    )
    out_specs = P("grp", "seq")
    return jax.shard_map(shards, mesh=mesh, in_specs=in_specs, out_specs=out_specs, check_vma=False)
```

```python
import math

import jax
import jax.numpy as jnp
import numpy as np
from jax import lax
from jax.experimental import pallas as pl
from jax.experimental.pallas import tpu as pltpu
from jax.sharding import PartitionSpec as P

COLS = 256
FREQS = 512
LANES = 128
PROJECT_VMEM = 54000 << 10
CONVOLVE_VMEM = 50000 << 10
MASKS = (0, 2, 1, 3)
BF16 = jnp.bfloat16
F32 = jnp.float32


def unit_circle(rows, cols, period):
    angle = (np.outer(rows, cols) % period) * (2.0 * math.pi / period)
    return np.cos(angle), np.sin(angle)


def transform_tables(shard_count, rows_dev):
    half = shard_count * rows_dev
    order = (np.arange(shard_count)[None, :] * rows_dev + np.arange(rows_dev)[:, None]).reshape(-1)
    freqs = np.arange(2 * half)
    cols = np.arange(COLS)
    padded = 2 * half * COLS
    cos1, sin1 = unit_circle(freqs, order, 2 * half)
    cos2, sin2 = unit_circle(cols, cols, COLS)
    cost, sint = unit_circle(freqs, cols, padded)
    first = np.concatenate([cos1, -sin1], 1)
    forward = np.block([[cos2, -sin2], [sin2, cos2]])
    backward = np.block([[cos2, sin2], [-sin2, cos2]])
    last = np.concatenate([cos1.T, -sin1.T], 0) / padded
    waves = np.concatenate([first, forward, backward, last], 0)
    return jnp.asarray(waves, BF16), jnp.asarray(np.concatenate([cost, sint], 1), F32)


def pack_spectra_body(spec_ref, out_ref):
    dests = out_ref.shape[0]
    per_dest = spec_ref.shape[1] // dests
    for part in range(2):
        for h in range(2):
            piece = spec_ref[part, :, :, h * LANES:(h + 1) * LANES]
            piece = piece.reshape(dests, per_dest, *piece.shape[1:]).astype(BF16)
            for c in range(per_dest):
                out_ref[:, 4 * c + 2 * part + h] = piece[:, c]


def pack_spectra(spectra, shard_count):
    _, channels, rows, cols = spectra.shape
    per_dest = channels // shard_count
    steps = 2
    return pl.pallas_call(
        pack_spectra_body,
        grid=(steps,),
        in_specs=[pl.BlockSpec((2, channels // steps, rows, cols), lambda i: (0, i, 0, 0))],
        out_specs=pl.BlockSpec((shard_count // steps, 4 * per_dest, rows, LANES), lambda i: (i, 0, 0, 0)),
        out_shape=jax.ShapeDtypeStruct((shard_count, 5 * per_dest, rows, LANES), BF16),
        cost_estimate=pl.CostEstimate(flops=0, bytes_accessed=6 * spectra.size, transcendentals=0),
        name="pack_spectra",
    )(spectra)


def project_body(*refs):
    grp_ref, mains, halos, weight_ref, taps_ref = refs[0], refs[1:5], refs[5:9], refs[9], refs[10]
    message_ref, kept_ref, token_ref, stream_ref, spread_ref, part_ref, sem = refs[12:]
    channels, tok = mains[0].shape
    width = tok + LANES
    grp = grp_ref[0]
    for mask, main, halo in zip(MASKS, mains, halos):
        rows = pl.ds(pl.multiple_of((grp ^ mask) * channels, 64), channels)
        token_ref[rows, :LANES] = halo[...]
        token_ref[rows, LANES:] = main[...]
    step = 384
    for col in range(0, width, step):
        stream_ref[:, col:col + step] = jnp.dot(
            weight_ref[...], token_ref[:, col:col + step], preferred_element_type=F32
        )
    rows = 16

    def chunk(index, carry):
        row = pl.multiple_of(index * rows, rows)
        smooth = []
        for s in range(3):
            x = stream_ref[pl.ds(s * channels + row, rows), :].astype(BF16).astype(F32)
            w = [taps_ref[pl.ds(row, rows), 3 * tap + s:3 * tap + s + 1] for tap in range(3)]
            y = w[0] * x + w[1] * pltpu.roll(x, 1, 1) + w[2] * pltpu.roll(x, 2, 1)
            smooth.append(y[:, LANES:])
        kept_ref[0, pl.ds(row, rows), :] = smooth[0].astype(BF16)
        signal = smooth[2] * smooth[1]
        kept_ref[1, pl.ds(row, rows), :] = signal.astype(BF16)
        for part in range(8):
            spread_ref[pl.ds(row * 8 + part, rows, stride=8), :] = signal[:, part * LANES:(part + 1) * LANES]
        return carry

    lax.fori_loop(0, channels // rows, chunk, 0)
    part_ref[...] = spread_ref[...].reshape(part_ref.shape).astype(BF16)
    per_dest = part_ref.shape[1]
    copy = pltpu.make_async_copy(part_ref, message_ref.at[:, pl.ds(4 * per_dest, per_dest)], sem)
    copy.start()
    copy.wait()


def project(grp, mains, halos, weight, taps, packed):
    channels, tok = mains[0].shape
    width = tok + LANES
    vmem = pl.BlockSpec(memory_space=pltpu.VMEM)
    anywhere = pl.BlockSpec(memory_space=pltpu.HBM)
    shards, pieces = packed.shape[:2]
    return pl.pallas_call(
        project_body,
        in_specs=[pl.BlockSpec(memory_space=pltpu.SMEM)] + [vmem] * 10 + [anywhere],
        out_specs=[anywhere, vmem],
        out_shape=[
            jax.ShapeDtypeStruct(packed.shape, BF16),
            jax.ShapeDtypeStruct((2, channels, tok), BF16),
        ],
        scratch_shapes=[
            pltpu.VMEM((4 * channels, width), BF16),
            pltpu.VMEM((3 * channels, width), F32),
            pltpu.VMEM((channels * 8, LANES), F32),
            pltpu.VMEM((shards, pieces // 5, 8, LANES), BF16),
            pltpu.SemaphoreType.DMA,
        ],
        input_output_aliases={11: 0},
        compiler_params=pltpu.CompilerParams(vmem_limit_bytes=PROJECT_VMEM),
        cost_estimate=pl.CostEstimate(flops=2 * 3 * channels * 4 * channels * width,
                                      bytes_accessed=6 << 20, transcendentals=0),
        name="project",
    )(grp, *mains, *halos, weight, taps, packed)


def convolve_body(m_ref, wave_hbm, twist_ref, out_ref,
                  spread_ref, grid_ref, mid_ref, tall_ref, done_ref, wave_ref, sems, wave_sems):
    channels, shards, pieces, lanes = done_ref.shape
    rows_dev = pieces // 2
    freqs = twist_ref.shape[0]
    first_ref, forward_ref, backward_ref, last_ref = (wave_ref.at[i] for i in range(4))
    loads = [
        pltpu.make_async_copy(wave_hbm.at[pl.ds(i * freqs, freqs)], wave_ref.at[i], wave_sems.at[i]) for i in range(4)
    ]
    for load in loads:
        load.start()
    for c in range(channels):
        spread_ref[c] = m_ref[:, 4 * channels + c].astype(F32).reshape(shards * pieces, lanes)
        for a in range(rows_dev):
            for h in range(2):
                grid_ref[c, a * shards:(a + 1) * shards, h * lanes:(h + 1) * lanes] = spread_ref[
                    c, pl.ds(2 * a + h, shards, stride=pieces), :].astype(BF16)
        if c == 0:
            loads[0].wait()
        real = jnp.dot(first_ref[:, :COLS], grid_ref[c], preferred_element_type=F32)
        imag = jnp.dot(first_ref[:, COLS:], grid_ref[c], preferred_element_type=F32)
        cosine, sine = twist_ref[:, :COLS], twist_ref[:, COLS:]
        mid_ref[c, :, :COLS] = (real * cosine + imag * sine).astype(BF16)
        mid_ref[c, :, COLS:] = (imag * cosine - real * sine).astype(BF16)
        if c == 0:
            loads[1].wait()
        freq = jnp.dot(mid_ref[c], forward_ref[...], preferred_element_type=F32)
        for h in range(2):
            low, high = h * lanes, COLS + h * lanes
            real, imag = freq[:, low:low + lanes], freq[:, high:high + lanes]
            h_real, h_imag = (
                m_ref[:, 4 * c + 2 * part + h].astype(F32).reshape(freqs, lanes) for part in range(2)
            )
            mid_ref[c, :, low:low + lanes] = (real * h_real - imag * h_imag).astype(BF16)
            mid_ref[c, :, high:high + lanes] = (real * h_imag + imag * h_real).astype(BF16)
        if c == 0:
            loads[2].wait()
        back = jnp.dot(mid_ref[c], backward_ref[...], preferred_element_type=F32)
        real, imag = back[:, :COLS], back[:, COLS:]
        tall_ref[c, :freqs, :] = (real * cosine - imag * sine).astype(BF16)
        tall_ref[c, freqs:, :] = (imag * cosine + real * sine).astype(BF16)
        if c == 0:
            loads[3].wait()
        out = jnp.dot(last_ref[:COLS, :], tall_ref[c, :freqs], preferred_element_type=F32)
        out += jnp.dot(last_ref[COLS:, :], tall_ref[c, freqs:], preferred_element_type=F32)
        for a in range(rows_dev):
            for h in range(2):
                spread_ref[c, pl.ds(2 * a + h, shards, stride=pieces), :] = out[
                    a * shards:(a + 1) * shards, h * lanes:(h + 1) * lanes]
        done_ref[c] = spread_ref[c].reshape(shards, pieces, lanes).astype(BF16)
        pltpu.make_async_copy(done_ref.at[c], out_ref.at[:, c], sems.at[c]).start()
    for c in range(channels):
        pltpu.make_async_copy(done_ref.at[c], out_ref.at[:, c], sems.at[c]).wait()


def convolve(received, tables):
    shards, kinds, pieces, lanes = received.shape
    channels = kinds // 5
    freqs = shards * pieces
    vmem = pl.BlockSpec(memory_space=pltpu.VMEM)
    return pl.pallas_call(
        convolve_body,
        in_specs=[vmem, pl.BlockSpec(memory_space=pltpu.HBM), vmem],
        out_specs=pl.BlockSpec(memory_space=pltpu.HBM),
        out_shape=jax.ShapeDtypeStruct((shards, channels, pieces, lanes), BF16),
        scratch_shapes=[
            pltpu.VMEM((channels, shards * pieces, lanes), F32),
            pltpu.VMEM((channels, freqs // 2, COLS), BF16),
            pltpu.VMEM((channels, freqs, 2 * COLS), BF16),
            pltpu.VMEM((channels, 2 * freqs, COLS), BF16),
            pltpu.VMEM((channels, shards, pieces, lanes), BF16),
            pltpu.VMEM((4, freqs, 2 * COLS), BF16),
            pltpu.SemaphoreType.DMA((channels,)),
            pltpu.SemaphoreType.DMA((4,)),
        ],
        compiler_params=pltpu.CompilerParams(vmem_limit_bytes=CONVOLVE_VMEM),
        cost_estimate=pl.CostEstimate(flops=3 << 30, bytes_accessed=6 << 20, transcendentals=0),
        name="convolve",
    )(received, *tables)


def gated_body(y_ref, kept_ref, bias_ref, out_ref, spread_ref):
    channels = out_ref.shape[0]
    spread_ref[...] = y_ref[...].astype(F32)
    bias = bias_ref[...]
    for part in range(8):
        cols = slice(part * LANES, (part + 1) * LANES)
        y = spread_ref[pl.ds(part, channels, stride=8), :]
        direct = bias * kept_ref[1, :, cols].astype(F32)
        out_ref[:, cols] = (kept_ref[0, :, cols].astype(F32) * (y + direct)).astype(BF16)


def gated(y, kept, bias):
    vmem = pl.BlockSpec(memory_space=pltpu.VMEM)
    return pl.pallas_call(
        gated_body,
        in_specs=[vmem] * 3,
        out_specs=vmem,
        out_shape=jax.ShapeDtypeStruct(kept.shape[1:], BF16),
        scratch_shapes=[pltpu.VMEM(y.shape, F32)],
        compiler_params=pltpu.CompilerParams(vmem_limit_bytes=8 << 20),
        cost_estimate=pl.CostEstimate(flops=4 * y.size, bytes_accessed=8 * y.size, transcendentals=0),
        name="gated",
    )(y, kept, bias)


def mixed_body(*refs):
    values, weights, out_ref = refs[:4], refs[4:8], refs[8]
    total = jnp.dot(weights[0][...], values[0][...], preferred_element_type=F32)
    for w, v in zip(weights[1:], values[1:]):
        total = total + jnp.dot(w[...], v[...], preferred_element_type=F32)
    out_ref[...] = total.astype(BF16)


def mixed(values, weights):
    vmem = pl.BlockSpec(memory_space=pltpu.VMEM)
    channels, tok = values[0].shape
    return pl.pallas_call(
        mixed_body,
        in_specs=[vmem] * 8,
        out_specs=vmem,
        out_shape=jax.ShapeDtypeStruct((weights[0].shape[0], tok), BF16),
        compiler_params=pltpu.CompilerParams(vmem_limit_bytes=12 << 20),
        cost_estimate=pl.CostEstimate(flops=8 * channels * channels * tok, bytes_accessed=3 << 20, transcendentals=0),
        name="mixed",
    )(*values, *weights)


def swapped(block, mask):
    return lax.ppermute(block, "grp", [(i, i ^ mask) for i in range(4)])


def gathered(block):
    far = swapped(block, 2)
    near = swapped(block, 1)
    return block, far, near, swapped(far, 1)


def previous_tail(tail, mask, shard_count):
    route = [
        ((s - 1) * 4 + (g ^ mask), s * 4 + g) for s in range(1, shard_count) for g in range(4)
    ]
    return lax.ppermute(tail, ("seq", "grp"), route)


def shards(tokens, in_weight, short_weight, filter_bias, spectra, out_weight):
    shard_count = lax.axis_size("seq")
    grp = lax.axis_index("grp")
    channels, tok = tokens.shape
    per_dest = channels // shard_count

    far = swapped(tokens, 2)
    near = swapped(tokens, 1)
    tail = tokens[:, -LANES:]
    halos = [previous_tail(tail, mask, shard_count) for mask in MASKS]
    packed = pack_spectra(spectra, shard_count)
    far, halos, packed = lax.optimization_barrier((far, halos, packed))
    mains = [tokens, far, near, swapped(far, 1)]
    taps = jnp.transpose(short_weight, (2, 0, 1)).reshape(channels, 9)
    message, kept = project(
        grp.reshape(1).astype(jnp.int32), mains, halos, in_weight.reshape(3 * channels, -1), taps, packed
    )
    message, out_weight, filter_bias, later = lax.optimization_barrier(
        (message, out_weight, filter_bias, grp)
    )
    received = lax.all_to_all(message, "seq", 0, 0, tiled=True)

    turned = out_weight.T
    parts = [
        lax.dynamic_slice_in_dim(turned, (later ^ mask) * channels, channels, 0) for mask in MASKS
    ]
    weights = [parts[0]] + [swapped(part, mask) for part, mask in zip(parts[1:], MASKS[1:])]
    zero = jnp.minimum(later, 0)
    tables = [t + zero.astype(t.dtype) for t in transform_tables(shard_count, tok // COLS)]
    bias = filter_bias[:, None] + zero.astype(F32)
    received, weights, tables, bias = lax.optimization_barrier((received, weights, tables, bias))

    result = convolve(received, tables)
    back = lax.all_to_all(result, "seq", 0, 0, tiled=True).reshape(channels * 8, LANES)
    weighted = gated(back, kept, bias)
    return mixed(gathered(weighted), weights)


def solution(mesh):
    in_specs = (
        P("grp", "seq"),
        P(None, "grp", None),
        P(None, None, "grp"),
        P("grp"),
        P(None, "grp", "seq", None),
        P("grp", None),
    )
    out_specs = P("grp", "seq")
    return jax.shard_map(shards, mesh=mesh, in_specs=in_specs, out_specs=out_specs, check_vma=False)
```

```python
import math

import jax
import jax.numpy as jnp
import numpy as np
from jax import lax
from jax.experimental import pallas as pl
from jax.experimental.pallas import tpu as pltpu
from jax.sharding import PartitionSpec as P

COLS = 256
FREQS = 512
LANES = 128
PROJECT_VMEM = 50000 << 10
CONVOLVE_VMEM = 50000 << 10
MASKS = (0, 2, 1, 3)
BF16 = jnp.bfloat16
F32 = jnp.float32


def unit_circle(rows, cols, period):
    angle = (np.outer(rows, cols) % period) * (2.0 * math.pi / period)
    return np.cos(angle), np.sin(angle)


def transform_tables(shard_count, rows_dev):
    half = shard_count * rows_dev
    order = (np.arange(shard_count)[None, :] * rows_dev + np.arange(rows_dev)[:, None]).reshape(-1)
    freqs = np.arange(2 * half)
    cols = np.arange(COLS)
    padded = 2 * half * COLS
    cos1, sin1 = unit_circle(freqs, order, 2 * half)
    cos2, sin2 = unit_circle(cols, cols, COLS)
    cost, sint = unit_circle(freqs, cols, padded)
    first = np.concatenate([cos1, -sin1], 1)
    forward = np.block([[cos2, -sin2], [sin2, cos2]])
    backward = np.block([[cos2, sin2], [-sin2, cos2]])
    last = np.concatenate([cos1.T, -sin1.T], 0) / padded
    waves = np.concatenate([first, forward, backward, last], 0)
    return jnp.asarray(waves, BF16), jnp.asarray(np.concatenate([cost, sint], 1), F32)


def pack_spectra_body(spec_ref, out_ref):
    dests = out_ref.shape[0]
    per_dest = spec_ref.shape[1] // dests
    for part in range(2):
        for h in range(2):
            piece = spec_ref[part, :, :, h * LANES:(h + 1) * LANES]
            piece = piece.reshape(dests, per_dest, *piece.shape[1:]).astype(BF16)
            for c in range(per_dest):
                out_ref[:, 4 * c + 2 * part + h] = piece[:, c]


def pack_spectra(spectra, shard_count):
    _, channels, rows, cols = spectra.shape
    per_dest = channels // shard_count
    steps = 2
    return pl.pallas_call(
        pack_spectra_body,
        grid=(steps,),
        in_specs=[pl.BlockSpec((2, channels // steps, rows, cols), lambda i: (0, i, 0, 0))],
        out_specs=pl.BlockSpec((shard_count // steps, 4 * per_dest, rows, LANES), lambda i: (i, 0, 0, 0)),
        out_shape=jax.ShapeDtypeStruct((shard_count, 5 * per_dest, rows, LANES), BF16),
        cost_estimate=pl.CostEstimate(flops=0, bytes_accessed=6 * spectra.size, transcendentals=0),
        name="pack_spectra",
    )(spectra)


def project_body(*refs):
    grp_ref, mains, halos, weight_ref, taps_ref = refs[0], refs[1:5], refs[5:9], refs[9], refs[10]
    message_ref, kept_ref, token_ref, stream_ref, spread_ref, part_ref, sem = refs[12:]
    channels, tok = mains[0].shape
    width = tok + LANES
    grp = grp_ref[0]
    for mask, main, halo in zip(MASKS, mains, halos):
        rows = pl.ds(pl.multiple_of((grp ^ mask) * channels, 64), channels)
        token_ref[rows, :LANES] = halo[...]
        token_ref[rows, LANES:] = main[...]
    step = 384
    for col in range(0, width, step):
        stream_ref[:, col:col + step] = jnp.dot(
            weight_ref[...], token_ref[:, col:col + step], preferred_element_type=F32
        )
    rows = 16

    def chunk(index, carry):
        row = pl.multiple_of(index * rows, rows)
        smooth = []
        for s in range(3):
            x = stream_ref[pl.ds(s * channels + row, rows), :].astype(BF16).astype(F32)
            w = [taps_ref[pl.ds(row, rows), 3 * tap + s:3 * tap + s + 1] for tap in range(3)]
            y = w[0] * x + w[1] * pltpu.roll(x, 1, 1) + w[2] * pltpu.roll(x, 2, 1)
            smooth.append(y[:, LANES:])
        kept_ref[0, pl.ds(row, rows), :] = smooth[0].astype(BF16)
        signal = smooth[2] * smooth[1]
        kept_ref[1, pl.ds(row, rows), :] = signal.astype(BF16)
        for part in range(8):
            spread_ref[pl.ds(row * 8 + part, rows, stride=8), :] = signal[:, part * LANES:(part + 1) * LANES]
        return carry

    shards, per_dest = part_ref.shape[:2]
    groups = 4
    each = channels // groups
    copies = []
    for group in range(groups):
        lax.fori_loop(group * each // rows, (group + 1) * each // rows, chunk, 0)
        dests = pl.ds(group * shards // groups, shards // groups)
        ready = spread_ref[pl.ds(group * each * 8, each * 8), :].astype(BF16)
        part_ref[dests] = ready.reshape(shards // groups, *part_ref.shape[1:])
        copies.append(pltpu.make_async_copy(
            part_ref.at[dests], message_ref.at[dests, pl.ds(4 * per_dest, per_dest)], sem.at[group]
        ))
        copies[-1].start()
    for copy in copies:
        copy.wait()


def project(grp, mains, halos, weight, taps, packed):
    channels, tok = mains[0].shape
    width = tok + LANES
    vmem = pl.BlockSpec(memory_space=pltpu.VMEM)
    anywhere = pl.BlockSpec(memory_space=pltpu.HBM)
    shards, pieces = packed.shape[:2]
    return pl.pallas_call(
        project_body,
        in_specs=[pl.BlockSpec(memory_space=pltpu.SMEM)] + [vmem] * 10 + [anywhere],
        out_specs=[anywhere, vmem],
        out_shape=[
            jax.ShapeDtypeStruct(packed.shape, BF16),
            jax.ShapeDtypeStruct((2, channels, tok), BF16),
        ],
        scratch_shapes=[
            pltpu.VMEM((4 * channels, width), BF16),
            pltpu.VMEM((3 * channels, width), F32),
            pltpu.VMEM((channels * 8, LANES), F32),
            pltpu.VMEM((shards, pieces // 5, 8, LANES), BF16),
            pltpu.SemaphoreType.DMA((4,)),
        ],
        input_output_aliases={11: 0},
        compiler_params=pltpu.CompilerParams(vmem_limit_bytes=PROJECT_VMEM),
        cost_estimate=pl.CostEstimate(flops=2 * 3 * channels * 4 * channels * width,
                                      bytes_accessed=6 << 20, transcendentals=0),
        name="project",
    )(grp, *mains, *halos, weight, taps, packed)


def convolve_body(m_ref, wave_hbm, twist_ref, out_ref,
                  spread_ref, grid_ref, mid_ref, tall_ref, done_ref, wave_ref, sems, wave_sems):
    channels, shards, pieces, lanes = done_ref.shape
    rows_dev = pieces // 2
    freqs = twist_ref.shape[0]
    first_ref, forward_ref, backward_ref, last_ref = (wave_ref.at[i] for i in range(4))
    loads = [
        pltpu.make_async_copy(wave_hbm.at[pl.ds(i * freqs, freqs)], wave_ref.at[i], wave_sems.at[i]) for i in range(4)
    ]
    for load in loads:
        load.start()
    for c in range(channels):
        spread_ref[c] = m_ref[:, 4 * channels + c].astype(F32).reshape(shards * pieces, lanes)
        for a in range(rows_dev):
            for h in range(2):
                grid_ref[c, a * shards:(a + 1) * shards, h * lanes:(h + 1) * lanes] = spread_ref[
                    c, pl.ds(2 * a + h, shards, stride=pieces), :].astype(BF16)
        if c == 0:
            loads[0].wait()
        real = jnp.dot(first_ref[:, :COLS], grid_ref[c], preferred_element_type=F32)
        imag = jnp.dot(first_ref[:, COLS:], grid_ref[c], preferred_element_type=F32)
        cosine, sine = twist_ref[:, :COLS], twist_ref[:, COLS:]
        mid_ref[c, :, :COLS] = (real * cosine + imag * sine).astype(BF16)
        mid_ref[c, :, COLS:] = (imag * cosine - real * sine).astype(BF16)
        if c == 0:
            loads[1].wait()
        freq = jnp.dot(mid_ref[c], forward_ref[...], preferred_element_type=F32)
        for h in range(2):
            low, high = h * lanes, COLS + h * lanes
            real, imag = freq[:, low:low + lanes], freq[:, high:high + lanes]
            h_real, h_imag = (
                m_ref[:, 4 * c + 2 * part + h].astype(F32).reshape(freqs, lanes) for part in range(2)
            )
            mid_ref[c, :, low:low + lanes] = (real * h_real - imag * h_imag).astype(BF16)
            mid_ref[c, :, high:high + lanes] = (real * h_imag + imag * h_real).astype(BF16)
        if c == 0:
            loads[2].wait()
        back = jnp.dot(mid_ref[c], backward_ref[...], preferred_element_type=F32)
        real, imag = back[:, :COLS], back[:, COLS:]
        tall_ref[c, :freqs, :] = (real * cosine - imag * sine).astype(BF16)
        tall_ref[c, freqs:, :] = (imag * cosine + real * sine).astype(BF16)
        if c == 0:
            loads[3].wait()
        out = jnp.dot(last_ref[:COLS, :], tall_ref[c, :freqs], preferred_element_type=F32)
        out += jnp.dot(last_ref[COLS:, :], tall_ref[c, freqs:], preferred_element_type=F32)
        for a in range(rows_dev):
            for h in range(2):
                spread_ref[c, pl.ds(2 * a + h, shards, stride=pieces), :] = out[
                    a * shards:(a + 1) * shards, h * lanes:(h + 1) * lanes]
        done_ref[c] = spread_ref[c].reshape(shards, pieces, lanes).astype(BF16)
        pltpu.make_async_copy(done_ref.at[c], out_ref.at[:, c], sems.at[c]).start()
    for c in range(channels):
        pltpu.make_async_copy(done_ref.at[c], out_ref.at[:, c], sems.at[c]).wait()


def convolve(received, tables):
    shards, kinds, pieces, lanes = received.shape
    channels = kinds // 5
    freqs = shards * pieces
    vmem = pl.BlockSpec(memory_space=pltpu.VMEM)
    return pl.pallas_call(
        convolve_body,
        in_specs=[vmem, pl.BlockSpec(memory_space=pltpu.HBM), vmem],
        out_specs=pl.BlockSpec(memory_space=pltpu.HBM),
        out_shape=jax.ShapeDtypeStruct((shards, channels, pieces, lanes), BF16),
        scratch_shapes=[
            pltpu.VMEM((channels, shards * pieces, lanes), F32),
            pltpu.VMEM((channels, freqs // 2, COLS), BF16),
            pltpu.VMEM((channels, freqs, 2 * COLS), BF16),
            pltpu.VMEM((channels, 2 * freqs, COLS), BF16),
            pltpu.VMEM((channels, shards, pieces, lanes), BF16),
            pltpu.VMEM((4, freqs, 2 * COLS), BF16),
            pltpu.SemaphoreType.DMA((channels,)),
            pltpu.SemaphoreType.DMA((4,)),
        ],
        compiler_params=pltpu.CompilerParams(vmem_limit_bytes=CONVOLVE_VMEM),
        cost_estimate=pl.CostEstimate(flops=3 << 30, bytes_accessed=6 << 20, transcendentals=0),
        name="convolve",
    )(received, *tables)


def gated_body(y_ref, kept_ref, bias_ref, out_ref, spread_ref):
    channels = out_ref.shape[0]
    spread_ref[...] = y_ref[...].astype(F32)
    bias = bias_ref[...]
    for part in range(8):
        cols = slice(part * LANES, (part + 1) * LANES)
        y = spread_ref[pl.ds(part, channels, stride=8), :]
        direct = bias * kept_ref[1, :, cols].astype(F32)
        out_ref[:, cols] = (kept_ref[0, :, cols].astype(F32) * (y + direct)).astype(BF16)


def gated(y, kept, bias):
    vmem = pl.BlockSpec(memory_space=pltpu.VMEM)
    return pl.pallas_call(
        gated_body,
        in_specs=[vmem] * 3,
        out_specs=vmem,
        out_shape=jax.ShapeDtypeStruct(kept.shape[1:], BF16),
        scratch_shapes=[pltpu.VMEM(y.shape, F32)],
        compiler_params=pltpu.CompilerParams(vmem_limit_bytes=8 << 20),
        cost_estimate=pl.CostEstimate(flops=4 * y.size, bytes_accessed=8 * y.size, transcendentals=0),
        name="gated",
    )(y, kept, bias)


def mixed_body(*refs):
    values, weights, out_ref = refs[:4], refs[4:8], refs[8]
    total = jnp.dot(weights[0][...], values[0][...], preferred_element_type=F32)
    for w, v in zip(weights[1:], values[1:]):
        total = total + jnp.dot(w[...], v[...], preferred_element_type=F32)
    out_ref[...] = total.astype(BF16)


def mixed(values, weights):
    vmem = pl.BlockSpec(memory_space=pltpu.VMEM)
    channels, tok = values[0].shape
    return pl.pallas_call(
        mixed_body,
        in_specs=[vmem] * 8,
        out_specs=vmem,
        out_shape=jax.ShapeDtypeStruct((weights[0].shape[0], tok), BF16),
        compiler_params=pltpu.CompilerParams(vmem_limit_bytes=12 << 20),
        cost_estimate=pl.CostEstimate(flops=8 * channels * channels * tok, bytes_accessed=3 << 20, transcendentals=0),
        name="mixed",
    )(*values, *weights)


def swapped(block, mask):
    return lax.ppermute(block, "grp", [(i, i ^ mask) for i in range(4)])


def gathered(block):
    far = swapped(block, 2)
    near = swapped(block, 1)
    return block, far, near, swapped(far, 1)


def shards(tokens, in_weight, short_weight, filter_bias, spectra, out_weight):
    shard_count = lax.axis_size("seq")
    grp = lax.axis_index("grp")
    channels, tok = tokens.shape
    per_dest = channels // shard_count

    far = swapped(tokens, 2)
    near = swapped(tokens, 1)
    route = [(i, i + 1) for i in range(shard_count - 1)]
    halo = lax.ppermute(tokens[:, -LANES:], "seq", route)
    packed = pack_spectra(spectra, shard_count)
    halo, packed = lax.optimization_barrier((halo, packed))
    halo_far = swapped(halo, 2)
    halo_near = swapped(halo, 1)
    far, halo_far = lax.optimization_barrier((far, halo_far))
    mains = [tokens, far, near, swapped(far, 1)]
    halos = [halo, halo_far, halo_near, swapped(halo_far, 1)]
    taps = jnp.transpose(short_weight, (2, 0, 1)).reshape(channels, 9)
    message, kept = project(
        grp.reshape(1).astype(jnp.int32), mains, halos, in_weight.reshape(3 * channels, -1), taps, packed
    )
    message, out_weight, filter_bias, later = lax.optimization_barrier(
        (message, out_weight, filter_bias, grp)
    )
    received = lax.all_to_all(message, "seq", 0, 0, tiled=True)

    turned = out_weight.T
    parts = [
        lax.dynamic_slice_in_dim(turned, (later ^ mask) * channels, channels, 0) for mask in MASKS
    ]
    weights = [parts[0]] + [swapped(part, mask) for part, mask in zip(parts[1:], MASKS[1:])]
    zero = jnp.minimum(later, 0)
    tables = [t + zero.astype(t.dtype) for t in transform_tables(shard_count, tok // COLS)]
    bias = filter_bias[:, None] + zero.astype(F32)
    received, weights, tables, bias = lax.optimization_barrier((received, weights, tables, bias))

    result = convolve(received, tables)
    back = lax.all_to_all(result, "seq", 0, 0, tiled=True).reshape(channels * 8, LANES)
    weighted = gated(back, kept, bias)
    return mixed(gathered(weighted), weights)


def solution(mesh):
    in_specs = (
        P("grp", "seq"),
        P(None, "grp", None),
        P(None, None, "grp"),
        P("grp"),
        P(None, "grp", "seq", None),
        P("grp", None),
    )
    out_specs = P("grp", "seq")
    return jax.shard_map(shards, mesh=mesh, in_specs=in_specs, out_specs=out_specs, check_vma=False)
```

```python
import math

import jax
import jax.numpy as jnp
import numpy as np
from jax import lax
from jax.experimental import pallas as pl
from jax.experimental.pallas import tpu as pltpu
from jax.sharding import PartitionSpec as P

COLS = 256
FREQS = 512
LANES = 128
PROJECT_VMEM = 53000 << 10
GATED_VMEM = 54000 << 10
CONVOLVE_VMEM = 50000 << 10
MASKS = (0, 2, 1, 3)
BF16 = jnp.bfloat16
F32 = jnp.float32


def unit_circle(rows, cols, period):
    angle = (np.outer(rows, cols) % period) * (2.0 * math.pi / period)
    return np.cos(angle), np.sin(angle)


def transform_tables(shard_count, rows_dev):
    half = shard_count * rows_dev
    order = (np.arange(shard_count)[None, :] * rows_dev + np.arange(rows_dev)[:, None]).reshape(-1)
    freqs = np.arange(2 * half)
    cols = np.arange(COLS)
    padded = 2 * half * COLS
    cos1, sin1 = unit_circle(freqs, order, 2 * half)
    cos2, sin2 = unit_circle(cols, cols, COLS)
    cost, sint = unit_circle(freqs, cols, padded)
    first = np.concatenate([cos1, -sin1], 1)
    forward = np.block([[cos2, -sin2], [sin2, cos2]])
    backward = np.block([[cos2, sin2], [-sin2, cos2]])
    last = np.concatenate([cos1.T, -sin1.T], 0) / padded
    waves = np.concatenate([first, forward, backward, last], 0)
    return jnp.asarray(waves, BF16), jnp.asarray(np.concatenate([cost, sint], 1), F32)


def pack_spectra_body(spec_ref, out_ref):
    dests = out_ref.shape[0]
    per_dest = spec_ref.shape[1] // dests
    for part in range(2):
        for h in range(2):
            piece = spec_ref[part, :, :, h * LANES:(h + 1) * LANES]
            piece = piece.reshape(dests, per_dest, *piece.shape[1:]).astype(BF16)
            for c in range(per_dest):
                out_ref[:, 4 * c + 2 * part + h] = piece[:, c]


def pack_spectra(spectra, shard_count):
    _, channels, rows, cols = spectra.shape
    per_dest = channels // shard_count
    steps = 2
    return pl.pallas_call(
        pack_spectra_body,
        grid=(steps,),
        in_specs=[pl.BlockSpec((2, channels // steps, rows, cols), lambda i: (0, i, 0, 0))],
        out_specs=pl.BlockSpec((shard_count // steps, 4 * per_dest, rows, LANES), lambda i: (i, 0, 0, 0)),
        out_shape=jax.ShapeDtypeStruct((shard_count, 5 * per_dest, rows, LANES), BF16),
        cost_estimate=pl.CostEstimate(flops=0, bytes_accessed=6 * spectra.size, transcendentals=0),
        name="pack_spectra",
    )(spectra)


def project_body(*refs):
    grp_ref, mains, halos, weight_hbm, taps_ref = refs[0], refs[1:5], refs[5:9], refs[9], refs[10]
    message_ref, kept_hbm, token_ref, stream_ref, spread_ref, part_ref, kept_ref, weight_ref, sem, kept_sem, weight_sem = refs[12:]
    channels, tok = mains[0].shape
    width = tok + LANES
    grp = grp_ref[0]
    load = pltpu.make_async_copy(weight_hbm, weight_ref, weight_sem)
    load.start()
    for mask, main, halo in zip(MASKS, mains, halos):
        rows = pl.ds(pl.multiple_of((grp ^ mask) * channels, 64), channels)
        token_ref[rows, :LANES] = halo[...]
        token_ref[rows, LANES:] = main[...]
    load.wait()
    step = 384
    for col in range(0, width, step):
        stream_ref[:, col:col + step] = jnp.dot(
            weight_ref[...], token_ref[:, col:col + step], preferred_element_type=F32
        )
    rows = 16

    def chunk(index, carry):
        row = pl.multiple_of(index * rows, rows)
        smooth = []
        for s in range(3):
            x = stream_ref[pl.ds(s * channels + row, rows), :].astype(BF16).astype(F32)
            w = [taps_ref[pl.ds(row, rows), 3 * tap + s:3 * tap + s + 1] for tap in range(3)]
            y = w[0] * x + w[1] * pltpu.roll(x, 1, 1) + w[2] * pltpu.roll(x, 2, 1)
            smooth.append(y[:, LANES:])
        kept_ref[0, pl.ds(row, rows), :] = smooth[0].astype(BF16)
        signal = smooth[2] * smooth[1]
        kept_ref[1, pl.ds(row, rows), :] = signal.astype(BF16)
        for part in range(8):
            spread_ref[pl.ds(row * 8 + part, rows, stride=8), :] = signal[:, part * LANES:(part + 1) * LANES]
        return carry

    shards, per_dest = part_ref.shape[:2]
    groups = 4
    each = channels // groups
    copies = []
    for group in range(groups):
        lax.fori_loop(group * each // rows, (group + 1) * each // rows, chunk, 0)
        dests = pl.ds(group * shards // groups, shards // groups)
        ready = spread_ref[pl.ds(group * each * 8, each * 8), :].astype(BF16)
        part_ref[dests] = ready.reshape(shards // groups, *part_ref.shape[1:])
        copies.append(pltpu.make_async_copy(
            part_ref.at[dests], message_ref.at[dests, pl.ds(4 * per_dest, per_dest)], sem.at[group]
        ))
        mine = pl.ds(group * each, each)
        copies.append(pltpu.make_async_copy(kept_ref.at[:, mine], kept_hbm.at[:, mine], kept_sem.at[group]))
        for copy in copies[-2:]:
            copy.start()
    for copy in copies:
        copy.wait()


def project(grp, mains, halos, weight, taps, packed):
    channels, tok = mains[0].shape
    width = tok + LANES
    vmem = pl.BlockSpec(memory_space=pltpu.VMEM)
    anywhere = pl.BlockSpec(memory_space=pltpu.HBM)
    shards, pieces = packed.shape[:2]
    return pl.pallas_call(
        project_body,
        in_specs=[pl.BlockSpec(memory_space=pltpu.SMEM)] + [vmem] * 8 + [anywhere, vmem, anywhere],
        out_specs=[anywhere] * 2,
        out_shape=[
            jax.ShapeDtypeStruct(packed.shape, BF16),
            jax.ShapeDtypeStruct((2, channels, tok), BF16),
        ],
        scratch_shapes=[
            pltpu.VMEM((4 * channels, width), BF16),
            pltpu.VMEM((3 * channels, width), F32),
            pltpu.VMEM((channels * 8, LANES), F32),
            pltpu.VMEM((shards, pieces // 5, 8, LANES), BF16),
            pltpu.VMEM((2, channels, tok), BF16),
            pltpu.VMEM(weight.shape, BF16),
            pltpu.SemaphoreType.DMA((4,)),
            pltpu.SemaphoreType.DMA((4,)),
            pltpu.SemaphoreType.DMA,
        ],
        input_output_aliases={11: 0},
        compiler_params=pltpu.CompilerParams(vmem_limit_bytes=PROJECT_VMEM),
        cost_estimate=pl.CostEstimate(flops=2 * 3 * channels * 4 * channels * width,
                                      bytes_accessed=6 << 20, transcendentals=0),
        name="project",
    )(grp, *mains, *halos, weight, taps, packed)


def convolve_body(m_ref, wave_hbm, twist_ref, out_ref,
                  spread_ref, grid_ref, mid_ref, tall_ref, done_ref, wave_ref, sems, wave_sems):
    channels, shards, pieces, lanes = done_ref.shape
    rows_dev = pieces // 2
    freqs = twist_ref.shape[0]
    first_ref, forward_ref, backward_ref, last_ref = (wave_ref.at[i] for i in range(4))
    loads = [
        pltpu.make_async_copy(wave_hbm.at[pl.ds(i * freqs, freqs)], wave_ref.at[i], wave_sems.at[i]) for i in range(4)
    ]
    for load in loads:
        load.start()
    for c in range(channels):
        spread_ref[c] = m_ref[:, 4 * channels + c].astype(F32).reshape(shards * pieces, lanes)
        for a in range(rows_dev):
            for h in range(2):
                grid_ref[c, a * shards:(a + 1) * shards, h * lanes:(h + 1) * lanes] = spread_ref[
                    c, pl.ds(2 * a + h, shards, stride=pieces), :].astype(BF16)
        if c == 0:
            loads[0].wait()
        real = jnp.dot(first_ref[:, :COLS], grid_ref[c], preferred_element_type=F32)
        imag = jnp.dot(first_ref[:, COLS:], grid_ref[c], preferred_element_type=F32)
        cosine, sine = twist_ref[:, :COLS], twist_ref[:, COLS:]
        mid_ref[c, :, :COLS] = (real * cosine + imag * sine).astype(BF16)
        mid_ref[c, :, COLS:] = (imag * cosine - real * sine).astype(BF16)
        if c == 0:
            loads[1].wait()
        freq = jnp.dot(mid_ref[c], forward_ref[...], preferred_element_type=F32)
        for h in range(2):
            low, high = h * lanes, COLS + h * lanes
            real, imag = freq[:, low:low + lanes], freq[:, high:high + lanes]
            h_real, h_imag = (
                m_ref[:, 4 * c + 2 * part + h].astype(F32).reshape(freqs, lanes) for part in range(2)
            )
            mid_ref[c, :, low:low + lanes] = (real * h_real - imag * h_imag).astype(BF16)
            mid_ref[c, :, high:high + lanes] = (real * h_imag + imag * h_real).astype(BF16)
        if c == 0:
            loads[2].wait()
        back = jnp.dot(mid_ref[c], backward_ref[...], preferred_element_type=F32)
        real, imag = back[:, :COLS], back[:, COLS:]
        tall_ref[c, :freqs, :] = (real * cosine - imag * sine).astype(BF16)
        tall_ref[c, freqs:, :] = (imag * cosine + real * sine).astype(BF16)
        if c == 0:
            loads[3].wait()
        out = jnp.dot(last_ref[:COLS, :], tall_ref[c, :freqs], preferred_element_type=F32)
        out += jnp.dot(last_ref[COLS:, :], tall_ref[c, freqs:], preferred_element_type=F32)
        for a in range(rows_dev):
            for h in range(2):
                spread_ref[c, pl.ds(2 * a + h, shards, stride=pieces), :] = out[
                    a * shards:(a + 1) * shards, h * lanes:(h + 1) * lanes]
        done_ref[c] = spread_ref[c].reshape(shards, pieces, lanes).astype(BF16)
        pltpu.make_async_copy(done_ref.at[c], out_ref.at[:, c], sems.at[c]).start()
    for c in range(channels):
        pltpu.make_async_copy(done_ref.at[c], out_ref.at[:, c], sems.at[c]).wait()


def convolve(received, tables):
    shards, kinds, pieces, lanes = received.shape
    channels = kinds // 5
    freqs = shards * pieces
    vmem = pl.BlockSpec(memory_space=pltpu.VMEM)
    return pl.pallas_call(
        convolve_body,
        in_specs=[vmem, pl.BlockSpec(memory_space=pltpu.HBM), vmem],
        out_specs=pl.BlockSpec(memory_space=pltpu.HBM),
        out_shape=jax.ShapeDtypeStruct((shards, channels, pieces, lanes), BF16),
        scratch_shapes=[
            pltpu.VMEM((channels, shards * pieces, lanes), F32),
            pltpu.VMEM((channels, freqs // 2, COLS), BF16),
            pltpu.VMEM((channels, freqs, 2 * COLS), BF16),
            pltpu.VMEM((channels, 2 * freqs, COLS), BF16),
            pltpu.VMEM((channels, shards, pieces, lanes), BF16),
            pltpu.VMEM((4, freqs, 2 * COLS), BF16),
            pltpu.SemaphoreType.DMA((channels,)),
            pltpu.SemaphoreType.DMA((4,)),
        ],
        compiler_params=pltpu.CompilerParams(vmem_limit_bytes=CONVOLVE_VMEM),
        cost_estimate=pl.CostEstimate(flops=3 << 30, bytes_accessed=6 << 20, transcendentals=0),
        name="convolve",
    )(received, *tables)


def gated_body(y_ref, kept_hbm, bias_ref, out_ref, spread_ref, kept_ref, sem):
    channels = out_ref.shape[0]
    load = pltpu.make_async_copy(kept_hbm, kept_ref, sem)
    load.start()
    spread_ref[...] = y_ref[...].astype(F32)
    bias = bias_ref[...]
    load.wait()
    for part in range(8):
        cols = slice(part * LANES, (part + 1) * LANES)
        y = spread_ref[pl.ds(part, channels, stride=8), :]
        direct = bias * kept_ref[1, :, cols].astype(F32)
        out_ref[:, cols] = (kept_ref[0, :, cols].astype(F32) * (y + direct)).astype(BF16)


def gated(y, kept, bias):
    vmem = pl.BlockSpec(memory_space=pltpu.VMEM)
    return pl.pallas_call(
        gated_body,
        in_specs=[vmem, pl.BlockSpec(memory_space=pltpu.HBM), vmem],
        out_specs=vmem,
        out_shape=jax.ShapeDtypeStruct(kept.shape[1:], BF16),
        scratch_shapes=[
            pltpu.VMEM(y.shape, F32),
            pltpu.VMEM(kept.shape, BF16),
            pltpu.SemaphoreType.DMA,
        ],
        compiler_params=pltpu.CompilerParams(vmem_limit_bytes=GATED_VMEM),
        cost_estimate=pl.CostEstimate(flops=4 * y.size, bytes_accessed=8 * y.size, transcendentals=0),
        name="gated",
    )(y, kept, bias)


def mixed_body(*refs):
    values, weights, out_ref = refs[:4], refs[4:8], refs[8]
    total = jnp.dot(weights[0][...], values[0][...], preferred_element_type=F32)
    for w, v in zip(weights[1:], values[1:]):
        total = total + jnp.dot(w[...], v[...], preferred_element_type=F32)
    out_ref[...] = total.astype(BF16)


def mixed(values, weights):
    vmem = pl.BlockSpec(memory_space=pltpu.VMEM)
    channels, tok = values[0].shape
    return pl.pallas_call(
        mixed_body,
        in_specs=[vmem] * 8,
        out_specs=vmem,
        out_shape=jax.ShapeDtypeStruct((weights[0].shape[0], tok), BF16),
        compiler_params=pltpu.CompilerParams(vmem_limit_bytes=12 << 20),
        cost_estimate=pl.CostEstimate(flops=8 * channels * channels * tok, bytes_accessed=3 << 20, transcendentals=0),
        name="mixed",
    )(*values, *weights)


def swapped(block, mask):
    return lax.ppermute(block, "grp", [(i, i ^ mask) for i in range(4)])


def gathered(block):
    far = swapped(block, 2)
    near = swapped(block, 1)
    return block, far, near, swapped(far, 1)


def shards(tokens, in_weight, short_weight, filter_bias, spectra, out_weight):
    shard_count = lax.axis_size("seq")
    grp = lax.axis_index("grp")
    channels, tok = tokens.shape
    per_dest = channels // shard_count

    far = swapped(tokens, 2)
    near = swapped(tokens, 1)
    route = [(i, i + 1) for i in range(shard_count - 1)]
    halo = lax.ppermute(tokens[:, -LANES:], "seq", route)
    packed = pack_spectra(spectra, shard_count)
    halo, packed = lax.optimization_barrier((halo, packed))
    halo_far = swapped(halo, 2)
    halo_near = swapped(halo, 1)
    far, halo_far = lax.optimization_barrier((far, halo_far))
    mains = [tokens, far, near, swapped(far, 1)]
    halos = [halo, halo_far, halo_near, swapped(halo_far, 1)]
    taps = jnp.transpose(short_weight, (2, 0, 1)).reshape(channels, 9)
    message, kept = project(
        grp.reshape(1).astype(jnp.int32), mains, halos, in_weight.reshape(3 * channels, -1), taps, packed
    )
    message, out_weight, filter_bias, later = lax.optimization_barrier(
        (message, out_weight, filter_bias, grp)
    )
    received = lax.all_to_all(message, "seq", 0, 0, tiled=True)

    turned = out_weight.T
    parts = [
        lax.dynamic_slice_in_dim(turned, (later ^ mask) * channels, channels, 0) for mask in MASKS
    ]
    weights = [parts[0]] + [swapped(part, mask) for part, mask in zip(parts[1:], MASKS[1:])]
    zero = jnp.minimum(later, 0)
    tables = [t + zero.astype(t.dtype) for t in transform_tables(shard_count, tok // COLS)]
    bias = filter_bias[:, None] + zero.astype(F32)
    received, weights, tables, bias = lax.optimization_barrier((received, weights, tables, bias))

    result = convolve(received, tables)
    back = lax.all_to_all(result, "seq", 0, 0, tiled=True).reshape(channels * 8, LANES)
    weighted = gated(back, kept, bias)
    return mixed(gathered(weighted), weights)


def solution(mesh):
    in_specs = (
        P("grp", "seq"),
        P(None, "grp", None),
        P(None, None, "grp"),
        P("grp"),
        P(None, "grp", "seq", None),
        P("grp", None),
    )
    out_specs = P("grp", "seq")
    return jax.shard_map(shards, mesh=mesh, in_specs=in_specs, out_specs=out_specs, check_vma=False)
```

```python
import math

import jax
import jax.numpy as jnp
import numpy as np
from jax import lax
from jax.experimental import pallas as pl
from jax.experimental.pallas import tpu as pltpu
from jax.sharding import PartitionSpec as P

COLS = 256
FREQS = 512
LANES = 128
PROJECT_VMEM = 44000 << 10
GATED_VMEM = 54000 << 10
CONVOLVE_VMEM = 50000 << 10
MASKS = (0, 2, 1, 3)
BF16 = jnp.bfloat16
F32 = jnp.float32


def unit_circle(rows, cols, period):
    angle = (np.outer(rows, cols) % period) * (2.0 * math.pi / period)
    return np.cos(angle), np.sin(angle)


def transform_tables(shard_count, rows_dev):
    half = shard_count * rows_dev
    order = (np.arange(shard_count)[None, :] * rows_dev + np.arange(rows_dev)[:, None]).reshape(-1)
    freqs = np.arange(2 * half)
    cols = np.arange(COLS)
    padded = 2 * half * COLS
    cos1, sin1 = unit_circle(freqs, order, 2 * half)
    cos2, sin2 = unit_circle(cols, cols, COLS)
    cost, sint = unit_circle(freqs, cols, padded)
    first = np.concatenate([cos1, -sin1], 1)
    forward = np.block([[cos2, -sin2], [sin2, cos2]])
    backward = np.block([[cos2, sin2], [-sin2, cos2]])
    last = np.concatenate([cos1.T, -sin1.T], 0) / padded
    waves = np.concatenate([first, forward, backward, last], 0)
    return jnp.asarray(waves, BF16), jnp.asarray(np.concatenate([cost, sint], 1), F32)


def pack_spectra_body(spec_ref, out_ref):
    dests = out_ref.shape[0]
    per_dest = spec_ref.shape[1] // dests
    for part in range(2):
        for h in range(2):
            piece = spec_ref[part, :, :, h * LANES:(h + 1) * LANES]
            piece = piece.reshape(dests, per_dest, *piece.shape[1:]).astype(BF16)
            for c in range(per_dest):
                out_ref[:, 4 * c + 2 * part + h] = piece[:, c]


def pack_spectra(spectra, shard_count):
    _, channels, rows, cols = spectra.shape
    per_dest = channels // shard_count
    steps = 2
    return pl.pallas_call(
        pack_spectra_body,
        grid=(steps,),
        in_specs=[pl.BlockSpec((2, channels // steps, rows, cols), lambda i: (0, i, 0, 0))],
        out_specs=pl.BlockSpec((shard_count // steps, 4 * per_dest, rows, LANES), lambda i: (i, 0, 0, 0)),
        out_shape=jax.ShapeDtypeStruct((shard_count, 5 * per_dest, rows, LANES), BF16),
        cost_estimate=pl.CostEstimate(flops=0, bytes_accessed=6 * spectra.size, transcendentals=0),
        name="pack_spectra",
    )(spectra)


def near_half_body(grp_ref, own_ref, near_ref, weight_hbm, out_ref, token_ref, weight_ref, sem):
    channels = own_ref.shape[0]
    grp = grp_ref[0]
    first = pl.multiple_of((grp // 2) * 2 * channels, LANES)
    load = pltpu.make_async_copy(weight_hbm.at[:, pl.ds(first, 2 * channels)], weight_ref, sem)
    load.start()
    side = grp % 2
    token_ref[pl.ds(pl.multiple_of(side * channels, 64), channels), :] = own_ref[...]
    token_ref[pl.ds(pl.multiple_of((1 - side) * channels, 64), channels), :] = near_ref[...]
    load.wait()
    step = 256
    for col in range(0, out_ref.shape[1], step):
        out_ref[:, col:col + step] = jnp.dot(
            weight_ref[...], token_ref[:, col:col + step], preferred_element_type=F32
        )


def near_half(grp, own, near, weight):
    channels, tok = own.shape
    vmem = pl.BlockSpec(memory_space=pltpu.VMEM)
    return pl.pallas_call(
        near_half_body,
        in_specs=[pl.BlockSpec(memory_space=pltpu.SMEM), vmem, vmem, pl.BlockSpec(memory_space=pltpu.HBM)],
        out_specs=vmem,
        out_shape=jax.ShapeDtypeStruct((weight.shape[0], tok), F32),
        scratch_shapes=[
            pltpu.VMEM((2 * channels, tok), BF16),
            pltpu.VMEM((weight.shape[0], 2 * channels), BF16),
            pltpu.SemaphoreType.DMA,
        ],
        compiler_params=pltpu.CompilerParams(vmem_limit_bytes=16 << 20),
        cost_estimate=pl.CostEstimate(flops=4 * weight.shape[0] * channels * tok,
                                      bytes_accessed=4 << 20, transcendentals=0),
        name="near_half",
    )(grp, own, near, weight)


def project_body(*refs):
    grp_ref, far_ref, diag_ref, halos, half_ref, weight_hbm, taps_ref = refs[0], refs[1], refs[2], refs[3:7], *refs[7:10]
    message_ref, kept_ref, token_ref, halo_ref, stream_ref, spread_ref, part_ref, weight_ref = refs[11:19]
    sem, weight_sem = refs[19:]
    channels, tok = far_ref.shape
    grp = grp_ref[0]
    load = pltpu.make_async_copy(weight_hbm, weight_ref, weight_sem)
    load.start()
    side = grp % 2
    token_ref[pl.ds(pl.multiple_of(side * channels, 64), channels), :] = far_ref[...]
    token_ref[pl.ds(pl.multiple_of((1 - side) * channels, 64), channels), :] = diag_ref[...]
    for mask, halo in zip(MASKS, halos):
        halo_ref[pl.ds(pl.multiple_of((grp ^ mask) * channels, 64), channels), :] = halo[...]
    load.wait()
    stream_ref[:, :LANES] = jnp.dot(weight_ref[...], halo_ref[...], preferred_element_type=F32)
    first = pl.multiple_of((1 - grp // 2) * 2 * channels, LANES)
    step = 256
    for col in range(0, tok, step):
        stream_ref[:, LANES + col:LANES + col + step] = half_ref[:, col:col + step] + jnp.dot(
            weight_ref[:, pl.ds(first, 2 * channels)], token_ref[:, col:col + step], preferred_element_type=F32
        )
    rows = 16

    def chunk(index, carry):
        row = pl.multiple_of(index * rows, rows)
        smooth = []
        for s in range(3):
            x = stream_ref[pl.ds(s * channels + row, rows), :].astype(BF16).astype(F32)
            w = [taps_ref[pl.ds(row, rows), 3 * tap + s:3 * tap + s + 1] for tap in range(3)]
            y = w[0] * x + w[1] * pltpu.roll(x, 1, 1) + w[2] * pltpu.roll(x, 2, 1)
            smooth.append(y[:, LANES:])
        kept_ref[0, pl.ds(row, rows), :] = smooth[0].astype(BF16)
        signal = smooth[2] * smooth[1]
        kept_ref[1, pl.ds(row, rows), :] = signal.astype(BF16)
        for part in range(8):
            spread_ref[pl.ds(row * 8 + part, rows, stride=8), :] = signal[:, part * LANES:(part + 1) * LANES]
        return carry

    shards, per_dest = part_ref.shape[:2]
    groups = 4
    each = channels // groups
    copies = []
    for group in range(groups):
        lax.fori_loop(group * each // rows, (group + 1) * each // rows, chunk, 0)
        dests = pl.ds(group * shards // groups, shards // groups)
        ready = spread_ref[pl.ds(group * each * 8, each * 8), :].astype(BF16)
        part_ref[dests] = ready.reshape(shards // groups, *part_ref.shape[1:])
        copies.append(pltpu.make_async_copy(
            part_ref.at[dests], message_ref.at[dests, pl.ds(4 * per_dest, per_dest)], sem.at[group]
        ))
        copies[-1].start()
    for copy in copies:
        copy.wait()


def project(grp, far, diag, halos, half, weight, taps, packed):
    channels, tok = far.shape
    width = tok + LANES
    vmem = pl.BlockSpec(memory_space=pltpu.VMEM)
    anywhere = pl.BlockSpec(memory_space=pltpu.HBM)
    shards, pieces = packed.shape[:2]
    return pl.pallas_call(
        project_body,
        in_specs=[pl.BlockSpec(memory_space=pltpu.SMEM)] + [vmem] * 7 + [anywhere, vmem, anywhere],
        out_specs=[anywhere, vmem],
        out_shape=[
            jax.ShapeDtypeStruct(packed.shape, BF16),
            jax.ShapeDtypeStruct((2, channels, tok), BF16),
        ],
        scratch_shapes=[
            pltpu.VMEM((2 * channels, tok), BF16),
            pltpu.VMEM((4 * channels, LANES), BF16),
            pltpu.VMEM((3 * channels, width), F32),
            pltpu.VMEM((channels * 8, LANES), F32),
            pltpu.VMEM((shards, pieces // 5, 8, LANES), BF16),
            pltpu.VMEM(weight.shape, BF16),
            pltpu.SemaphoreType.DMA((4,)),
            pltpu.SemaphoreType.DMA,
        ],
        input_output_aliases={10: 0},
        compiler_params=pltpu.CompilerParams(vmem_limit_bytes=PROJECT_VMEM),
        cost_estimate=pl.CostEstimate(flops=3 * channels * 4 * channels * width,
                                      bytes_accessed=6 << 20, transcendentals=0),
        name="project",
    )(grp, far, diag, *halos, half, weight, taps, packed)


def convolve_body(m_ref, wave_hbm, twist_ref, out_ref,
                  spread_ref, grid_ref, mid_ref, tall_ref, done_ref, wave_ref, sems, wave_sems):
    channels, shards, pieces, lanes = done_ref.shape
    rows_dev = pieces // 2
    freqs = twist_ref.shape[0]
    first_ref, forward_ref, backward_ref, last_ref = (wave_ref.at[i] for i in range(4))
    loads = [
        pltpu.make_async_copy(wave_hbm.at[pl.ds(i * freqs, freqs)], wave_ref.at[i], wave_sems.at[i]) for i in range(4)
    ]
    for load in loads:
        load.start()
    cosine, sine = twist_ref[:, :COLS], twist_ref[:, COLS:]

    def arrange(c):
        spread_ref[c] = m_ref[:, 4 * channels + c].astype(F32).reshape(shards * pieces, lanes)
        for a in range(rows_dev):
            for h in range(2):
                grid_ref[c, a * shards:(a + 1) * shards, h * lanes:(h + 1) * lanes] = spread_ref[
                    c, pl.ds(2 * a + h, shards, stride=pieces), :].astype(BF16)

    def rows_forward(c):
        real = jnp.dot(first_ref[:, :COLS], grid_ref[c], preferred_element_type=F32)
        return real, jnp.dot(first_ref[:, COLS:], grid_ref[c], preferred_element_type=F32)

    def twist_forward(c, wave):
        real, imag = wave
        mid_ref[c, :, :COLS] = (real * cosine + imag * sine).astype(BF16)
        mid_ref[c, :, COLS:] = (imag * cosine - real * sine).astype(BF16)

    def cols_forward(c):
        return jnp.dot(mid_ref[c], forward_ref[...], preferred_element_type=F32)

    def respond(c, freq):
        for h in range(2):
            low, high = h * lanes, COLS + h * lanes
            real, imag = freq[:, low:low + lanes], freq[:, high:high + lanes]
            h_real, h_imag = (
                m_ref[:, 4 * c + 2 * part + h].astype(F32).reshape(freqs, lanes) for part in range(2)
            )
            mid_ref[c, :, low:low + lanes] = (real * h_real - imag * h_imag).astype(BF16)
            mid_ref[c, :, high:high + lanes] = (real * h_imag + imag * h_real).astype(BF16)

    def cols_backward(c):
        return jnp.dot(mid_ref[c], backward_ref[...], preferred_element_type=F32)

    def twist_backward(c, back):
        real, imag = back[:, :COLS], back[:, COLS:]
        tall_ref[c, :freqs, :] = (real * cosine - imag * sine).astype(BF16)
        tall_ref[c, freqs:, :] = (imag * cosine + real * sine).astype(BF16)

    def rows_backward(c):
        out = jnp.dot(last_ref[:COLS, :], tall_ref[c, :freqs], preferred_element_type=F32)
        return out + jnp.dot(last_ref[COLS:, :], tall_ref[c, freqs:], preferred_element_type=F32)

    def send(c, out):
        for a in range(rows_dev):
            for h in range(2):
                spread_ref[c, pl.ds(2 * a + h, shards, stride=pieces), :] = out[
                    a * shards:(a + 1) * shards, h * lanes:(h + 1) * lanes]
        done_ref[c] = spread_ref[c].reshape(shards, pieces, lanes).astype(BF16)
        pltpu.make_async_copy(done_ref.at[c], out_ref.at[:, c], sems.at[c]).start()

    for c in range(channels):
        arrange(c)
    stages = (
        (rows_forward, twist_forward), (cols_forward, respond), (cols_backward, twist_backward), (rows_backward, send)
    )
    waiting = None
    for stage, (multiply, finish) in enumerate(stages):
        loads[stage].wait()
        for c in range(channels):
            product = multiply(c)
            if waiting is not None:
                waiting[0](*waiting[1:])
            waiting = (finish, c, product)
    waiting[0](*waiting[1:])
    for c in range(channels):
        pltpu.make_async_copy(done_ref.at[c], out_ref.at[:, c], sems.at[c]).wait()


def convolve(received, tables):
    shards, kinds, pieces, lanes = received.shape
    channels = kinds // 5
    freqs = shards * pieces
    vmem = pl.BlockSpec(memory_space=pltpu.VMEM)
    return pl.pallas_call(
        convolve_body,
        in_specs=[vmem, pl.BlockSpec(memory_space=pltpu.HBM), vmem],
        out_specs=pl.BlockSpec(memory_space=pltpu.HBM),
        out_shape=jax.ShapeDtypeStruct((shards, channels, pieces, lanes), BF16),
        scratch_shapes=[
            pltpu.VMEM((channels, shards * pieces, lanes), F32),
            pltpu.VMEM((channels, freqs // 2, COLS), BF16),
            pltpu.VMEM((channels, freqs, 2 * COLS), BF16),
            pltpu.VMEM((channels, 2 * freqs, COLS), BF16),
            pltpu.VMEM((channels, shards, pieces, lanes), BF16),
            pltpu.VMEM((4, freqs, 2 * COLS), BF16),
            pltpu.SemaphoreType.DMA((channels,)),
            pltpu.SemaphoreType.DMA((4,)),
        ],
        compiler_params=pltpu.CompilerParams(vmem_limit_bytes=CONVOLVE_VMEM),
        cost_estimate=pl.CostEstimate(flops=3 << 30, bytes_accessed=6 << 20, transcendentals=0),
        name="convolve",
    )(received, *tables)


def gated_body(y_ref, kept_hbm, bias_ref, out_ref, spread_ref, kept_ref, sem):
    channels = out_ref.shape[0]
    load = pltpu.make_async_copy(kept_hbm, kept_ref, sem)
    load.start()
    spread_ref[...] = y_ref[...].astype(F32)
    bias = bias_ref[...]
    load.wait()
    for part in range(8):
        cols = slice(part * LANES, (part + 1) * LANES)
        y = spread_ref[pl.ds(part, channels, stride=8), :]
        direct = bias * kept_ref[1, :, cols].astype(F32)
        out_ref[:, cols] = (kept_ref[0, :, cols].astype(F32) * (y + direct)).astype(BF16)


def gated(y, kept, bias):
    vmem = pl.BlockSpec(memory_space=pltpu.VMEM)
    return pl.pallas_call(
        gated_body,
        in_specs=[vmem, pl.BlockSpec(memory_space=pltpu.HBM), vmem],
        out_specs=vmem,
        out_shape=jax.ShapeDtypeStruct(kept.shape[1:], BF16),
        scratch_shapes=[
            pltpu.VMEM(y.shape, F32),
            pltpu.VMEM(kept.shape, BF16),
            pltpu.SemaphoreType.DMA,
        ],
        compiler_params=pltpu.CompilerParams(vmem_limit_bytes=GATED_VMEM),
        cost_estimate=pl.CostEstimate(flops=4 * y.size, bytes_accessed=8 * y.size, transcendentals=0),
        name="gated",
    )(y, kept, bias)


def mixed_body(*refs):
    values, weights, out_ref = refs[:2], refs[2:4], refs[-1]
    total = refs[4][...] if len(refs) == 6 else 0.0
    for w, v in zip(weights, values):
        total = total + jnp.dot(w[...], v[...], preferred_element_type=F32)
    out_ref[...] = total.astype(out_ref.dtype)


def mixed(values, weights, dtype, *earlier):
    vmem = pl.BlockSpec(memory_space=pltpu.VMEM)
    channels, tok = values[0].shape
    return pl.pallas_call(
        mixed_body,
        in_specs=[vmem] * (4 + len(earlier)),
        out_specs=vmem,
        out_shape=jax.ShapeDtypeStruct((weights[0].shape[0], tok), dtype),
        compiler_params=pltpu.CompilerParams(vmem_limit_bytes=12 << 20),
        cost_estimate=pl.CostEstimate(flops=4 * channels * channels * tok, bytes_accessed=2 << 20, transcendentals=0),
        name="mixed",
    )(*values, *weights, *earlier)


def swapped(block, mask):
    return lax.ppermute(block, "grp", [(i, i ^ mask) for i in range(4)])


def shards(tokens, in_weight, short_weight, filter_bias, spectra, out_weight):
    shard_count = lax.axis_size("seq")
    grp = lax.axis_index("grp")
    channels, tok = tokens.shape
    per_dest = channels // shard_count

    far = swapped(tokens, 2)
    tail, own = lax.optimization_barrier((tokens[:, -LANES:], tokens))
    near = swapped(own, 1)
    route = [(i, i + 1) for i in range(shard_count - 1)]
    halo = lax.ppermute(tail, "seq", route)
    packed = pack_spectra(spectra, shard_count)
    halo, packed = lax.optimization_barrier((halo, packed))
    halo_far = swapped(halo, 2)
    halo_near = swapped(halo, 1)
    where = grp.reshape(1).astype(jnp.int32)
    weight = in_weight.reshape(3 * channels, -1)
    half = near_half(where, tokens, near, weight)
    far, halo_far, half = lax.optimization_barrier((far, halo_far, half))
    diag = swapped(far, 1)
    halos = [halo, halo_far, halo_near, swapped(halo_far, 1)]
    taps = jnp.transpose(short_weight, (2, 0, 1)).reshape(channels, 9)
    message, kept = project(where, far, diag, halos, half, weight, taps, packed)
    message, out_weight, filter_bias, later = lax.optimization_barrier(
        (message, out_weight, filter_bias, grp)
    )
    received = lax.all_to_all(message, "seq", 0, 0, tiled=True)

    turned = out_weight.T
    parts = [
        lax.dynamic_slice_in_dim(turned, (later ^ mask) * channels, channels, 0) for mask in MASKS
    ]
    weights = [parts[0]] + [swapped(part, mask) for part, mask in zip(parts[1:], MASKS[1:])]
    zero = jnp.minimum(later, 0)
    tables = [t + zero.astype(t.dtype) for t in transform_tables(shard_count, tok // COLS)]
    bias = filter_bias[:, None] + zero.astype(F32)
    received, weights, tables, bias = lax.optimization_barrier((received, weights, tables, bias))

    result = convolve(received, tables)
    back = lax.all_to_all(result, "seq", 0, 0, tiled=True).reshape(channels * 8, LANES)
    weighted = gated(back, kept, bias)
    far, near = swapped(weighted, 2), swapped(weighted, 1)
    half = mixed((weighted, near), (weights[0], weights[2]), F32)
    far, half = lax.optimization_barrier((far, half))
    return mixed((far, swapped(far, 1)), (weights[1], weights[3]), BF16, half)


def solution(mesh):
    in_specs = (
        P("grp", "seq"),
        P(None, "grp", None),
        P(None, None, "grp"),
        P("grp"),
        P(None, "grp", "seq", None),
        P("grp", None),
    )
    out_specs = P("grp", "seq")
    return jax.shard_map(shards, mesh=mesh, in_specs=in_specs, out_specs=out_specs, check_vma=False)
```

```python
import math

import jax
import jax.numpy as jnp
import numpy as np
from jax import lax
from jax.experimental import pallas as pl
from jax.experimental.pallas import tpu as pltpu
from jax.sharding import PartitionSpec as P

COLS = 256
FREQS = 512
LANES = 128
PROJECT_VMEM = 51500 << 10
GATED_VMEM = 54000 << 10
MIXED_VMEM = 12 << 20
CONVOLVE_VMEM = 50000 << 10
MASKS = (0, 2, 1, 3)
BF16 = jnp.bfloat16
F32 = jnp.float32


def unit_circle(rows, cols, period):
    angle = (np.outer(rows, cols) % period) * (2.0 * math.pi / period)
    return np.cos(angle), np.sin(angle)


def transform_tables(shard_count, rows_dev):
    half = shard_count * rows_dev
    order = (np.arange(shard_count)[None, :] * rows_dev + np.arange(rows_dev)[:, None]).reshape(-1)
    freqs = np.arange(2 * half)
    cols = np.arange(COLS)
    padded = 2 * half * COLS
    cos1, sin1 = unit_circle(freqs, order, 2 * half)
    cos2, sin2 = unit_circle(cols, cols, COLS)
    cost, sint = unit_circle(freqs, cols, padded)
    first = np.concatenate([cos1, -sin1], 1)
    forward = np.block([[cos2, -sin2], [sin2, cos2]])
    backward = np.block([[cos2, sin2], [-sin2, cos2]])
    last = np.concatenate([cos1.T, -sin1.T], 0) / padded
    waves = np.concatenate([first, forward, backward, last], 0)
    return jnp.asarray(waves, BF16), jnp.asarray(np.concatenate([cost, sint], 1), F32)


def pack_spectra_body(spec_ref, out_ref):
    dests = out_ref.shape[0]
    per_dest = spec_ref.shape[1] // dests
    for part in range(2):
        for h in range(2):
            piece = spec_ref[part, :, :, h * LANES:(h + 1) * LANES]
            piece = piece.reshape(dests, per_dest, *piece.shape[1:]).astype(BF16)
            for c in range(per_dest):
                out_ref[:, 4 * c + 2 * part + h] = piece[:, c]


def pack_spectra(spectra, shard_count):
    _, channels, rows, cols = spectra.shape
    per_dest = channels // shard_count
    steps = 2
    return pl.pallas_call(
        pack_spectra_body,
        grid=(steps,),
        in_specs=[pl.BlockSpec((2, channels // steps, rows, cols), lambda i: (0, i, 0, 0))],
        out_specs=pl.BlockSpec((shard_count // steps, 4 * per_dest, rows, LANES), lambda i: (i, 0, 0, 0)),
        out_shape=jax.ShapeDtypeStruct((shard_count, 5 * per_dest, rows, LANES), BF16),
        cost_estimate=pl.CostEstimate(flops=0, bytes_accessed=6 * spectra.size, transcendentals=0),
        name="pack_spectra",
    )(spectra)


def filtered(stream, taps_ref, row, s):
    x = stream.astype(F32)
    w = [taps_ref[pl.ds(row, x.shape[0]), 3 * tap + s:3 * tap + s + 1] for tap in range(3)]
    y = w[0] * x + w[1] * pltpu.roll(x, 1, 1) + w[2] * pltpu.roll(x, 2, 1)
    return y[:, LANES:]


def project_body(*refs):
    grp_ref, mains, halos, weight_ref, taps_ref = refs[0], refs[1:5], refs[5:9], refs[9], refs[10]
    message_ref, gate_ref, token_ref, stream_ref, spread_ref, part_ref, sem = refs[12:]
    channels, tok = mains[0].shape
    width = tok + LANES
    grp = grp_ref[0]
    for mask, main, halo in zip(MASKS, mains, halos):
        rows = pl.ds(pl.multiple_of((grp ^ mask) * channels, 64), channels)
        token_ref[rows, :LANES] = halo[...]
        token_ref[rows, LANES:] = main[...]
    step = 384
    for col in range(0, width, step):
        stream_ref[:, col:col + step] = jnp.dot(
            weight_ref[...], token_ref[:, col:col + step], preferred_element_type=F32
        )
    rows = 16

    def chunk(index, carry):
        row = pl.multiple_of(index * rows, rows)
        gate_ref[pl.ds(row, rows), :] = stream_ref[pl.ds(row, rows), :].astype(BF16)
        first, second = (
            filtered(stream_ref[pl.ds(s * channels + row, rows), :].astype(BF16), taps_ref, row, s) for s in (1, 2)
        )
        signal = second * first
        for part in range(8):
            spread_ref[pl.ds(row * 8 + part, rows, stride=8), :] = signal[:, part * LANES:(part + 1) * LANES]
        return carry

    shards, per_dest = part_ref.shape[:2]
    groups = 4
    each = channels // groups
    copies = []
    for group in range(groups):
        lax.fori_loop(group * each // rows, (group + 1) * each // rows, chunk, 0)
        dests = pl.ds(group * shards // groups, shards // groups)
        ready = spread_ref[pl.ds(group * each * 8, each * 8), :].astype(BF16)
        part_ref[dests] = ready.reshape(shards // groups, *part_ref.shape[1:])
        copies.append(pltpu.make_async_copy(
            part_ref.at[dests], message_ref.at[dests, pl.ds(4 * per_dest, per_dest)], sem.at[group]
        ))
        copies[-1].start()
    for copy in copies:
        copy.wait()


def project(grp, mains, halos, weight, taps, packed):
    channels, tok = mains[0].shape
    width = tok + LANES
    vmem = pl.BlockSpec(memory_space=pltpu.VMEM)
    anywhere = pl.BlockSpec(memory_space=pltpu.HBM)
    shards, pieces = packed.shape[:2]
    return pl.pallas_call(
        project_body,
        in_specs=[pl.BlockSpec(memory_space=pltpu.SMEM)] + [vmem] * 10 + [anywhere],
        out_specs=[anywhere, vmem],
        out_shape=[
            jax.ShapeDtypeStruct(packed.shape, BF16),
            jax.ShapeDtypeStruct((channels, width), BF16),
        ],
        scratch_shapes=[
            pltpu.VMEM((4 * channels, width), BF16),
            pltpu.VMEM((3 * channels, width), F32),
            pltpu.VMEM((channels * 8, LANES), F32),
            pltpu.VMEM((shards, pieces // 5, 8, LANES), BF16),
            pltpu.SemaphoreType.DMA((4,)),
        ],
        input_output_aliases={11: 0},
        compiler_params=pltpu.CompilerParams(vmem_limit_bytes=PROJECT_VMEM),
        cost_estimate=pl.CostEstimate(flops=2 * 3 * channels * 4 * channels * width,
                                      bytes_accessed=6 << 20, transcendentals=0),
        name="project",
    )(grp, *mains, *halos, weight, taps, packed)


def keep_body(message_hbm, gate_ref, taps_ref, kept_ref, part_ref, spread_ref, sem):
    channels = gate_ref.shape[0]
    per_dest = part_ref.shape[1]
    load = pltpu.make_async_copy(message_hbm.at[:, pl.ds(4 * per_dest, per_dest)], part_ref, sem)
    load.start()
    rows = 16

    def chunk(index, carry):
        row = pl.multiple_of(index * rows, rows)
        kept_ref[0, pl.ds(row, rows), :] = filtered(gate_ref[pl.ds(row, rows), :], taps_ref, row, 0).astype(BF16)
        return carry

    lax.fori_loop(0, channels // rows, chunk, 0)
    load.wait()
    spread_ref[...] = part_ref[...].astype(F32).reshape(spread_ref.shape)
    for part in range(8):
        column = spread_ref[pl.ds(part, channels, stride=8), :]
        kept_ref[1, :, part * LANES:(part + 1) * LANES] = column.astype(BF16)


def keep(message, gate_stream, taps):
    channels, width = gate_stream.shape
    shards, pieces = message.shape[:2]
    vmem = pl.BlockSpec(memory_space=pltpu.VMEM)
    return pl.pallas_call(
        keep_body,
        in_specs=[pl.BlockSpec(memory_space=pltpu.HBM), vmem, vmem],
        out_specs=vmem,
        out_shape=jax.ShapeDtypeStruct((2, channels, width - LANES), BF16),
        scratch_shapes=[
            pltpu.VMEM((shards, pieces // 5, 8, LANES), BF16),
            pltpu.VMEM((channels * 8, LANES), F32),
            pltpu.SemaphoreType.DMA,
        ],
        cost_estimate=pl.CostEstimate(flops=8 * channels * width, bytes_accessed=2 << 20, transcendentals=0),
        name="keep",
    )(message, gate_stream, taps)


def convolve_body(m_ref, wave_hbm, twist_ref, out_ref,
                  spread_ref, grid_ref, mid_ref, tall_ref, done_ref, wave_ref, sems, wave_sems):
    channels, shards, pieces, lanes = done_ref.shape
    rows_dev = pieces // 2
    freqs = twist_ref.shape[0]
    first_ref, forward_ref, backward_ref, last_ref = (wave_ref.at[i] for i in range(4))
    loads = [
        pltpu.make_async_copy(wave_hbm.at[pl.ds(i * freqs, freqs)], wave_ref.at[i], wave_sems.at[i]) for i in range(4)
    ]
    for load in loads:
        load.start()
    cosine, sine = twist_ref[:, :COLS], twist_ref[:, COLS:]

    def arrange(c):
        spread_ref[c] = m_ref[:, 4 * channels + c].astype(F32).reshape(shards * pieces, lanes)
        for a in range(rows_dev):
            for h in range(2):
                grid_ref[c, a * shards:(a + 1) * shards, h * lanes:(h + 1) * lanes] = spread_ref[
                    c, pl.ds(2 * a + h, shards, stride=pieces), :].astype(BF16)

    def rows_forward(c):
        real = jnp.dot(first_ref[:, :COLS], grid_ref[c], preferred_element_type=F32)
        return real, jnp.dot(first_ref[:, COLS:], grid_ref[c], preferred_element_type=F32)

    def twist_forward(c, wave):
        real, imag = wave
        mid_ref[c, :, :COLS] = (real * cosine + imag * sine).astype(BF16)
        mid_ref[c, :, COLS:] = (imag * cosine - real * sine).astype(BF16)

    def cols_forward(c):
        return jnp.dot(mid_ref[c], forward_ref[...], preferred_element_type=F32)

    def respond(c, freq):
        for h in range(2):
            low, high = h * lanes, COLS + h * lanes
            real, imag = freq[:, low:low + lanes], freq[:, high:high + lanes]
            h_real, h_imag = (
                m_ref[:, 4 * c + 2 * part + h].astype(F32).reshape(freqs, lanes) for part in range(2)
            )
            mid_ref[c, :, low:low + lanes] = (real * h_real - imag * h_imag).astype(BF16)
            mid_ref[c, :, high:high + lanes] = (real * h_imag + imag * h_real).astype(BF16)

    def cols_backward(c):
        return jnp.dot(mid_ref[c], backward_ref[...], preferred_element_type=F32)

    def twist_backward(c, back):
        real, imag = back[:, :COLS], back[:, COLS:]
        tall_ref[c, :freqs, :] = (real * cosine - imag * sine).astype(BF16)
        tall_ref[c, freqs:, :] = (imag * cosine + real * sine).astype(BF16)

    def rows_backward(c):
        out = jnp.dot(last_ref[:COLS, :], tall_ref[c, :freqs], preferred_element_type=F32)
        return out + jnp.dot(last_ref[COLS:, :], tall_ref[c, freqs:], preferred_element_type=F32)

    def send(c, out):
        for a in range(rows_dev):
            for h in range(2):
                spread_ref[c, pl.ds(2 * a + h, shards, stride=pieces), :] = out[
                    a * shards:(a + 1) * shards, h * lanes:(h + 1) * lanes]
        done_ref[c] = spread_ref[c].reshape(shards, pieces, lanes).astype(BF16)
        pltpu.make_async_copy(done_ref.at[c], out_ref.at[:, c], sems.at[c]).start()

    for c in range(channels):
        arrange(c)
    stages = (
        (rows_forward, twist_forward), (cols_forward, respond), (cols_backward, twist_backward), (rows_backward, send)
    )
    waiting = None
    for stage, (multiply, finish) in enumerate(stages):
        loads[stage].wait()
        for c in range(channels):
            product = multiply(c)
            if waiting is not None:
                waiting[0](*waiting[1:])
            waiting = (finish, c, product)
    waiting[0](*waiting[1:])
    for c in range(channels):
        pltpu.make_async_copy(done_ref.at[c], out_ref.at[:, c], sems.at[c]).wait()


def convolve(received, tables):
    shards, kinds, pieces, lanes = received.shape
    channels = kinds // 5
    freqs = shards * pieces
    vmem = pl.BlockSpec(memory_space=pltpu.VMEM)
    return pl.pallas_call(
        convolve_body,
        in_specs=[vmem, pl.BlockSpec(memory_space=pltpu.HBM), vmem],
        out_specs=pl.BlockSpec(memory_space=pltpu.HBM),
        out_shape=jax.ShapeDtypeStruct((shards, channels, pieces, lanes), BF16),
        scratch_shapes=[
            pltpu.VMEM((channels, shards * pieces, lanes), F32),
            pltpu.VMEM((channels, freqs // 2, COLS), BF16),
            pltpu.VMEM((channels, freqs, 2 * COLS), BF16),
            pltpu.VMEM((channels, 2 * freqs, COLS), BF16),
            pltpu.VMEM((channels, shards, pieces, lanes), BF16),
            pltpu.VMEM((4, freqs, 2 * COLS), BF16),
            pltpu.SemaphoreType.DMA((channels,)),
            pltpu.SemaphoreType.DMA((4,)),
        ],
        compiler_params=pltpu.CompilerParams(vmem_limit_bytes=CONVOLVE_VMEM),
        cost_estimate=pl.CostEstimate(flops=3 << 30, bytes_accessed=6 << 20, transcendentals=0),
        name="convolve",
    )(received, *tables)


def gated_body(y_ref, kept_hbm, bias_ref, early_ref, late_ref, spread_ref, kept_ref, sem):
    channels = early_ref.shape[0]
    load = pltpu.make_async_copy(kept_hbm, kept_ref, sem)
    load.start()
    spread_ref[...] = y_ref[...].astype(F32)
    bias = bias_ref[...]
    load.wait()
    for part in range(8):
        cols = slice(part * LANES, (part + 1) * LANES)
        y = spread_ref[pl.ds(part, channels, stride=8), :]
        direct = bias * kept_ref[1, :, cols].astype(F32)
        out_ref, at = (early_ref, part) if part < 4 else (late_ref, part - 4)
        value = kept_ref[0, :, cols].astype(F32) * (y + direct)
        out_ref[:, at * LANES:(at + 1) * LANES] = value.astype(BF16)


def gated(y, kept, bias):
    vmem = pl.BlockSpec(memory_space=pltpu.VMEM)
    return pl.pallas_call(
        gated_body,
        in_specs=[vmem, pl.BlockSpec(memory_space=pltpu.HBM), vmem],
        out_specs=[vmem] * 2,
        out_shape=[jax.ShapeDtypeStruct((kept.shape[1], kept.shape[2] // 2), BF16)] * 2,
        scratch_shapes=[
            pltpu.VMEM(y.shape, F32),
            pltpu.VMEM(kept.shape, BF16),
            pltpu.SemaphoreType.DMA,
        ],
        compiler_params=pltpu.CompilerParams(vmem_limit_bytes=GATED_VMEM),
        cost_estimate=pl.CostEstimate(flops=4 * y.size, bytes_accessed=8 * y.size, transcendentals=0),
        name="gated",
    )(y, kept, bias)


def mixed_body(*refs):
    values, weights, out_ref = refs[:4], refs[4:8], refs[-1]
    total = jnp.dot(weights[0][...], values[0][...], preferred_element_type=F32)
    for w, v in zip(weights[1:], values[1:]):
        total = total + jnp.dot(w[...], v[...], preferred_element_type=F32)
    out_ref[...] = total.astype(BF16)


def mixed(values, weights, half, *earlier):
    channels, tok = values[0].shape
    whole = [pl.BlockSpec(memory_space=pltpu.VMEM)] * 8
    return pl.pallas_call(
        mixed_body,
        grid=(1,),
        in_specs=whole + [pl.BlockSpec(memory_space=pl.ANY)] * len(earlier),
        out_specs=pl.BlockSpec((weights[0].shape[0], tok), lambda i: (0, half)),
        out_shape=jax.ShapeDtypeStruct((weights[0].shape[0], 2 * tok), BF16),
        input_output_aliases={8: 0} if earlier else {},
        compiler_params=pltpu.CompilerParams(vmem_limit_bytes=MIXED_VMEM),
        cost_estimate=pl.CostEstimate(flops=8 * channels * channels * tok, bytes_accessed=2 << 20, transcendentals=0),
        name="mixed",
    )(*values, *weights, *earlier)


def swapped(block, mask):
    return lax.ppermute(block, "grp", [(i, i ^ mask) for i in range(4)])


def shards(tokens, in_weight, short_weight, filter_bias, spectra, out_weight):
    shard_count = lax.axis_size("seq")
    grp = lax.axis_index("grp")
    channels, tok = tokens.shape
    per_dest = channels // shard_count

    far = swapped(tokens, 2)
    near = swapped(tokens, 1)
    route = [(i, i + 1) for i in range(shard_count - 1)]
    halo = lax.ppermute(tokens[:, -LANES:], "seq", route)
    packed = pack_spectra(spectra, shard_count)
    halo, packed = lax.optimization_barrier((halo, packed))
    halo_far = swapped(halo, 2)
    halo_near = swapped(halo, 1)
    far, halo_far = lax.optimization_barrier((far, halo_far))
    mains = [tokens, far, near, swapped(far, 1)]
    halos = [halo, halo_far, halo_near, swapped(halo_far, 1)]
    taps = jnp.transpose(short_weight, (2, 0, 1)).reshape(channels, 9)
    message, gate_stream = project(
        grp.reshape(1).astype(jnp.int32), mains, halos, in_weight.reshape(3 * channels, -1), taps, packed
    )
    message, out_weight, filter_bias, later, gate_stream = lax.optimization_barrier(
        (message, out_weight, filter_bias, grp, gate_stream)
    )
    kept = keep(message, gate_stream, taps)
    received = lax.all_to_all(message, "seq", 0, 0, tiled=True)

    turned = out_weight.T
    parts = [
        lax.dynamic_slice_in_dim(turned, (later ^ mask) * channels, channels, 0) for mask in MASKS
    ]
    weights = [parts[0]] + [swapped(part, mask) for part, mask in zip(parts[1:], MASKS[1:])]
    zero = jnp.minimum(later, 0)
    tables = [t + zero.astype(t.dtype) for t in transform_tables(shard_count, tok // COLS)]
    bias = filter_bias[:, None] + zero.astype(F32)
    received, weights, tables, bias, kept = lax.optimization_barrier((received, weights, tables, bias, kept))

    result = convolve(received, tables)
    back = lax.all_to_all(result, "seq", 0, 0, tiled=True).reshape(channels * 8, LANES)
    early, late = gated(back, kept, bias)
    far_early, far_late = swapped(early, 2), swapped(late, 2)
    far_early, early, late = lax.optimization_barrier((far_early, early, late))
    near_early, near_late = swapped(early, 1), swapped(late, 1)
    out = mixed((early, far_early, near_early, swapped(far_early, 1)), weights, 0)
    return mixed((late, far_late, near_late, swapped(far_late, 1)), weights, 1, out)


def solution(mesh):
    in_specs = (
        P("grp", "seq"),
        P(None, "grp", None),
        P(None, None, "grp"),
        P("grp"),
        P(None, "grp", "seq", None),
        P("grp", None),
    )
    out_specs = P("grp", "seq")
    return jax.shard_map(shards, mesh=mesh, in_specs=in_specs, out_specs=out_specs, check_vma=False)
```

```python
import math

import jax
import jax.numpy as jnp
import numpy as np
from jax import lax
from jax.experimental import pallas as pl
from jax.experimental.pallas import tpu as pltpu
from jax.sharding import PartitionSpec as P

COLS = 256
FREQS = 512
LANES = 128
PROJECT_VMEM = 53100 << 10
GATED_VMEM = 54000 << 10
MIXED_VMEM = 12 << 20
CONVOLVE_VMEM = 50000 << 10
MASKS = (0, 2, 1, 3)
BF16 = jnp.bfloat16
F32 = jnp.float32


def unit_circle(rows, cols, period):
    angle = (np.outer(rows, cols) % period) * (2.0 * math.pi / period)
    return np.cos(angle), np.sin(angle)


def transform_tables(shard_count, rows_dev):
    half = shard_count * rows_dev
    order = (np.arange(shard_count)[None, :] * rows_dev + np.arange(rows_dev)[:, None]).reshape(-1)
    freqs = np.arange(2 * half)
    cols = np.arange(COLS)
    padded = 2 * half * COLS
    cos1, sin1 = unit_circle(freqs, order, 2 * half)
    cos2, sin2 = unit_circle(cols, cols, COLS)
    cost, sint = unit_circle(freqs, cols, padded)
    first = np.concatenate([cos1, -sin1], 1)
    forward = np.block([[cos2, -sin2], [sin2, cos2]])
    backward = np.block([[cos2, sin2], [-sin2, cos2]])
    last = np.concatenate([cos1.T, -sin1.T], 0) / padded
    waves = np.concatenate([first, forward, backward, last], 0)
    return jnp.asarray(waves, BF16), jnp.asarray(np.concatenate([cost, sint], 1), F32)


def pack_spectra_body(spec_ref, out_ref):
    dests = out_ref.shape[0]
    per_dest = spec_ref.shape[1] // dests
    for part in range(2):
        for h in range(2):
            piece = spec_ref[part, :, :, h * LANES:(h + 1) * LANES]
            piece = piece.reshape(dests, per_dest, *piece.shape[1:]).astype(BF16)
            for c in range(per_dest):
                out_ref[:, 4 * c + 2 * part + h] = piece[:, c]


def pack_spectra(spectra, shard_count):
    _, channels, rows, cols = spectra.shape
    per_dest = channels // shard_count
    steps = 2
    return pl.pallas_call(
        pack_spectra_body,
        grid=(steps,),
        in_specs=[pl.BlockSpec((2, channels // steps, rows, cols), lambda i: (0, i, 0, 0))],
        out_specs=pl.BlockSpec((shard_count // steps, 4 * per_dest, rows, LANES), lambda i: (i, 0, 0, 0)),
        out_shape=jax.ShapeDtypeStruct((shard_count, 5 * per_dest, rows, LANES), BF16),
        cost_estimate=pl.CostEstimate(flops=0, bytes_accessed=6 * spectra.size, transcendentals=0),
        name="pack_spectra",
    )(spectra)


def filtered(stream, taps_ref, row, s):
    x = stream.astype(F32)
    w = [taps_ref[pl.ds(row, x.shape[0]), 3 * tap + s:3 * tap + s + 1] for tap in range(3)]
    y = w[0] * x + w[1] * pltpu.roll(x, 1, 1) + w[2] * pltpu.roll(x, 2, 1)
    return y[:, LANES:]


def project_body(*refs):
    grp_ref, mains, halos, weight_hbm, taps_ref = refs[0], refs[1:5], refs[5:9], refs[9], refs[10]
    message_ref, gate_hbm, token_ref, stream_ref, spread_ref, part_ref, gate_ref, weight_ref, sem, gate_sem, load_sem = refs[12:]
    channels, tok = mains[0].shape
    width = tok + LANES
    grp = grp_ref[0]
    load = pltpu.make_async_copy(weight_hbm, weight_ref, load_sem)
    load.start()
    for mask, main, halo in zip(MASKS, mains, halos):
        rows = pl.ds(pl.multiple_of((grp ^ mask) * channels, 64), channels)
        token_ref[rows, :LANES] = halo[...]
        token_ref[rows, LANES:] = main[...]
    load.wait()
    step = 384
    for col in range(0, width, step):
        stream_ref[:, col:col + step] = jnp.dot(
            weight_ref[...], token_ref[:, col:col + step], preferred_element_type=F32
        )
    rows = 16

    def chunk(index, carry):
        row = pl.multiple_of(index * rows, rows)
        gate_ref[pl.ds(row, rows), :] = stream_ref[pl.ds(row, rows), :].astype(BF16)
        first, second = (
            filtered(stream_ref[pl.ds(s * channels + row, rows), :].astype(BF16), taps_ref, row, s) for s in (1, 2)
        )
        signal = second * first
        for part in range(8):
            spread_ref[pl.ds(row * 8 + part, rows, stride=8), :] = signal[:, part * LANES:(part + 1) * LANES]
        return carry

    shards, per_dest = part_ref.shape[:2]
    groups = 4
    each = channels // groups
    copies = []
    for group in range(groups):
        lax.fori_loop(group * each // rows, (group + 1) * each // rows, chunk, 0)
        dests = pl.ds(group * shards // groups, shards // groups)
        ready = spread_ref[pl.ds(group * each * 8, each * 8), :].astype(BF16)
        part_ref[dests] = ready.reshape(shards // groups, *part_ref.shape[1:])
        copies.append(pltpu.make_async_copy(
            part_ref.at[dests], message_ref.at[dests, pl.ds(4 * per_dest, per_dest)], sem.at[group]
        ))
        mine = pl.ds(group * each, each)
        copies.append(pltpu.make_async_copy(gate_ref.at[mine], gate_hbm.at[mine], gate_sem.at[group]))
        for copy in copies[-2:]:
            copy.start()
    for copy in copies:
        copy.wait()


def project(grp, mains, halos, weight, taps, packed):
    channels, tok = mains[0].shape
    width = tok + LANES
    vmem = pl.BlockSpec(memory_space=pltpu.VMEM)
    anywhere = pl.BlockSpec(memory_space=pltpu.HBM)
    shards, pieces = packed.shape[:2]
    return pl.pallas_call(
        project_body,
        in_specs=[pl.BlockSpec(memory_space=pltpu.SMEM)] + [vmem] * 8 + [anywhere, vmem, anywhere],
        out_specs=[anywhere] * 2,
        out_shape=[
            jax.ShapeDtypeStruct(packed.shape, BF16),
            jax.ShapeDtypeStruct((channels, width), BF16),
        ],
        scratch_shapes=[
            pltpu.VMEM((4 * channels, width), BF16),
            pltpu.VMEM((3 * channels, width), F32),
            pltpu.VMEM((channels * 8, LANES), F32),
            pltpu.VMEM((shards, pieces // 5, 8, LANES), BF16),
            pltpu.VMEM((channels, width), BF16),
            pltpu.VMEM(weight.shape, BF16),
            pltpu.SemaphoreType.DMA((4,)),
            pltpu.SemaphoreType.DMA((4,)),
            pltpu.SemaphoreType.DMA,
        ],
        input_output_aliases={11: 0},
        compiler_params=pltpu.CompilerParams(vmem_limit_bytes=PROJECT_VMEM),
        cost_estimate=pl.CostEstimate(flops=2 * 3 * channels * 4 * channels * width,
                                      bytes_accessed=6 << 20, transcendentals=0),
        name="project",
    )(grp, *mains, *halos, weight, taps, packed)


def keep_body(message_hbm, gate_ref, taps_ref, kept_ref, part_ref, spread_ref, sem):
    channels = gate_ref.shape[0]
    per_dest = part_ref.shape[1]
    load = pltpu.make_async_copy(message_hbm.at[:, pl.ds(4 * per_dest, per_dest)], part_ref, sem)
    load.start()
    rows = 16

    def chunk(index, carry):
        row = pl.multiple_of(index * rows, rows)
        kept_ref[0, pl.ds(row, rows), :] = filtered(gate_ref[pl.ds(row, rows), :], taps_ref, row, 0).astype(BF16)
        return carry

    lax.fori_loop(0, channels // rows, chunk, 0)
    load.wait()
    spread_ref[...] = part_ref[...].astype(F32).reshape(spread_ref.shape)
    for part in range(8):
        column = spread_ref[pl.ds(part, channels, stride=8), :]
        kept_ref[1, :, part * LANES:(part + 1) * LANES] = column.astype(BF16)


def keep(message, gate_stream, taps):
    channels, width = gate_stream.shape
    shards, pieces = message.shape[:2]
    vmem = pl.BlockSpec(memory_space=pltpu.VMEM)
    return pl.pallas_call(
        keep_body,
        in_specs=[pl.BlockSpec(memory_space=pltpu.HBM), vmem, vmem],
        out_specs=vmem,
        out_shape=jax.ShapeDtypeStruct((2, channels, width - LANES), BF16),
        scratch_shapes=[
            pltpu.VMEM((shards, pieces // 5, 8, LANES), BF16),
            pltpu.VMEM((channels * 8, LANES), F32),
            pltpu.SemaphoreType.DMA,
        ],
        cost_estimate=pl.CostEstimate(flops=8 * channels * width, bytes_accessed=2 << 20, transcendentals=0),
        name="keep",
    )(message, gate_stream, taps)


def convolve_body(m_ref, wave_hbm, twist_ref, out_ref,
                  spread_ref, grid_ref, mid_ref, tall_ref, done_ref, wave_ref, sems, wave_sems):
    channels, shards, pieces, lanes = done_ref.shape
    rows_dev = pieces // 2
    freqs = twist_ref.shape[0]
    first_ref, forward_ref, backward_ref, last_ref = (wave_ref.at[i] for i in range(4))
    loads = [
        pltpu.make_async_copy(wave_hbm.at[pl.ds(i * freqs, freqs)], wave_ref.at[i], wave_sems.at[i]) for i in range(4)
    ]
    for load in loads:
        load.start()
    cosine, sine = twist_ref[:, :COLS], twist_ref[:, COLS:]

    def arrange(c):
        spread_ref[c] = m_ref[:, 4 * channels + c].astype(F32).reshape(shards * pieces, lanes)
        for a in range(rows_dev):
            for h in range(2):
                grid_ref[c, a * shards:(a + 1) * shards, h * lanes:(h + 1) * lanes] = spread_ref[
                    c, pl.ds(2 * a + h, shards, stride=pieces), :].astype(BF16)

    def rows_forward(c):
        real = jnp.dot(first_ref[:, :COLS], grid_ref[c], preferred_element_type=F32)
        return real, jnp.dot(first_ref[:, COLS:], grid_ref[c], preferred_element_type=F32)

    def twist_forward(c, wave):
        real, imag = wave
        mid_ref[c, :, :COLS] = (real * cosine + imag * sine).astype(BF16)
        mid_ref[c, :, COLS:] = (imag * cosine - real * sine).astype(BF16)

    def cols_forward(c):
        return jnp.dot(mid_ref[c], forward_ref[...], preferred_element_type=F32)

    def respond(c, freq):
        for h in range(2):
            low, high = h * lanes, COLS + h * lanes
            real, imag = freq[:, low:low + lanes], freq[:, high:high + lanes]
            h_real, h_imag = (
                m_ref[:, 4 * c + 2 * part + h].astype(F32).reshape(freqs, lanes) for part in range(2)
            )
            mid_ref[c, :, low:low + lanes] = (real * h_real - imag * h_imag).astype(BF16)
            mid_ref[c, :, high:high + lanes] = (real * h_imag + imag * h_real).astype(BF16)

    def cols_backward(c):
        return jnp.dot(mid_ref[c], backward_ref[...], preferred_element_type=F32)

    def twist_backward(c, back):
        real, imag = back[:, :COLS], back[:, COLS:]
        tall_ref[c, :freqs, :] = (real * cosine - imag * sine).astype(BF16)
        tall_ref[c, freqs:, :] = (imag * cosine + real * sine).astype(BF16)

    def rows_backward(c):
        out = jnp.dot(last_ref[:COLS, :], tall_ref[c, :freqs], preferred_element_type=F32)
        return out + jnp.dot(last_ref[COLS:, :], tall_ref[c, freqs:], preferred_element_type=F32)

    def send(c, out):
        for a in range(rows_dev):
            for h in range(2):
                spread_ref[c, pl.ds(2 * a + h, shards, stride=pieces), :] = out[
                    a * shards:(a + 1) * shards, h * lanes:(h + 1) * lanes]
        done_ref[c] = spread_ref[c].reshape(shards, pieces, lanes).astype(BF16)
        pltpu.make_async_copy(done_ref.at[c], out_ref.at[:, c], sems.at[c]).start()

    for c in range(channels):
        arrange(c)
    stages = (
        (rows_forward, twist_forward), (cols_forward, respond), (cols_backward, twist_backward), (rows_backward, send)
    )
    waiting = None
    for stage, (multiply, finish) in enumerate(stages):
        loads[stage].wait()
        for c in range(channels):
            product = multiply(c)
            if waiting is not None:
                waiting[0](*waiting[1:])
            waiting = (finish, c, product)
    waiting[0](*waiting[1:])
    for c in range(channels):
        pltpu.make_async_copy(done_ref.at[c], out_ref.at[:, c], sems.at[c]).wait()


def convolve(received, tables):
    shards, kinds, pieces, lanes = received.shape
    channels = kinds // 5
    freqs = shards * pieces
    vmem = pl.BlockSpec(memory_space=pltpu.VMEM)
    return pl.pallas_call(
        convolve_body,
        in_specs=[vmem, pl.BlockSpec(memory_space=pltpu.HBM), vmem],
        out_specs=pl.BlockSpec(memory_space=pltpu.HBM),
        out_shape=jax.ShapeDtypeStruct((shards, channels, pieces, lanes), BF16),
        scratch_shapes=[
            pltpu.VMEM((channels, shards * pieces, lanes), F32),
            pltpu.VMEM((channels, freqs // 2, COLS), BF16),
            pltpu.VMEM((channels, freqs, 2 * COLS), BF16),
            pltpu.VMEM((channels, 2 * freqs, COLS), BF16),
            pltpu.VMEM((channels, shards, pieces, lanes), BF16),
            pltpu.VMEM((4, freqs, 2 * COLS), BF16),
            pltpu.SemaphoreType.DMA((channels,)),
            pltpu.SemaphoreType.DMA((4,)),
        ],
        compiler_params=pltpu.CompilerParams(vmem_limit_bytes=CONVOLVE_VMEM),
        cost_estimate=pl.CostEstimate(flops=3 << 30, bytes_accessed=6 << 20, transcendentals=0),
        name="convolve",
    )(received, *tables)


def gated_body(y_ref, kept_hbm, bias_ref, early_ref, late_ref, spread_ref, kept_ref, sem):
    channels = early_ref.shape[0]
    load = pltpu.make_async_copy(kept_hbm, kept_ref, sem)
    load.start()
    spread_ref[...] = y_ref[...].astype(F32)
    bias = bias_ref[...]
    load.wait()
    for part in range(8):
        cols = slice(part * LANES, (part + 1) * LANES)
        y = spread_ref[pl.ds(part, channels, stride=8), :]
        direct = bias * kept_ref[1, :, cols].astype(F32)
        out_ref, at = (early_ref, part) if part < 4 else (late_ref, part - 4)
        value = kept_ref[0, :, cols].astype(F32) * (y + direct)
        out_ref[:, at * LANES:(at + 1) * LANES] = value.astype(BF16)


def gated(y, kept, bias):
    vmem = pl.BlockSpec(memory_space=pltpu.VMEM)
    return pl.pallas_call(
        gated_body,
        in_specs=[vmem, pl.BlockSpec(memory_space=pltpu.HBM), vmem],
        out_specs=[vmem] * 2,
        out_shape=[jax.ShapeDtypeStruct((kept.shape[1], kept.shape[2] // 2), BF16)] * 2,
        scratch_shapes=[
            pltpu.VMEM(y.shape, F32),
            pltpu.VMEM(kept.shape, BF16),
            pltpu.SemaphoreType.DMA,
        ],
        compiler_params=pltpu.CompilerParams(vmem_limit_bytes=GATED_VMEM),
        cost_estimate=pl.CostEstimate(flops=4 * y.size, bytes_accessed=8 * y.size, transcendentals=0),
        name="gated",
    )(y, kept, bias)


def mixed_body(*refs):
    values, weights, out_ref = refs[:4], refs[4:8], refs[-1]
    total = jnp.dot(weights[0][...], values[0][...], preferred_element_type=F32)
    for w, v in zip(weights[1:], values[1:]):
        total = total + jnp.dot(w[...], v[...], preferred_element_type=F32)
    out_ref[...] = total.astype(BF16)


def mixed(values, weights, half, *earlier):
    channels, tok = values[0].shape
    whole = [pl.BlockSpec(memory_space=pltpu.VMEM)] * 8
    return pl.pallas_call(
        mixed_body,
        grid=(1,),
        in_specs=whole + [pl.BlockSpec(memory_space=pl.ANY)] * len(earlier),
        out_specs=pl.BlockSpec((weights[0].shape[0], tok), lambda i: (0, half)),
        out_shape=jax.ShapeDtypeStruct((weights[0].shape[0], 2 * tok), BF16),
        input_output_aliases={8: 0} if earlier else {},
        compiler_params=pltpu.CompilerParams(vmem_limit_bytes=MIXED_VMEM),
        cost_estimate=pl.CostEstimate(flops=8 * channels * channels * tok, bytes_accessed=2 << 20, transcendentals=0),
        name="mixed",
    )(*values, *weights, *earlier)


def swapped(block, mask):
    return lax.ppermute(block, "grp", [(i, i ^ mask) for i in range(4)])


def shards(tokens, in_weight, short_weight, filter_bias, spectra, out_weight):
    shard_count = lax.axis_size("seq")
    grp = lax.axis_index("grp")
    channels, tok = tokens.shape
    per_dest = channels // shard_count

    far = swapped(tokens, 2)
    near = swapped(tokens, 1)
    route = [(i, i + 1) for i in range(shard_count - 1)]
    halo = lax.ppermute(tokens[:, -LANES:], "seq", route)
    packed = pack_spectra(spectra, shard_count)
    halo, packed = lax.optimization_barrier((halo, packed))
    halo_far = swapped(halo, 2)
    halo_near = swapped(halo, 1)
    far, halo_far = lax.optimization_barrier((far, halo_far))
    mains = [tokens, far, near, swapped(far, 1)]
    halos = [halo, halo_far, halo_near, swapped(halo_far, 1)]
    taps = jnp.transpose(short_weight, (2, 0, 1)).reshape(channels, 9)
    message, gate_stream = project(
        grp.reshape(1).astype(jnp.int32), mains, halos, in_weight.reshape(3 * channels, -1), taps, packed
    )
    message, out_weight, filter_bias, later, gate_stream = lax.optimization_barrier(
        (message, out_weight, filter_bias, grp, gate_stream)
    )
    kept = keep(message, gate_stream, taps)
    received = lax.all_to_all(message, "seq", 0, 0, tiled=True)

    turned = out_weight.T
    parts = [
        lax.dynamic_slice_in_dim(turned, (later ^ mask) * channels, channels, 0) for mask in MASKS
    ]
    weights = [parts[0]] + [swapped(part, mask) for part, mask in zip(parts[1:], MASKS[1:])]
    zero = jnp.minimum(later, 0)
    tables = [t + zero.astype(t.dtype) for t in transform_tables(shard_count, tok // COLS)]
    bias = filter_bias[:, None] + zero.astype(F32)
    received, weights, tables, bias, kept = lax.optimization_barrier((received, weights, tables, bias, kept))

    result = convolve(received, tables)
    back = lax.all_to_all(result, "seq", 0, 0, tiled=True).reshape(channels * 8, LANES)
    early, late = gated(back, kept, bias)
    far_early, far_late = swapped(early, 2), swapped(late, 2)
    near_early, near_late = swapped(early, 1), swapped(late, 1)
    out = mixed((early, far_early, near_early, swapped(far_early, 1)), weights, 0)
    return mixed((late, far_late, near_late, swapped(far_late, 1)), weights, 1, out)


def solution(mesh):
    in_specs = (
        P("grp", "seq"),
        P(None, "grp", None),
        P(None, None, "grp"),
        P("grp"),
        P(None, "grp", "seq", None),
        P("grp", None),
    )
    out_specs = P("grp", "seq")
    return jax.shard_map(shards, mesh=mesh, in_specs=in_specs, out_specs=out_specs, check_vma=False)
```

```python
import math

import jax
import jax.numpy as jnp
import numpy as np
from jax import lax
from jax.experimental import pallas as pl
from jax.experimental.pallas import tpu as pltpu
from jax.sharding import PartitionSpec as P

COLS = 256
FREQS = 512
LANES = 128
PROJECT_VMEM = 53100 << 10
GATED_VMEM = 8 << 20
KEEP_VMEM = 52500 << 10
MIXED_VMEM = 12 << 20
CONVOLVE_VMEM = 52000 << 10
MASKS = (0, 2, 1, 3)
BF16 = jnp.bfloat16
F32 = jnp.float32


def unit_circle(rows, cols, period):
    angle = (np.outer(rows, cols) % period) * (2.0 * math.pi / period)
    return np.cos(angle), np.sin(angle)


def transform_tables(shard_count, rows_dev):
    half = shard_count * rows_dev
    order = (np.arange(shard_count)[None, :] * rows_dev + np.arange(rows_dev)[:, None]).reshape(-1)
    freqs = np.arange(2 * half)
    cols = np.arange(COLS)
    padded = 2 * half * COLS
    cos1, sin1 = unit_circle(freqs, order, 2 * half)
    cos2, sin2 = unit_circle(cols, cols, COLS)
    cost, sint = unit_circle(freqs, cols, padded)
    first = np.concatenate([cos1, -sin1], 1)
    forward = np.block([[cos2, -sin2], [sin2, cos2]])
    backward = np.block([[cos2, sin2], [-sin2, cos2]])
    last = np.concatenate([cos1.T, -sin1.T], 0) / padded
    waves = np.concatenate([first, forward, backward, last], 0)
    return jnp.asarray(waves, BF16), jnp.asarray(np.concatenate([cost, sint], 1), F32)


def pack_spectra_body(spec_ref, out_ref):
    dests = out_ref.shape[0]
    per_dest = spec_ref.shape[1] // dests
    for part in range(2):
        for h in range(2):
            piece = spec_ref[part, :, :, h * LANES:(h + 1) * LANES]
            piece = piece.reshape(dests, per_dest, *piece.shape[1:]).astype(BF16)
            for c in range(per_dest):
                out_ref[:, 4 * c + 2 * part + h] = piece[:, c]


def pack_spectra(spectra, shard_count):
    _, channels, rows, cols = spectra.shape
    per_dest = channels // shard_count
    steps = 2
    return pl.pallas_call(
        pack_spectra_body,
        grid=(steps,),
        in_specs=[pl.BlockSpec((2, channels // steps, rows, cols), lambda i: (0, i, 0, 0))],
        out_specs=pl.BlockSpec((shard_count // steps, 4 * per_dest, rows, LANES), lambda i: (i, 0, 0, 0)),
        out_shape=jax.ShapeDtypeStruct((shard_count, 5 * per_dest, rows, LANES), BF16),
        cost_estimate=pl.CostEstimate(flops=0, bytes_accessed=6 * spectra.size, transcendentals=0),
        name="pack_spectra",
    )(spectra)


def filtered(stream, taps_ref, row, s):
    x = stream.astype(F32)
    w = [taps_ref[pl.ds(row, x.shape[0]), 3 * tap + s:3 * tap + s + 1] for tap in range(3)]
    y = w[0] * x + w[1] * pltpu.roll(x, 1, 1) + w[2] * pltpu.roll(x, 2, 1)
    return y[:, LANES:]


def project_body(*refs):
    grp_ref, mains, halos, weight_hbm, taps_ref = refs[0], refs[1:5], refs[5:9], refs[9], refs[10]
    message_ref, gate_hbm, token_ref, stream_ref, spread_ref, part_ref, gate_ref, weight_ref, sem, gate_sem, load_sem = refs[12:]
    channels, tok = mains[0].shape
    width = tok + LANES
    grp = grp_ref[0]
    load = pltpu.make_async_copy(weight_hbm, weight_ref, load_sem)
    load.start()
    for mask, main, halo in zip(MASKS, mains, halos):
        rows = pl.ds(pl.multiple_of((grp ^ mask) * channels, 64), channels)
        token_ref[rows, :LANES] = halo[...]
        token_ref[rows, LANES:] = main[...]
    load.wait()
    step = 384
    for col in range(0, width, step):
        stream_ref[:, col:col + step] = jnp.dot(
            weight_ref[...], token_ref[:, col:col + step], preferred_element_type=F32
        )
    rows = 16

    def chunk(index, carry):
        row = pl.multiple_of(index * rows, rows)
        gate_ref[pl.ds(row, rows), :] = stream_ref[pl.ds(row, rows), :].astype(BF16)
        first, second = (
            filtered(stream_ref[pl.ds(s * channels + row, rows), :].astype(BF16), taps_ref, row, s) for s in (1, 2)
        )
        signal = second * first
        for part in range(8):
            spread_ref[pl.ds(row * 8 + part, rows, stride=8), :] = signal[:, part * LANES:(part + 1) * LANES]
        return carry

    shards, per_dest = part_ref.shape[:2]
    groups = 4
    each = channels // groups
    copies = []
    for group in range(groups):
        lax.fori_loop(group * each // rows, (group + 1) * each // rows, chunk, 0)
        dests = pl.ds(group * shards // groups, shards // groups)
        ready = spread_ref[pl.ds(group * each * 8, each * 8), :].astype(BF16)
        part_ref[dests] = ready.reshape(shards // groups, *part_ref.shape[1:])
        copies.append(pltpu.make_async_copy(
            part_ref.at[dests], message_ref.at[dests, pl.ds(4 * per_dest, per_dest)], sem.at[group]
        ))
        mine = pl.ds(group * each, each)
        copies.append(pltpu.make_async_copy(gate_ref.at[mine], gate_hbm.at[mine], gate_sem.at[group]))
        for copy in copies[-2:]:
            copy.start()
    for copy in copies:
        copy.wait()


def project(grp, mains, halos, weight, taps, packed):
    channels, tok = mains[0].shape
    width = tok + LANES
    vmem = pl.BlockSpec(memory_space=pltpu.VMEM)
    anywhere = pl.BlockSpec(memory_space=pltpu.HBM)
    shards, pieces = packed.shape[:2]
    return pl.pallas_call(
        project_body,
        in_specs=[pl.BlockSpec(memory_space=pltpu.SMEM)] + [vmem] * 8 + [anywhere, vmem, anywhere],
        out_specs=[anywhere] * 2,
        out_shape=[
            jax.ShapeDtypeStruct(packed.shape, BF16),
            jax.ShapeDtypeStruct((channels, width), BF16),
        ],
        scratch_shapes=[
            pltpu.VMEM((4 * channels, width), BF16),
            pltpu.VMEM((3 * channels, width), F32),
            pltpu.VMEM((channels * 8, LANES), F32),
            pltpu.VMEM((shards, pieces // 5, 8, LANES), BF16),
            pltpu.VMEM((channels, width), BF16),
            pltpu.VMEM(weight.shape, BF16),
            pltpu.SemaphoreType.DMA((4,)),
            pltpu.SemaphoreType.DMA((4,)),
            pltpu.SemaphoreType.DMA,
        ],
        input_output_aliases={11: 0},
        compiler_params=pltpu.CompilerParams(vmem_limit_bytes=PROJECT_VMEM),
        cost_estimate=pl.CostEstimate(flops=2 * 3 * channels * 4 * channels * width,
                                      bytes_accessed=6 << 20, transcendentals=0),
        name="project",
    )(grp, *mains, *halos, weight, taps, packed)


def keep_body(message_hbm, gate_ref, taps_ref, *refs):
    weights, kept_ref, stacked_ref, part_ref, spread_ref, sem = refs[:4], *refs[4:]
    channels = gate_ref.shape[0]
    per_dest = part_ref.shape[1]
    load = pltpu.make_async_copy(message_hbm.at[:, pl.ds(4 * per_dest, per_dest)], part_ref, sem)
    load.start()
    rows = 16

    def chunk(index, carry):
        row = pl.multiple_of(index * rows, rows)
        kept_ref[0, pl.ds(row, rows), :] = filtered(gate_ref[pl.ds(row, rows), :], taps_ref, row, 0).astype(BF16)
        return carry

    lax.fori_loop(0, channels // rows, chunk, 0)
    feats = weights[0].shape[0]
    for i, weight in enumerate(weights):
        stacked_ref[i * feats:(i + 1) * feats] = weight[...]
    load.wait()
    spread_ref[...] = part_ref[...].astype(F32).reshape(spread_ref.shape)
    for part in range(8):
        column = spread_ref[pl.ds(part, channels, stride=8), :]
        kept_ref[1, :, part * LANES:(part + 1) * LANES] = column.astype(BF16)


def keep(message, gate_stream, taps, weights):
    channels, width = gate_stream.shape
    shards, pieces = message.shape[:2]
    vmem = pl.BlockSpec(memory_space=pltpu.VMEM)
    return pl.pallas_call(
        keep_body,
        in_specs=[pl.BlockSpec(memory_space=pltpu.HBM)] + [vmem] * 6,
        out_specs=[vmem] * 2,
        out_shape=[
            jax.ShapeDtypeStruct((2, channels, width - LANES), BF16),
            jax.ShapeDtypeStruct((4 * weights[0].shape[0], channels), BF16),
        ],
        scratch_shapes=[
            pltpu.VMEM((shards, pieces // 5, 8, LANES), BF16),
            pltpu.VMEM((channels * 8, LANES), F32),
            pltpu.SemaphoreType.DMA,
        ],
        compiler_params=pltpu.CompilerParams(vmem_limit_bytes=KEEP_VMEM),
        cost_estimate=pl.CostEstimate(flops=8 * channels * width, bytes_accessed=2 << 20, transcendentals=0),
        name="keep",
    )(message, gate_stream, taps, *weights)


def convolve_body(m_hbm, wave_hbm, twist_ref, out_ref,
                  spread_ref, grid_ref, mid_ref, tall_ref, done_ref, wave_ref, m_ref, sems, wave_sems, m_sems):
    channels, shards, pieces, lanes = done_ref.shape
    rows_dev = pieces // 2
    freqs = twist_ref.shape[0]
    first_ref, forward_ref, backward_ref, last_ref = (wave_ref.at[i] for i in range(4))
    loads = [
        pltpu.make_async_copy(wave_hbm.at[pl.ds(i * freqs, freqs)], wave_ref.at[i], wave_sems.at[i]) for i in range(4)
    ]
    signals = pl.ds(4 * channels, channels)
    arrival = pltpu.make_async_copy(m_hbm.at[:, signals], m_ref.at[:, signals], m_sems.at[channels])
    responses = [
        pltpu.make_async_copy(m_hbm.at[:, pl.ds(4 * c, 4)], m_ref.at[:, pl.ds(4 * c, 4)], m_sems.at[c])
        for c in range(channels)
    ]
    for load in (arrival, *loads[:2], *responses, *loads[2:]):
        load.start()
    cosine, sine = twist_ref[:, :COLS], twist_ref[:, COLS:]

    def arrange(c):
        spread_ref[c] = m_ref[:, 4 * channels + c].astype(F32).reshape(shards * pieces, lanes)
        for a in range(rows_dev):
            for h in range(2):
                grid_ref[c, a * shards:(a + 1) * shards, h * lanes:(h + 1) * lanes] = spread_ref[
                    c, pl.ds(2 * a + h, shards, stride=pieces), :].astype(BF16)

    def rows_forward(c):
        real = jnp.dot(first_ref[:, :COLS], grid_ref[c], preferred_element_type=F32)
        return real, jnp.dot(first_ref[:, COLS:], grid_ref[c], preferred_element_type=F32)

    def twist_forward(c, wave):
        real, imag = wave
        mid_ref[c, :, :COLS] = (real * cosine + imag * sine).astype(BF16)
        mid_ref[c, :, COLS:] = (imag * cosine - real * sine).astype(BF16)

    def cols_forward(c):
        return jnp.dot(mid_ref[c], forward_ref[...], preferred_element_type=F32)

    def respond(c, freq):
        responses[c].wait()
        for h in range(2):
            low, high = h * lanes, COLS + h * lanes
            real, imag = freq[:, low:low + lanes], freq[:, high:high + lanes]
            h_real, h_imag = (
                m_ref[:, 4 * c + 2 * part + h].astype(F32).reshape(freqs, lanes) for part in range(2)
            )
            mid_ref[c, :, low:low + lanes] = (real * h_real - imag * h_imag).astype(BF16)
            mid_ref[c, :, high:high + lanes] = (real * h_imag + imag * h_real).astype(BF16)

    def cols_backward(c):
        return jnp.dot(mid_ref[c], backward_ref[...], preferred_element_type=F32)

    def twist_backward(c, back):
        real, imag = back[:, :COLS], back[:, COLS:]
        tall_ref[c, :freqs, :] = (real * cosine - imag * sine).astype(BF16)
        tall_ref[c, freqs:, :] = (imag * cosine + real * sine).astype(BF16)

    def rows_backward(c):
        out = jnp.dot(last_ref[:COLS, :], tall_ref[c, :freqs], preferred_element_type=F32)
        return out + jnp.dot(last_ref[COLS:, :], tall_ref[c, freqs:], preferred_element_type=F32)

    def send(c, out):
        for a in range(rows_dev):
            for h in range(2):
                spread_ref[c, pl.ds(2 * a + h, shards, stride=pieces), :] = out[
                    a * shards:(a + 1) * shards, h * lanes:(h + 1) * lanes]
        done_ref[c] = spread_ref[c].reshape(shards, pieces, lanes).astype(BF16)
        pltpu.make_async_copy(done_ref.at[c], out_ref.at[:, c], sems.at[c]).start()

    arrival.wait()
    for c in range(channels):
        arrange(c)
    stages = (
        (rows_forward, twist_forward), (cols_forward, respond), (cols_backward, twist_backward), (rows_backward, send)
    )
    waiting = None
    for stage, (multiply, finish) in enumerate(stages):
        loads[stage].wait()
        for c in range(channels):
            product = multiply(c)
            if waiting is not None:
                waiting[0](*waiting[1:])
            waiting = (finish, c, product)
    waiting[0](*waiting[1:])
    for c in range(channels):
        pltpu.make_async_copy(done_ref.at[c], out_ref.at[:, c], sems.at[c]).wait()


def convolve(received, tables):
    shards, kinds, pieces, lanes = received.shape
    channels = kinds // 5
    freqs = shards * pieces
    vmem = pl.BlockSpec(memory_space=pltpu.VMEM)
    return pl.pallas_call(
        convolve_body,
        in_specs=[vmem] * 3,
        out_specs=pl.BlockSpec(memory_space=pltpu.HBM),
        out_shape=jax.ShapeDtypeStruct((shards, channels, pieces, lanes), BF16),
        scratch_shapes=[
            pltpu.VMEM((channels, shards * pieces, lanes), F32),
            pltpu.VMEM((channels, freqs // 2, COLS), BF16),
            pltpu.VMEM((channels, freqs, 2 * COLS), BF16),
            pltpu.VMEM((channels, 2 * freqs, COLS), BF16),
            pltpu.VMEM((channels, shards, pieces, lanes), BF16),
            pltpu.VMEM((4, freqs, 2 * COLS), BF16),
            pltpu.VMEM(received.shape, BF16),
            pltpu.SemaphoreType.DMA((channels,)),
            pltpu.SemaphoreType.DMA((4,)),
            pltpu.SemaphoreType.DMA((channels + 1,)),
        ],
        compiler_params=pltpu.CompilerParams(vmem_limit_bytes=CONVOLVE_VMEM),
        cost_estimate=pl.CostEstimate(flops=3 << 30, bytes_accessed=6 << 20, transcendentals=0),
        name="convolve",
    )(received, *tables)


def gated_body(y_ref, kept_ref, bias_ref, early_ref, late_ref, spread_ref):
    channels = early_ref.shape[0]
    spread_ref[...] = y_ref[...].astype(F32)
    bias = bias_ref[...]
    for part in range(8):
        cols = slice(part * LANES, (part + 1) * LANES)
        y = spread_ref[pl.ds(part, channels, stride=8), :]
        direct = bias * kept_ref[1, :, cols].astype(F32)
        out_ref, at = (early_ref, part) if part < 4 else (late_ref, part - 4)
        value = kept_ref[0, :, cols].astype(F32) * (y + direct)
        out_ref[:, at * LANES:(at + 1) * LANES] = value.astype(BF16)


def gated(y, kept, bias):
    vmem = pl.BlockSpec(memory_space=pltpu.VMEM)
    return pl.pallas_call(
        gated_body,
        in_specs=[vmem] * 3,
        out_specs=[vmem] * 2,
        out_shape=[jax.ShapeDtypeStruct((kept.shape[1], kept.shape[2] // 2), BF16)] * 2,
        scratch_shapes=[
            pltpu.VMEM(y.shape, F32),
        ],
        compiler_params=pltpu.CompilerParams(vmem_limit_bytes=GATED_VMEM),
        cost_estimate=pl.CostEstimate(flops=4 * y.size, bytes_accessed=8 * y.size, transcendentals=0),
        name="gated",
    )(y, kept, bias)


def mixed_body(*refs):
    values, weights_ref, out_ref = refs[:4], refs[4], refs[-1]
    rows = values[0].shape[0]
    total = jnp.dot(weights_ref[:rows], values[0][...], preferred_element_type=F32)
    for i in range(1, 4):
        total = total + jnp.dot(weights_ref[i * rows:(i + 1) * rows], values[i][...], preferred_element_type=F32)
    out_ref[...] = total.astype(BF16)


def mixed(values, weights, half, *earlier):
    channels, tok = values[0].shape
    feats = weights.shape[0] // 4
    return pl.pallas_call(
        mixed_body,
        grid=(1,),
        in_specs=[pl.BlockSpec(memory_space=pltpu.VMEM)] * 5 + [pl.BlockSpec(memory_space=pl.ANY)] * len(earlier),
        out_specs=pl.BlockSpec((feats, tok), lambda i: (0, half)),
        out_shape=jax.ShapeDtypeStruct((feats, 2 * tok), BF16),
        input_output_aliases={5: 0} if earlier else {},
        compiler_params=pltpu.CompilerParams(vmem_limit_bytes=MIXED_VMEM),
        cost_estimate=pl.CostEstimate(flops=8 * channels * feats * tok, bytes_accessed=2 << 20, transcendentals=0),
        name="mixed",
    )(*values, weights, *earlier)


def swapped(block, mask):
    return lax.ppermute(block, "grp", [(i, i ^ mask) for i in range(4)])


def shards(tokens, in_weight, short_weight, filter_bias, spectra, out_weight):
    shard_count = lax.axis_size("seq")
    grp = lax.axis_index("grp")
    channels, tok = tokens.shape
    per_dest = channels // shard_count

    far = swapped(tokens, 2)
    near = swapped(tokens, 1)
    route = [(i, i + 1) for i in range(shard_count - 1)]
    halo = lax.ppermute(tokens[:, -LANES:], "seq", route)
    packed = pack_spectra(spectra, shard_count)
    halo, packed = lax.optimization_barrier((halo, packed))
    halo_far = swapped(halo, 2)
    halo_near = swapped(halo, 1)
    far, halo_far = lax.optimization_barrier((far, halo_far))
    mains = [tokens, far, near, swapped(far, 1)]
    halos = [halo, halo_far, halo_near, swapped(halo_far, 1)]
    taps = jnp.transpose(short_weight, (2, 0, 1)).reshape(channels, 9)
    message, gate_stream = project(
        grp.reshape(1).astype(jnp.int32), mains, halos, in_weight.reshape(3 * channels, -1), taps, packed
    )
    message, out_weight, filter_bias, later, gate_stream = lax.optimization_barrier(
        (message, out_weight, filter_bias, grp, gate_stream)
    )
    received = lax.all_to_all(message, "seq", 0, 0, tiled=True)

    turned = out_weight.T
    parts = [
        lax.dynamic_slice_in_dim(turned, (later ^ mask) * channels, channels, 0) for mask in MASKS
    ]
    weights = [parts[0]] + [swapped(part, mask) for part, mask in zip(parts[1:], MASKS[1:])]
    zero = jnp.minimum(later, 0)
    tables = [t + zero.astype(t.dtype) for t in transform_tables(shard_count, tok // COLS)]
    bias = filter_bias[:, None] + zero.astype(F32)
    received, weights, tables, bias = lax.optimization_barrier((received, weights, tables, bias))

    result = convolve(received, tables)
    result, message, gate_stream, weights, taps = lax.optimization_barrier(
        (result, message, gate_stream, weights, taps)
    )
    kept, weights = keep(message, gate_stream, taps, weights)
    back = lax.all_to_all(result, "seq", 0, 0, tiled=True).reshape(channels * 8, LANES)
    early, late = gated(back, kept, bias)
    far_early, far_late = swapped(early, 2), swapped(late, 2)
    near_early, near_late = swapped(early, 1), swapped(late, 1)
    out = mixed((early, far_early, near_early, swapped(far_early, 1)), weights, 0)
    return mixed((late, far_late, near_late, swapped(far_late, 1)), weights, 1, out)


def solution(mesh):
    in_specs = (
        P("grp", "seq"),
        P(None, "grp", None),
        P(None, None, "grp"),
        P("grp"),
        P(None, "grp", "seq", None),
        P("grp", None),
    )
    out_specs = P("grp", "seq")
    return jax.shard_map(shards, mesh=mesh, in_specs=in_specs, out_specs=out_specs, check_vma=False)
```

```python
import math

import jax
import jax.numpy as jnp
import numpy as np
from jax import lax
from jax.experimental import pallas as pl
from jax.experimental.pallas import tpu as pltpu
from jax.sharding import PartitionSpec as P

COLS = 256
FREQS = 512
LANES = 128
PROJECT_VMEM = 53100 << 10
GATED_VMEM = 8 << 20
KEEP_VMEM = 52500 << 10
MIXED_VMEM = 12 << 20
CONVOLVE_VMEM = 50600 << 10
MASKS = (0, 2, 1, 3)
BF16 = jnp.bfloat16
F32 = jnp.float32


def unit_circle(rows, cols, period):
    angle = (np.outer(rows, cols) % period) * (2.0 * math.pi / period)
    return np.cos(angle), np.sin(angle)


def transform_tables(shard_count, rows_dev):
    half = shard_count * rows_dev
    order = (np.arange(shard_count)[None, :] * rows_dev + np.arange(rows_dev)[:, None]).reshape(-1)
    freqs = np.arange(2 * half)
    cols = np.arange(COLS)
    padded = 2 * half * COLS
    cos1, sin1 = unit_circle(freqs, order, 2 * half)
    cos2, sin2 = unit_circle(cols, cols, COLS)
    cost, sint = unit_circle(freqs, cols, padded)
    first = np.concatenate([cos1, -sin1], 1)
    forward = np.block([[cos2, -sin2], [sin2, cos2]])
    last = np.concatenate([cos1.T, -sin1.T], 0) / padded
    waves = np.concatenate([first, forward, last], 0)
    return jnp.asarray(waves, BF16), jnp.asarray(np.concatenate([cost, sint], 1), F32)


def pack_spectra_body(spec_ref, out_ref):
    dests = out_ref.shape[0]
    per_dest = spec_ref.shape[1] // dests
    for part in range(2):
        for h in range(2):
            piece = spec_ref[part, :, :, h * LANES:(h + 1) * LANES]
            piece = piece.reshape(dests, per_dest, *piece.shape[1:]).astype(BF16)
            for c in range(per_dest):
                out_ref[:, 4 * c + 2 * part + h] = piece[:, c]


def pack_spectra(spectra, shard_count):
    _, channels, rows, cols = spectra.shape
    per_dest = channels // shard_count
    steps = 2
    return pl.pallas_call(
        pack_spectra_body,
        grid=(steps,),
        in_specs=[pl.BlockSpec((2, channels // steps, rows, cols), lambda i: (0, i, 0, 0))],
        out_specs=pl.BlockSpec((shard_count // steps, 4 * per_dest, rows, LANES), lambda i: (i, 0, 0, 0)),
        out_shape=jax.ShapeDtypeStruct((shard_count, 5 * per_dest, rows, LANES), BF16),
        cost_estimate=pl.CostEstimate(flops=0, bytes_accessed=6 * spectra.size, transcendentals=0),
        name="pack_spectra",
    )(spectra)


def filtered(stream, taps_ref, row, s):
    x = stream.astype(F32)
    w = [taps_ref[pl.ds(row, x.shape[0]), 3 * tap + s:3 * tap + s + 1] for tap in range(3)]
    y = w[0] * x + w[1] * pltpu.roll(x, 1, 1) + w[2] * pltpu.roll(x, 2, 1)
    return y[:, LANES:]


def project_body(*refs):
    grp_ref, mains, halos, weight_hbm, taps_ref = refs[0], refs[1:5], refs[5:9], refs[9], refs[10]
    message_ref, gate_hbm, token_ref, stream_ref, spread_ref, part_ref, gate_ref, weight_ref, sem, gate_sem, load_sem = refs[12:]
    channels, tok = mains[0].shape
    width = tok + LANES
    grp = grp_ref[0]
    load = pltpu.make_async_copy(weight_hbm, weight_ref, load_sem)
    load.start()
    for mask, main, halo in zip(MASKS, mains, halos):
        rows = pl.ds(pl.multiple_of((grp ^ mask) * channels, 64), channels)
        token_ref[rows, :LANES] = halo[...]
        token_ref[rows, LANES:] = main[...]
    load.wait()
    step = 384
    for col in range(0, width, step):
        stream_ref[:, col:col + step] = jnp.dot(
            weight_ref[...], token_ref[:, col:col + step], preferred_element_type=F32
        )
    rows = 16

    def chunk(index, carry):
        row = pl.multiple_of(index * rows, rows)
        gate_ref[pl.ds(row, rows), :] = stream_ref[pl.ds(row, rows), :].astype(BF16)
        first, second = (
            filtered(stream_ref[pl.ds(s * channels + row, rows), :].astype(BF16), taps_ref, row, s) for s in (1, 2)
        )
        signal = second * first
        for part in range(8):
            spread_ref[pl.ds(row * 8 + part, rows, stride=8), :] = signal[:, part * LANES:(part + 1) * LANES]
        return carry

    shards, per_dest = part_ref.shape[:2]
    groups = 4
    each = channels // groups
    copies = []
    for group in range(groups):
        lax.fori_loop(group * each // rows, (group + 1) * each // rows, chunk, 0)
        dests = pl.ds(group * shards // groups, shards // groups)
        ready = spread_ref[pl.ds(group * each * 8, each * 8), :].astype(BF16)
        part_ref[dests] = ready.reshape(shards // groups, *part_ref.shape[1:])
        copies.append(pltpu.make_async_copy(
            part_ref.at[dests], message_ref.at[dests, pl.ds(4 * per_dest, per_dest)], sem.at[group]
        ))
        mine = pl.ds(group * each, each)
        copies.append(pltpu.make_async_copy(gate_ref.at[mine], gate_hbm.at[mine], gate_sem.at[group]))
        for copy in copies[-2:]:
            copy.start()
    for copy in copies:
        copy.wait()


def project(grp, mains, halos, weight, taps, packed):
    channels, tok = mains[0].shape
    width = tok + LANES
    vmem = pl.BlockSpec(memory_space=pltpu.VMEM)
    anywhere = pl.BlockSpec(memory_space=pltpu.HBM)
    shards, pieces = packed.shape[:2]
    return pl.pallas_call(
        project_body,
        in_specs=[pl.BlockSpec(memory_space=pltpu.SMEM)] + [vmem] * 8 + [anywhere, vmem, anywhere],
        out_specs=[anywhere] * 2,
        out_shape=[
            jax.ShapeDtypeStruct(packed.shape, BF16),
            jax.ShapeDtypeStruct((channels, width), BF16),
        ],
        scratch_shapes=[
            pltpu.VMEM((4 * channels, width), BF16),
            pltpu.VMEM((3 * channels, width), F32),
            pltpu.VMEM((channels * 8, LANES), F32),
            pltpu.VMEM((shards, pieces // 5, 8, LANES), BF16),
            pltpu.VMEM((channels, width), BF16),
            pltpu.VMEM(weight.shape, BF16),
            pltpu.SemaphoreType.DMA((4,)),
            pltpu.SemaphoreType.DMA((4,)),
            pltpu.SemaphoreType.DMA,
        ],
        input_output_aliases={11: 0},
        compiler_params=pltpu.CompilerParams(vmem_limit_bytes=PROJECT_VMEM),
        cost_estimate=pl.CostEstimate(flops=2 * 3 * channels * 4 * channels * width,
                                      bytes_accessed=6 << 20, transcendentals=0),
        name="project",
    )(grp, *mains, *halos, weight, taps, packed)


def keep_body(message_hbm, gate_ref, taps_ref, *refs):
    weights, kept_ref, stacked_ref, part_ref, spread_ref, sem = refs[:4], *refs[4:]
    channels = gate_ref.shape[0]
    per_dest = part_ref.shape[1]
    load = pltpu.make_async_copy(message_hbm.at[:, pl.ds(4 * per_dest, per_dest)], part_ref, sem)
    load.start()
    rows = 16

    def chunk(index, carry):
        row = pl.multiple_of(index * rows, rows)
        kept_ref[0, pl.ds(row, rows), :] = filtered(gate_ref[pl.ds(row, rows), :], taps_ref, row, 0).astype(BF16)
        return carry

    lax.fori_loop(0, channels // rows, chunk, 0)
    feats = weights[0].shape[0]
    for i, weight in enumerate(weights):
        stacked_ref[i * feats:(i + 1) * feats] = weight[...]
    load.wait()
    spread_ref[...] = part_ref[...].astype(F32).reshape(spread_ref.shape)
    for part in range(8):
        column = spread_ref[pl.ds(part, channels, stride=8), :]
        kept_ref[1, :, part * LANES:(part + 1) * LANES] = column.astype(BF16)


def keep(message, gate_stream, taps, weights):
    channels, width = gate_stream.shape
    shards, pieces = message.shape[:2]
    vmem = pl.BlockSpec(memory_space=pltpu.VMEM)
    return pl.pallas_call(
        keep_body,
        in_specs=[pl.BlockSpec(memory_space=pltpu.HBM)] + [vmem] * 6,
        out_specs=[vmem] * 2,
        out_shape=[
            jax.ShapeDtypeStruct((2, channels, width - LANES), BF16),
            jax.ShapeDtypeStruct((4 * weights[0].shape[0], channels), BF16),
        ],
        scratch_shapes=[
            pltpu.VMEM((shards, pieces // 5, 8, LANES), BF16),
            pltpu.VMEM((channels * 8, LANES), F32),
            pltpu.SemaphoreType.DMA,
        ],
        compiler_params=pltpu.CompilerParams(vmem_limit_bytes=KEEP_VMEM),
        cost_estimate=pl.CostEstimate(flops=8 * channels * width, bytes_accessed=2 << 20, transcendentals=0),
        name="keep",
    )(message, gate_stream, taps, *weights)


def convolve_body(m_hbm, wave_ref, twist_ref, out_ref,
                  spread_ref, grid_ref, mid_ref, tall_ref, done_ref, m_ref, sems, m_sems):
    channels, shards, pieces, lanes = done_ref.shape
    rows_dev = pieces // 2
    freqs = twist_ref.shape[0]
    first_ref, forward_ref, last_ref = (wave_ref.at[pl.ds(i * freqs, freqs)] for i in range(3))
    signals = pl.ds(4 * channels, channels)
    arrival = pltpu.make_async_copy(m_hbm.at[:, signals], m_ref.at[:, signals], m_sems.at[channels])
    responses = [
        pltpu.make_async_copy(m_hbm.at[:, pl.ds(4 * c, 4)], m_ref.at[:, pl.ds(4 * c, 4)], m_sems.at[c])
        for c in range(channels)
    ]
    for load in (arrival, *responses):
        load.start()
    cosine, sine = twist_ref[:, :COLS], twist_ref[:, COLS:]

    def arrange(c):
        spread_ref[c] = m_ref[:, 4 * channels + c].astype(F32).reshape(shards * pieces, lanes)
        for a in range(rows_dev):
            for h in range(2):
                grid_ref[c, a * shards:(a + 1) * shards, h * lanes:(h + 1) * lanes] = spread_ref[
                    c, pl.ds(2 * a + h, shards, stride=pieces), :].astype(BF16)

    def rows_forward(c):
        real = jnp.dot(first_ref[:, :COLS], grid_ref[c], preferred_element_type=F32)
        return real, jnp.dot(first_ref[:, COLS:], grid_ref[c], preferred_element_type=F32)

    def twist_forward(c, wave):
        real, imag = wave
        mid_ref[c, :, :COLS] = (real * cosine + imag * sine).astype(BF16)
        mid_ref[c, :, COLS:] = (imag * cosine - real * sine).astype(BF16)

    def cols_forward(c):
        return jnp.dot(mid_ref[c], forward_ref[...], preferred_element_type=F32)

    def respond(c, freq):
        responses[c].wait()
        for h in range(2):
            low, high = h * lanes, COLS + h * lanes
            real, imag = freq[:, low:low + lanes], freq[:, high:high + lanes]
            h_real, h_imag = (
                m_ref[:, 4 * c + 2 * part + h].astype(F32).reshape(freqs, lanes) for part in range(2)
            )
            mid_ref[c, :, low:low + lanes] = (real * h_real - imag * h_imag).astype(BF16)
            mid_ref[c, :, high:high + lanes] = (-(real * h_imag) - imag * h_real).astype(BF16)

    def cols_backward(c):
        return jnp.dot(mid_ref[c], forward_ref[...], preferred_element_type=F32)

    def twist_backward(c, back):
        real, minus = back[:, :COLS], back[:, COLS:]
        tall_ref[c, :freqs, :] = (real * cosine + minus * sine).astype(BF16)
        tall_ref[c, freqs:, :] = (real * sine - minus * cosine).astype(BF16)

    def rows_backward(c):
        out = jnp.dot(last_ref[:COLS, :], tall_ref[c, :freqs], preferred_element_type=F32)
        return out + jnp.dot(last_ref[COLS:, :], tall_ref[c, freqs:], preferred_element_type=F32)

    def send(c, out):
        for a in range(rows_dev):
            for h in range(2):
                spread_ref[c, pl.ds(2 * a + h, shards, stride=pieces), :] = out[
                    a * shards:(a + 1) * shards, h * lanes:(h + 1) * lanes]
        done_ref[c] = spread_ref[c].reshape(shards, pieces, lanes).astype(BF16)
        pltpu.make_async_copy(done_ref.at[c], out_ref.at[:, c], sems.at[c]).start()

    arrival.wait()
    for c in range(channels):
        arrange(c)
    stages = (
        (rows_forward, twist_forward), (cols_forward, respond), (cols_backward, twist_backward), (rows_backward, send)
    )
    waiting = None
    for multiply, finish in stages:
        for c in range(channels):
            product = multiply(c)
            if waiting is not None:
                waiting[0](*waiting[1:])
            waiting = (finish, c, product)
    waiting[0](*waiting[1:])
    for c in range(channels):
        pltpu.make_async_copy(done_ref.at[c], out_ref.at[:, c], sems.at[c]).wait()


def convolve(received, tables):
    shards, kinds, pieces, lanes = received.shape
    channels = kinds // 5
    freqs = shards * pieces
    vmem = pl.BlockSpec(memory_space=pltpu.VMEM)
    return pl.pallas_call(
        convolve_body,
        in_specs=[vmem] * 3,
        out_specs=pl.BlockSpec(memory_space=pltpu.HBM),
        out_shape=jax.ShapeDtypeStruct((shards, channels, pieces, lanes), BF16),
        scratch_shapes=[
            pltpu.VMEM((channels, shards * pieces, lanes), F32),
            pltpu.VMEM((channels, freqs // 2, COLS), BF16),
            pltpu.VMEM((channels, freqs, 2 * COLS), BF16),
            pltpu.VMEM((channels, 2 * freqs, COLS), BF16),
            pltpu.VMEM((channels, shards, pieces, lanes), BF16),
            pltpu.VMEM(received.shape, BF16),
            pltpu.SemaphoreType.DMA((channels,)),
            pltpu.SemaphoreType.DMA((channels + 1,)),
        ],
        compiler_params=pltpu.CompilerParams(vmem_limit_bytes=CONVOLVE_VMEM),
        cost_estimate=pl.CostEstimate(flops=3 << 30, bytes_accessed=6 << 20, transcendentals=0),
        name="convolve",
    )(received, *tables)


def gated_body(y_ref, kept_ref, bias_ref, early_ref, late_ref, spread_ref):
    channels = early_ref.shape[0]
    spread_ref[...] = y_ref[...].astype(F32)
    bias = bias_ref[...]
    for part in range(8):
        cols = slice(part * LANES, (part + 1) * LANES)
        y = spread_ref[pl.ds(part, channels, stride=8), :]
        direct = bias * kept_ref[1, :, cols].astype(F32)
        out_ref, at = (early_ref, part) if part < 4 else (late_ref, part - 4)
        value = kept_ref[0, :, cols].astype(F32) * (y + direct)
        out_ref[:, at * LANES:(at + 1) * LANES] = value.astype(BF16)


def gated(y, kept, bias):
    vmem = pl.BlockSpec(memory_space=pltpu.VMEM)
    return pl.pallas_call(
        gated_body,
        in_specs=[vmem] * 3,
        out_specs=[vmem] * 2,
        out_shape=[jax.ShapeDtypeStruct((kept.shape[1], kept.shape[2] // 2), BF16)] * 2,
        scratch_shapes=[
            pltpu.VMEM(y.shape, F32),
        ],
        compiler_params=pltpu.CompilerParams(vmem_limit_bytes=GATED_VMEM),
        cost_estimate=pl.CostEstimate(flops=4 * y.size, bytes_accessed=8 * y.size, transcendentals=0),
        name="gated",
    )(y, kept, bias)


def mixed_body(*refs):
    values, weights_ref, out_ref = refs[:4], refs[4], refs[-1]
    rows = values[0].shape[0]
    total = jnp.dot(weights_ref[:rows], values[0][...], preferred_element_type=F32)
    for i in range(1, 4):
        total = total + jnp.dot(weights_ref[i * rows:(i + 1) * rows], values[i][...], preferred_element_type=F32)
    out_ref[...] = total.astype(BF16)


def mixed(values, weights, half, *earlier):
    channels, tok = values[0].shape
    feats = weights.shape[0] // 4
    return pl.pallas_call(
        mixed_body,
        grid=(1,),
        in_specs=[pl.BlockSpec(memory_space=pltpu.VMEM)] * 5 + [pl.BlockSpec(memory_space=pl.ANY)] * len(earlier),
        out_specs=pl.BlockSpec((feats, tok), lambda i: (0, half)),
        out_shape=jax.ShapeDtypeStruct((feats, 2 * tok), BF16),
        input_output_aliases={5: 0} if earlier else {},
        compiler_params=pltpu.CompilerParams(vmem_limit_bytes=MIXED_VMEM),
        cost_estimate=pl.CostEstimate(flops=8 * channels * feats * tok, bytes_accessed=2 << 20, transcendentals=0),
        name="mixed",
    )(*values, weights, *earlier)


def swapped(block, mask):
    return lax.ppermute(block, "grp", [(i, i ^ mask) for i in range(4)])


def shards(tokens, in_weight, short_weight, filter_bias, spectra, out_weight):
    shard_count = lax.axis_size("seq")
    grp = lax.axis_index("grp")
    channels, tok = tokens.shape
    per_dest = channels // shard_count

    far = swapped(tokens, 2)
    near = swapped(tokens, 1)
    route = [(i, i + 1) for i in range(shard_count - 1)]
    halo = lax.ppermute(tokens[:, -LANES:], "seq", route)
    packed = pack_spectra(spectra, shard_count)
    halo, packed = lax.optimization_barrier((halo, packed))
    halo_far = swapped(halo, 2)
    halo_near = swapped(halo, 1)
    far, halo_far = lax.optimization_barrier((far, halo_far))
    mains = [tokens, far, near, swapped(far, 1)]
    halos = [halo, halo_far, halo_near, swapped(halo_far, 1)]
    taps = jnp.transpose(short_weight, (2, 0, 1)).reshape(channels, 9)
    message, gate_stream = project(
        grp.reshape(1).astype(jnp.int32), mains, halos, in_weight.reshape(3 * channels, -1), taps, packed
    )
    message, out_weight, filter_bias, later, gate_stream = lax.optimization_barrier(
        (message, out_weight, filter_bias, grp, gate_stream)
    )
    received = lax.all_to_all(message, "seq", 0, 0, tiled=True)

    turned = out_weight.T
    parts = [
        lax.dynamic_slice_in_dim(turned, (later ^ mask) * channels, channels, 0) for mask in MASKS
    ]
    weights = [parts[0]] + [swapped(part, mask) for part, mask in zip(parts[1:], MASKS[1:])]
    zero = jnp.minimum(later, 0)
    tables = [t + zero.astype(t.dtype) for t in transform_tables(shard_count, tok // COLS)]
    bias = filter_bias[:, None] + zero.astype(F32)
    received, weights, tables, bias = lax.optimization_barrier((received, weights, tables, bias))

    result = convolve(received, tables)
    result, message, gate_stream, weights, taps = lax.optimization_barrier(
        (result, message, gate_stream, weights, taps)
    )
    kept, weights = keep(message, gate_stream, taps, weights)
    back = lax.all_to_all(result, "seq", 0, 0, tiled=True).reshape(channels * 8, LANES)
    early, late = gated(back, kept, bias)
    far_early, far_late = swapped(early, 2), swapped(late, 2)
    near_early, near_late = swapped(early, 1), swapped(late, 1)
    out = mixed((early, far_early, near_early, swapped(far_early, 1)), weights, 0)
    return mixed((late, far_late, near_late, swapped(far_late, 1)), weights, 1, out)


def solution(mesh):
    in_specs = (
        P("grp", "seq"),
        P(None, "grp", None),
        P(None, None, "grp"),
        P("grp"),
        P(None, "grp", "seq", None),
        P("grp", None),
    )
    out_specs = P("grp", "seq")
    return jax.shard_map(shards, mesh=mesh, in_specs=in_specs, out_specs=out_specs, check_vma=False)
```

```python
import math

import jax
import jax.numpy as jnp
import numpy as np
from jax import lax
from jax.experimental import pallas as pl
from jax.experimental.pallas import tpu as pltpu
from jax.sharding import PartitionSpec as P

COLS = 256
FREQS = 512
LANES = 128
PROJECT_VMEM = 51500 << 10
GATED_VMEM = 54000 << 10
MIXED_VMEM = 12 << 20
CONVOLVE_VMEM = 50000 << 10
MASKS = (0, 2, 1, 3)
BF16 = jnp.bfloat16
F32 = jnp.float32


def unit_circle(rows, cols, period):
    angle = (np.outer(rows, cols) % period) * (2.0 * math.pi / period)
    return np.cos(angle), np.sin(angle)


def transform_tables(shard_count, rows_dev):
    half = shard_count * rows_dev
    order = (np.arange(shard_count)[None, :] * rows_dev + np.arange(rows_dev)[:, None]).reshape(-1)
    freqs = np.arange(2 * half)
    cols = np.arange(COLS)
    padded = 2 * half * COLS
    cos1, sin1 = unit_circle(freqs, order, 2 * half)
    cos2, sin2 = unit_circle(cols, cols, COLS)
    cost, sint = unit_circle(freqs, cols, padded)
    first = np.concatenate([cos1, -sin1], 1)
    forward = np.block([[cos2, -sin2], [sin2, cos2]])
    backward = np.block([[cos2, sin2], [-sin2, cos2]])
    last = np.concatenate([cos1.T, -sin1.T], 0) / padded
    waves = np.concatenate([first, forward, backward, last], 0)
    return jnp.asarray(waves, BF16), jnp.asarray(np.concatenate([cost, sint], 1), F32)


def pack_spectra_body(spec_ref, out_ref):
    dests = out_ref.shape[0]
    per_dest = spec_ref.shape[1] // dests
    for part in range(2):
        for h in range(2):
            piece = spec_ref[part, :, :, h * LANES:(h + 1) * LANES]
            piece = piece.reshape(dests, per_dest, *piece.shape[1:]).astype(BF16)
            for c in range(per_dest):
                out_ref[:, 4 * c + 2 * part + h] = piece[:, c]


def pack_spectra(spectra, shard_count):
    _, channels, rows, cols = spectra.shape
    per_dest = channels // shard_count
    steps = 2
    return pl.pallas_call(
        pack_spectra_body,
        grid=(steps,),
        in_specs=[pl.BlockSpec((2, channels // steps, rows, cols), lambda i: (0, i, 0, 0))],
        out_specs=pl.BlockSpec((shard_count // steps, 4 * per_dest, rows, LANES), lambda i: (i, 0, 0, 0)),
        out_shape=jax.ShapeDtypeStruct((shard_count, 5 * per_dest, rows, LANES), BF16),
        cost_estimate=pl.CostEstimate(flops=0, bytes_accessed=6 * spectra.size, transcendentals=0),
        name="pack_spectra",
    )(spectra)


def filtered(stream, taps_ref, row, s):
    x = stream.astype(F32)
    w = [taps_ref[pl.ds(row, x.shape[0]), 3 * tap + s:3 * tap + s + 1] for tap in range(3)]
    y = w[0] * x + w[1] * pltpu.roll(x, 1, 1) + w[2] * pltpu.roll(x, 2, 1)
    return y[:, LANES:]


def project_body(*refs):
    grp_ref, mains, halos, weight_ref, taps_ref = refs[0], refs[1:5], refs[5:9], refs[9], refs[10]
    message_ref, gate_ref, token_ref, stream_ref, spread_ref, part_ref, sem = refs[12:]
    channels, tok = mains[0].shape
    width = tok + LANES
    grp = grp_ref[0]
    for mask, main, halo in zip(MASKS, mains, halos):
        rows = pl.ds(pl.multiple_of((grp ^ mask) * channels, 64), channels)
        token_ref[rows, :LANES] = halo[...]
        token_ref[rows, LANES:] = main[...]
    step = 384
    for col in range(0, width, step):
        stream_ref[:, col:col + step] = jnp.dot(
            weight_ref[...], token_ref[:, col:col + step], preferred_element_type=F32
        )
    rows = 16

    def chunk(index, carry):
        row = pl.multiple_of(index * rows, rows)
        gate_ref[pl.ds(row, rows), :] = stream_ref[pl.ds(row, rows), :].astype(BF16)
        first, second = (
            filtered(stream_ref[pl.ds(s * channels + row, rows), :].astype(BF16), taps_ref, row, s) for s in (1, 2)
        )
        signal = second * first
        for part in range(8):
            spread_ref[pl.ds(row * 8 + part, rows, stride=8), :] = signal[:, part * LANES:(part + 1) * LANES]
        return carry

    shards, per_dest = part_ref.shape[:2]
    groups = 4
    each = channels // groups
    copies = []
    for group in range(groups):
        lax.fori_loop(group * each // rows, (group + 1) * each // rows, chunk, 0)
        dests = pl.ds(group * shards // groups, shards // groups)
        ready = spread_ref[pl.ds(group * each * 8, each * 8), :].astype(BF16)
        part_ref[dests] = ready.reshape(shards // groups, *part_ref.shape[1:])
        copies.append(pltpu.make_async_copy(
            part_ref.at[dests], message_ref.at[dests, pl.ds(4 * per_dest, per_dest)], sem.at[group]
        ))
        copies[-1].start()
    for copy in copies:
        copy.wait()


def project(grp, mains, halos, weight, taps, packed):
    channels, tok = mains[0].shape
    width = tok + LANES
    vmem = pl.BlockSpec(memory_space=pltpu.VMEM)
    anywhere = pl.BlockSpec(memory_space=pltpu.HBM)
    shards, pieces = packed.shape[:2]
    return pl.pallas_call(
        project_body,
        in_specs=[pl.BlockSpec(memory_space=pltpu.SMEM)] + [vmem] * 10 + [anywhere],
        out_specs=[anywhere, vmem],
        out_shape=[
            jax.ShapeDtypeStruct(packed.shape, BF16),
            jax.ShapeDtypeStruct((channels, width), BF16),
        ],
        scratch_shapes=[
            pltpu.VMEM((4 * channels, width), BF16),
            pltpu.VMEM((3 * channels, width), F32),
            pltpu.VMEM((channels * 8, LANES), F32),
            pltpu.VMEM((shards, pieces // 5, 8, LANES), BF16),
            pltpu.SemaphoreType.DMA((4,)),
        ],
        input_output_aliases={11: 0},
        compiler_params=pltpu.CompilerParams(vmem_limit_bytes=PROJECT_VMEM),
        cost_estimate=pl.CostEstimate(flops=2 * 3 * channels * 4 * channels * width,
                                      bytes_accessed=6 << 20, transcendentals=0),
        name="project",
    )(grp, *mains, *halos, weight, taps, packed)


def keep_body(message_hbm, gate_ref, taps_ref, kept_ref, part_ref, spread_ref, sem):
    channels = gate_ref.shape[0]
    per_dest = part_ref.shape[1]
    load = pltpu.make_async_copy(message_hbm.at[:, pl.ds(4 * per_dest, per_dest)], part_ref, sem)
    load.start()
    rows = 16

    def chunk(index, carry):
        row = pl.multiple_of(index * rows, rows)
        kept_ref[0, pl.ds(row, rows), :] = filtered(gate_ref[pl.ds(row, rows), :], taps_ref, row, 0).astype(BF16)
        return carry

    lax.fori_loop(0, channels // rows, chunk, 0)
    load.wait()
    spread_ref[...] = part_ref[...].astype(F32).reshape(spread_ref.shape)
    for part in range(8):
        column = spread_ref[pl.ds(part, channels, stride=8), :]
        kept_ref[1, :, part * LANES:(part + 1) * LANES] = column.astype(BF16)


def keep(message, gate_stream, taps):
    channels, width = gate_stream.shape
    shards, pieces = message.shape[:2]
    vmem = pl.BlockSpec(memory_space=pltpu.VMEM)
    return pl.pallas_call(
        keep_body,
        in_specs=[pl.BlockSpec(memory_space=pltpu.HBM), vmem, vmem],
        out_specs=vmem,
        out_shape=jax.ShapeDtypeStruct((2, channels, width - LANES), BF16),
        scratch_shapes=[
            pltpu.VMEM((shards, pieces // 5, 8, LANES), BF16),
            pltpu.VMEM((channels * 8, LANES), F32),
            pltpu.SemaphoreType.DMA,
        ],
        cost_estimate=pl.CostEstimate(flops=8 * channels * width, bytes_accessed=2 << 20, transcendentals=0),
        name="keep",
    )(message, gate_stream, taps)


def convolve_body(m_ref, wave_hbm, twist_ref, out_ref,
                  spread_ref, grid_ref, mid_ref, tall_ref, done_ref, wave_ref, sems, wave_sems):
    channels, shards, pieces, lanes = done_ref.shape
    rows_dev = pieces // 2
    freqs = twist_ref.shape[0]
    first_ref, forward_ref, backward_ref, last_ref = (wave_ref.at[i] for i in range(4))
    loads = [
        pltpu.make_async_copy(wave_hbm.at[pl.ds(i * freqs, freqs)], wave_ref.at[i], wave_sems.at[i]) for i in range(4)
    ]
    for load in loads:
        load.start()
    cosine, sine = twist_ref[:, :COLS], twist_ref[:, COLS:]

    def arrange(c):
        spread_ref[c] = m_ref[:, 4 * channels + c].astype(F32).reshape(shards * pieces, lanes)
        for a in range(rows_dev):
            for h in range(2):
                grid_ref[c, a * shards:(a + 1) * shards, h * lanes:(h + 1) * lanes] = spread_ref[
                    c, pl.ds(2 * a + h, shards, stride=pieces), :].astype(BF16)

    def rows_forward(c):
        real = jnp.dot(first_ref[:, :COLS], grid_ref[c], preferred_element_type=F32)
        return real, jnp.dot(first_ref[:, COLS:], grid_ref[c], preferred_element_type=F32)

    def twist_forward(c, wave):
        real, imag = wave
        mid_ref[c, :, :COLS] = (real * cosine + imag * sine).astype(BF16)
        mid_ref[c, :, COLS:] = (imag * cosine - real * sine).astype(BF16)

    def cols_forward(c):
        return jnp.dot(mid_ref[c], forward_ref[...], preferred_element_type=F32)

    def respond(c, freq):
        for h in range(2):
            low, high = h * lanes, COLS + h * lanes
            real, imag = freq[:, low:low + lanes], freq[:, high:high + lanes]
            h_real, h_imag = (
                m_ref[:, 4 * c + 2 * part + h].astype(F32).reshape(freqs, lanes) for part in range(2)
            )
            mid_ref[c, :, low:low + lanes] = (real * h_real - imag * h_imag).astype(BF16)
            mid_ref[c, :, high:high + lanes] = (real * h_imag + imag * h_real).astype(BF16)

    def cols_backward(c):
        return jnp.dot(mid_ref[c], backward_ref[...], preferred_element_type=F32)

    def twist_backward(c, back):
        real, imag = back[:, :COLS], back[:, COLS:]
        tall_ref[c, :freqs, :] = (real * cosine - imag * sine).astype(BF16)
        tall_ref[c, freqs:, :] = (imag * cosine + real * sine).astype(BF16)

    def rows_backward(c):
        out = jnp.dot(last_ref[:COLS, :], tall_ref[c, :freqs], preferred_element_type=F32)
        return out + jnp.dot(last_ref[COLS:, :], tall_ref[c, freqs:], preferred_element_type=F32)

    def send(c, out):
        for a in range(rows_dev):
            for h in range(2):
                spread_ref[c, pl.ds(2 * a + h, shards, stride=pieces), :] = out[
                    a * shards:(a + 1) * shards, h * lanes:(h + 1) * lanes]
        done_ref[c] = spread_ref[c].reshape(shards, pieces, lanes).astype(BF16)
        pltpu.make_async_copy(done_ref.at[c], out_ref.at[:, c], sems.at[c]).start()

    for c in range(channels):
        arrange(c)
    stages = (
        (rows_forward, twist_forward), (cols_forward, respond), (cols_backward, twist_backward), (rows_backward, send)
    )
    waiting = None
    for stage, (multiply, finish) in enumerate(stages):
        loads[stage].wait()
        for c in range(channels):
            product = multiply(c)
            if waiting is not None:
                waiting[0](*waiting[1:])
            waiting = (finish, c, product)
    waiting[0](*waiting[1:])
    for c in range(channels):
        pltpu.make_async_copy(done_ref.at[c], out_ref.at[:, c], sems.at[c]).wait()


def convolve(received, tables):
    shards, kinds, pieces, lanes = received.shape
    channels = kinds // 5
    freqs = shards * pieces
    vmem = pl.BlockSpec(memory_space=pltpu.VMEM)
    return pl.pallas_call(
        convolve_body,
        in_specs=[vmem, pl.BlockSpec(memory_space=pltpu.HBM), vmem],
        out_specs=pl.BlockSpec(memory_space=pltpu.HBM),
        out_shape=jax.ShapeDtypeStruct((shards, channels, pieces, lanes), BF16),
        scratch_shapes=[
            pltpu.VMEM((channels, shards * pieces, lanes), F32),
            pltpu.VMEM((channels, freqs // 2, COLS), BF16),
            pltpu.VMEM((channels, freqs, 2 * COLS), BF16),
            pltpu.VMEM((channels, 2 * freqs, COLS), BF16),
            pltpu.VMEM((channels, shards, pieces, lanes), BF16),
            pltpu.VMEM((4, freqs, 2 * COLS), BF16),
            pltpu.SemaphoreType.DMA((channels,)),
            pltpu.SemaphoreType.DMA((4,)),
        ],
        compiler_params=pltpu.CompilerParams(vmem_limit_bytes=CONVOLVE_VMEM),
        cost_estimate=pl.CostEstimate(flops=3 << 30, bytes_accessed=6 << 20, transcendentals=0),
        name="convolve",
    )(received, *tables)


def gated_body(y_ref, kept_hbm, bias_ref, early_ref, late_ref, spread_ref, kept_ref, sem):
    channels = early_ref.shape[0]
    load = pltpu.make_async_copy(kept_hbm, kept_ref, sem)
    load.start()
    spread_ref[...] = y_ref[...].astype(F32)
    bias = bias_ref[...]
    load.wait()
    for part in range(8):
        cols = slice(part * LANES, (part + 1) * LANES)
        y = spread_ref[pl.ds(part, channels, stride=8), :]
        direct = bias * kept_ref[1, :, cols].astype(F32)
        out_ref, at = (early_ref, part) if part < 4 else (late_ref, part - 4)
        value = kept_ref[0, :, cols].astype(F32) * (y + direct)
        out_ref[:, at * LANES:(at + 1) * LANES] = value.astype(BF16)


def gated(y, kept, bias):
    vmem = pl.BlockSpec(memory_space=pltpu.VMEM)
    return pl.pallas_call(
        gated_body,
        in_specs=[vmem, pl.BlockSpec(memory_space=pltpu.HBM), vmem],
        out_specs=[vmem] * 2,
        out_shape=[jax.ShapeDtypeStruct((kept.shape[1], kept.shape[2] // 2), BF16)] * 2,
        scratch_shapes=[
            pltpu.VMEM(y.shape, F32),
            pltpu.VMEM(kept.shape, BF16),
            pltpu.SemaphoreType.DMA,
        ],
        compiler_params=pltpu.CompilerParams(vmem_limit_bytes=GATED_VMEM),
        cost_estimate=pl.CostEstimate(flops=4 * y.size, bytes_accessed=8 * y.size, transcendentals=0),
        name="gated",
    )(y, kept, bias)


def mixed_body(*refs):
    values, weights, out_ref = refs[:4], refs[4:8], refs[-1]
    total = jnp.dot(weights[0][...], values[0][...], preferred_element_type=F32)
    for w, v in zip(weights[1:], values[1:]):
        total = total + jnp.dot(w[...], v[...], preferred_element_type=F32)
    out_ref[...] = total.astype(BF16)


def mixed(values, weights, half, *earlier):
    channels, tok = values[0].shape
    whole = [pl.BlockSpec(memory_space=pltpu.VMEM)] * 8
    return pl.pallas_call(
        mixed_body,
        grid=(1,),
        in_specs=whole + [pl.BlockSpec(memory_space=pl.ANY)] * len(earlier),
        out_specs=pl.BlockSpec((weights[0].shape[0], tok), lambda i: (0, half)),
        out_shape=jax.ShapeDtypeStruct((weights[0].shape[0], 2 * tok), BF16),
        input_output_aliases={8: 0} if earlier else {},
        compiler_params=pltpu.CompilerParams(vmem_limit_bytes=MIXED_VMEM),
        cost_estimate=pl.CostEstimate(flops=8 * channels * channels * tok, bytes_accessed=2 << 20, transcendentals=0),
        name="mixed",
    )(*values, *weights, *earlier)


def swapped(block, mask):
    return lax.ppermute(block, "grp", [(i, i ^ mask) for i in range(4)])


def shards(tokens, in_weight, short_weight, filter_bias, spectra, out_weight):
    shard_count = lax.axis_size("seq")
    grp = lax.axis_index("grp")
    channels, tok = tokens.shape
    per_dest = channels // shard_count

    far = swapped(tokens, 2)
    near = swapped(tokens, 1)
    route = [(i, i + 1) for i in range(shard_count - 1)]
    halo = lax.ppermute(tokens[:, -LANES:], "seq", route)
    packed = pack_spectra(spectra, shard_count)
    halo, packed = lax.optimization_barrier((halo, packed))
    halo_far = swapped(halo, 2)
    halo_near = swapped(halo, 1)
    taps = jnp.transpose(short_weight, (2, 0, 1)).reshape(channels, 9)
    far, halo_far, halo_near, near, taps = lax.optimization_barrier((far, halo_far, halo_near, near, taps))
    mains = [tokens, far, near, swapped(far, 1)]
    halos = [halo, halo_far, halo_near, swapped(halo_far, 1)]
    message, gate_stream = project(
        grp.reshape(1).astype(jnp.int32), mains, halos, in_weight.reshape(3 * channels, -1), taps, packed
    )
    message, out_weight, filter_bias, later, gate_stream = lax.optimization_barrier(
        (message, out_weight, filter_bias, grp, gate_stream)
    )
    kept = keep(message, gate_stream, taps)
    received = lax.all_to_all(message, "seq", 0, 0, tiled=True)

    turned = out_weight.T
    parts = [
        lax.dynamic_slice_in_dim(turned, (later ^ mask) * channels, channels, 0) for mask in MASKS
    ]
    weights = [parts[0]] + [swapped(part, mask) for part, mask in zip(parts[1:], MASKS[1:])]
    zero = jnp.minimum(later, 0)
    tables = [t + zero.astype(t.dtype) for t in transform_tables(shard_count, tok // COLS)]
    bias = filter_bias[:, None] + zero.astype(F32)
    received, weights, tables, bias, kept = lax.optimization_barrier((received, weights, tables, bias, kept))

    result = convolve(received, tables)
    back = lax.all_to_all(result, "seq", 0, 0, tiled=True).reshape(channels * 8, LANES)
    early, late = gated(back, kept, bias)
    far_early, far_late = swapped(early, 2), swapped(late, 2)
    near_early, near_late = swapped(early, 1), swapped(late, 1)
    out = mixed((early, far_early, near_early, swapped(far_early, 1)), weights, 0)
    return mixed((late, far_late, near_late, swapped(far_late, 1)), weights, 1, out)


def solution(mesh):
    in_specs = (
        P("grp", "seq"),
        P(None, "grp", None),
        P(None, None, "grp"),
        P("grp"),
        P(None, "grp", "seq", None),
        P("grp", None),
    )
    out_specs = P("grp", "seq")
    return jax.shard_map(shards, mesh=mesh, in_specs=in_specs, out_specs=out_specs, check_vma=False)
```

```python
import math

import jax
import jax.numpy as jnp
import numpy as np
from jax import lax
from jax.experimental import pallas as pl
from jax.experimental.pallas import tpu as pltpu
from jax.sharding import PartitionSpec as P

COLS = 256
FREQS = 512
LANES = 128
PROJECT_VMEM = 51500 << 10
GATED_VMEM = 54000 << 10
MIXED_VMEM = 12 << 20
CONVOLVE_VMEM = 50000 << 10
MASKS = (0, 2, 1, 3)
BF16 = jnp.bfloat16
F32 = jnp.float32


def unit_circle(rows, cols, period):
    angle = (np.outer(rows, cols) % period) * (2.0 * math.pi / period)
    return np.cos(angle), np.sin(angle)


def transform_tables(shard_count, rows_dev):
    half = shard_count * rows_dev
    order = (np.arange(shard_count)[None, :] * rows_dev + np.arange(rows_dev)[:, None]).reshape(-1)
    freqs = np.arange(2 * half)
    cols = np.arange(COLS)
    padded = 2 * half * COLS
    cos1, sin1 = unit_circle(freqs, order, 2 * half)
    cos2, sin2 = unit_circle(cols, cols, COLS)
    cost, sint = unit_circle(freqs, cols, padded)
    first = np.concatenate([cos1, -sin1], 1)
    forward = np.block([[cos2, -sin2], [sin2, cos2]])
    backward = np.block([[cos2, sin2], [-sin2, cos2]])
    last = np.concatenate([cos1.T, -sin1.T], 0) / padded
    waves = np.concatenate([first, forward, backward, last], 0)
    return jnp.asarray(waves, BF16), jnp.asarray(np.concatenate([cost, sint], 1), F32)


def pack_spectra_body(spec_ref, out_ref):
    dests = out_ref.shape[0]
    per_dest = spec_ref.shape[1] // dests
    for part in range(2):
        for h in range(2):
            piece = spec_ref[part, :, :, h * LANES:(h + 1) * LANES]
            piece = piece.reshape(dests, per_dest, *piece.shape[1:]).astype(BF16)
            for c in range(per_dest):
                out_ref[:, 4 * c + 2 * part + h] = piece[:, c]


def pack_spectra(spectra, shard_count):
    _, channels, rows, cols = spectra.shape
    per_dest = channels // shard_count
    steps = 2
    return pl.pallas_call(
        pack_spectra_body,
        grid=(steps,),
        in_specs=[pl.BlockSpec((2, channels // steps, rows, cols), lambda i: (0, i, 0, 0))],
        out_specs=pl.BlockSpec((shard_count // steps, 4 * per_dest, rows, LANES), lambda i: (i, 0, 0, 0)),
        out_shape=jax.ShapeDtypeStruct((shard_count, 5 * per_dest, rows, LANES), BF16),
        cost_estimate=pl.CostEstimate(flops=0, bytes_accessed=6 * spectra.size, transcendentals=0),
        name="pack_spectra",
    )(spectra)


def filtered(stream, taps_ref, row, s):
    x = stream.astype(F32)
    w = [taps_ref[pl.ds(row, x.shape[0]), 3 * tap + s:3 * tap + s + 1] for tap in range(3)]
    y = w[0] * x + w[1] * pltpu.roll(x, 1, 1) + w[2] * pltpu.roll(x, 2, 1)
    return y[:, LANES:]


def project_body(*refs):
    grp_ref, mains, halos, weight_ref, taps_ref = refs[0], refs[1:5], refs[5:9], refs[9], refs[10]
    message_ref, gate_ref, token_ref, stream_ref, spread_ref, part_ref, sem = refs[12:]
    channels, tok = mains[0].shape
    width = tok + LANES
    grp = grp_ref[0]
    for mask, main, halo in zip(MASKS, mains, halos):
        rows = pl.ds(pl.multiple_of((grp ^ mask) * channels, 64), channels)
        token_ref[rows, :LANES] = halo[...]
        token_ref[rows, LANES:] = main[...]
    step = 384
    for col in range(0, width, step):
        stream_ref[:, col:col + step] = jnp.dot(
            weight_ref[...], token_ref[:, col:col + step], preferred_element_type=F32
        )
    rows = 16

    def chunk(index, carry):
        row = pl.multiple_of(index * rows, rows)
        gate_ref[pl.ds(row, rows), :] = stream_ref[pl.ds(row, rows), :].astype(BF16)
        first, second = (
            filtered(stream_ref[pl.ds(s * channels + row, rows), :].astype(BF16), taps_ref, row, s) for s in (1, 2)
        )
        signal = second * first
        for part in range(8):
            spread_ref[pl.ds(row * 8 + part, rows, stride=8), :] = signal[:, part * LANES:(part + 1) * LANES]
        return carry

    shards, per_dest = part_ref.shape[:2]
    groups = 4
    each = channels // groups
    copies = []
    for group in range(groups):
        lax.fori_loop(group * each // rows, (group + 1) * each // rows, chunk, 0)
        dests = pl.ds(group * shards // groups, shards // groups)
        ready = spread_ref[pl.ds(group * each * 8, each * 8), :].astype(BF16)
        part_ref[dests] = ready.reshape(shards // groups, *part_ref.shape[1:])
        copies.append(pltpu.make_async_copy(
            part_ref.at[dests], message_ref.at[dests, pl.ds(4 * per_dest, per_dest)], sem.at[group]
        ))
        copies[-1].start()
    for copy in copies:
        copy.wait()


def project(grp, mains, halos, weight, taps, packed):
    channels, tok = mains[0].shape
    width = tok + LANES
    vmem = pl.BlockSpec(memory_space=pltpu.VMEM)
    anywhere = pl.BlockSpec(memory_space=pltpu.HBM)
    shards, pieces = packed.shape[:2]
    return pl.pallas_call(
        project_body,
        in_specs=[pl.BlockSpec(memory_space=pltpu.SMEM)] + [vmem] * 10 + [anywhere],
        out_specs=[anywhere, vmem],
        out_shape=[
            jax.ShapeDtypeStruct(packed.shape, BF16),
            jax.ShapeDtypeStruct((channels, width), BF16),
        ],
        scratch_shapes=[
            pltpu.VMEM((4 * channels, width), BF16),
            pltpu.VMEM((3 * channels, width), F32),
            pltpu.VMEM((channels * 8, LANES), F32),
            pltpu.VMEM((shards, pieces // 5, 8, LANES), BF16),
            pltpu.SemaphoreType.DMA((4,)),
        ],
        input_output_aliases={11: 0},
        compiler_params=pltpu.CompilerParams(vmem_limit_bytes=PROJECT_VMEM),
        cost_estimate=pl.CostEstimate(flops=2 * 3 * channels * 4 * channels * width,
                                      bytes_accessed=6 << 20, transcendentals=0),
        name="project",
    )(grp, *mains, *halos, weight, taps, packed)


def keep_body(message_hbm, gate_ref, taps_ref, kept_ref, part_ref, spread_ref, sem):
    channels = gate_ref.shape[0]
    per_dest = part_ref.shape[1]
    load = pltpu.make_async_copy(message_hbm.at[:, pl.ds(4 * per_dest, per_dest)], part_ref, sem)
    load.start()
    rows = 16

    def chunk(index, carry):
        row = pl.multiple_of(index * rows, rows)
        kept_ref[0, pl.ds(row, rows), :] = filtered(gate_ref[pl.ds(row, rows), :], taps_ref, row, 0).astype(BF16)
        return carry

    lax.fori_loop(0, channels // rows, chunk, 0)
    load.wait()
    spread_ref[...] = part_ref[...].astype(F32).reshape(spread_ref.shape)
    for part in range(8):
        column = spread_ref[pl.ds(part, channels, stride=8), :]
        kept_ref[1, :, part * LANES:(part + 1) * LANES] = column.astype(BF16)


def keep(message, gate_stream, taps):
    channels, width = gate_stream.shape
    shards, pieces = message.shape[:2]
    vmem = pl.BlockSpec(memory_space=pltpu.VMEM)
    return pl.pallas_call(
        keep_body,
        in_specs=[pl.BlockSpec(memory_space=pltpu.HBM), vmem, vmem],
        out_specs=vmem,
        out_shape=jax.ShapeDtypeStruct((2, channels, width - LANES), BF16),
        scratch_shapes=[
            pltpu.VMEM((shards, pieces // 5, 8, LANES), BF16),
            pltpu.VMEM((channels * 8, LANES), F32),
            pltpu.SemaphoreType.DMA,
        ],
        cost_estimate=pl.CostEstimate(flops=8 * channels * width, bytes_accessed=2 << 20, transcendentals=0),
        name="keep",
    )(message, gate_stream, taps)


def convolve_body(m_ref, wave_hbm, twist_ref, out_ref,
                  spread_ref, grid_ref, mid_ref, tall_ref, done_ref, wave_ref, sems, wave_sems):
    channels, shards, pieces, lanes = done_ref.shape
    rows_dev = pieces // 2
    freqs = twist_ref.shape[0]
    first_ref, forward_ref, _, last_ref = (wave_ref.at[i] for i in range(4))
    loads = [
        pltpu.make_async_copy(wave_hbm.at[pl.ds(i * freqs, freqs)], wave_ref.at[i], wave_sems.at[i]) for i in range(4)
    ]
    for i in (0, 1, 3):
        loads[i].start()
    cosine, sine = twist_ref[:, :COLS], twist_ref[:, COLS:]

    def arrange(c):
        spread_ref[c] = m_ref[:, 4 * channels + c].astype(F32).reshape(shards * pieces, lanes)
        for a in range(rows_dev):
            for h in range(2):
                grid_ref[c, a * shards:(a + 1) * shards, h * lanes:(h + 1) * lanes] = spread_ref[
                    c, pl.ds(2 * a + h, shards, stride=pieces), :].astype(BF16)

    def rows_forward(c):
        real = jnp.dot(first_ref[:, :COLS], grid_ref[c], preferred_element_type=F32)
        return real, jnp.dot(first_ref[:, COLS:], grid_ref[c], preferred_element_type=F32)

    def twist_forward(c, wave):
        real, imag = wave
        mid_ref[c, :, :COLS] = (real * cosine + imag * sine).astype(BF16)
        mid_ref[c, :, COLS:] = (imag * cosine - real * sine).astype(BF16)

    def cols_forward(c):
        return jnp.dot(mid_ref[c], forward_ref[...], preferred_element_type=F32)

    def respond(c, freq):
        for h in range(2):
            low, high = h * lanes, COLS + h * lanes
            real, imag = freq[:, low:low + lanes], freq[:, high:high + lanes]
            h_real, h_imag = (
                m_ref[:, 4 * c + 2 * part + h].astype(F32).reshape(freqs, lanes) for part in range(2)
            )
            mid_ref[c, :, low:low + lanes] = (real * h_real - imag * h_imag).astype(BF16)
            mid_ref[c, :, high:high + lanes] = (-(real * h_imag) - imag * h_real).astype(BF16)

    def cols_backward(c):
        return jnp.dot(mid_ref[c], forward_ref[...], preferred_element_type=F32)

    def twist_backward(c, back):
        real, minus = back[:, :COLS], back[:, COLS:]
        tall_ref[c, :freqs, :] = (real * cosine + minus * sine).astype(BF16)
        tall_ref[c, freqs:, :] = (real * sine - minus * cosine).astype(BF16)

    def rows_backward(c):
        out = jnp.dot(last_ref[:COLS, :], tall_ref[c, :freqs], preferred_element_type=F32)
        return out + jnp.dot(last_ref[COLS:, :], tall_ref[c, freqs:], preferred_element_type=F32)

    def send(c, out):
        for a in range(rows_dev):
            for h in range(2):
                spread_ref[c, pl.ds(2 * a + h, shards, stride=pieces), :] = out[
                    a * shards:(a + 1) * shards, h * lanes:(h + 1) * lanes]
        done_ref[c] = spread_ref[c].reshape(shards, pieces, lanes).astype(BF16)
        pltpu.make_async_copy(done_ref.at[c], out_ref.at[:, c], sems.at[c]).start()

    for c in range(channels):
        arrange(c)
    stages = (
        (rows_forward, twist_forward), (cols_forward, respond), (cols_backward, twist_backward), (rows_backward, send)
    )
    waiting = None
    for stage, (multiply, finish) in enumerate(stages):
        if stage != 2:
            loads[stage].wait()
        for c in range(channels):
            product = multiply(c)
            if waiting is not None:
                waiting[0](*waiting[1:])
            waiting = (finish, c, product)
    waiting[0](*waiting[1:])
    for c in range(channels):
        pltpu.make_async_copy(done_ref.at[c], out_ref.at[:, c], sems.at[c]).wait()


def convolve(received, tables):
    shards, kinds, pieces, lanes = received.shape
    channels = kinds // 5
    freqs = shards * pieces
    vmem = pl.BlockSpec(memory_space=pltpu.VMEM)
    return pl.pallas_call(
        convolve_body,
        in_specs=[vmem, pl.BlockSpec(memory_space=pltpu.HBM), vmem],
        out_specs=pl.BlockSpec(memory_space=pltpu.HBM),
        out_shape=jax.ShapeDtypeStruct((shards, channels, pieces, lanes), BF16),
        scratch_shapes=[
            pltpu.VMEM((channels, shards * pieces, lanes), F32),
            pltpu.VMEM((channels, freqs // 2, COLS), BF16),
            pltpu.VMEM((channels, freqs, 2 * COLS), BF16),
            pltpu.VMEM((channels, 2 * freqs, COLS), BF16),
            pltpu.VMEM((channels, shards, pieces, lanes), BF16),
            pltpu.VMEM((4, freqs, 2 * COLS), BF16),
            pltpu.SemaphoreType.DMA((channels,)),
            pltpu.SemaphoreType.DMA((4,)),
        ],
        compiler_params=pltpu.CompilerParams(vmem_limit_bytes=CONVOLVE_VMEM),
        cost_estimate=pl.CostEstimate(flops=3 << 30, bytes_accessed=6 << 20, transcendentals=0),
        name="convolve",
    )(received, *tables)


def gated_body(y_ref, kept_hbm, bias_ref, early_ref, late_ref, spread_ref, kept_ref, sem):
    channels = early_ref.shape[0]
    load = pltpu.make_async_copy(kept_hbm, kept_ref, sem)
    load.start()
    spread_ref[...] = y_ref[...].astype(F32)
    bias = bias_ref[...]
    load.wait()
    for part in range(8):
        cols = slice(part * LANES, (part + 1) * LANES)
        y = spread_ref[pl.ds(part, channels, stride=8), :]
        direct = bias * kept_ref[1, :, cols].astype(F32)
        out_ref, at = (early_ref, part) if part < 4 else (late_ref, part - 4)
        value = kept_ref[0, :, cols].astype(F32) * (y + direct)
        out_ref[:, at * LANES:(at + 1) * LANES] = value.astype(BF16)


def gated(y, kept, bias):
    vmem = pl.BlockSpec(memory_space=pltpu.VMEM)
    return pl.pallas_call(
        gated_body,
        in_specs=[vmem, pl.BlockSpec(memory_space=pltpu.HBM), vmem],
        out_specs=[vmem] * 2,
        out_shape=[jax.ShapeDtypeStruct((kept.shape[1], kept.shape[2] // 2), BF16)] * 2,
        scratch_shapes=[
            pltpu.VMEM(y.shape, F32),
            pltpu.VMEM(kept.shape, BF16),
            pltpu.SemaphoreType.DMA,
        ],
        compiler_params=pltpu.CompilerParams(vmem_limit_bytes=GATED_VMEM),
        cost_estimate=pl.CostEstimate(flops=4 * y.size, bytes_accessed=8 * y.size, transcendentals=0),
        name="gated",
    )(y, kept, bias)


def mixed_body(*refs):
    values, weights, out_ref = refs[:4], refs[4:8], refs[-1]
    total = jnp.dot(weights[0][...], values[0][...], preferred_element_type=F32)
    for w, v in zip(weights[1:], values[1:]):
        total = total + jnp.dot(w[...], v[...], preferred_element_type=F32)
    out_ref[...] = total.astype(BF16)


def mixed(values, weights, half, *earlier):
    channels, tok = values[0].shape
    whole = [pl.BlockSpec(memory_space=pltpu.VMEM)] * 8
    return pl.pallas_call(
        mixed_body,
        grid=(1,),
        in_specs=whole + [pl.BlockSpec(memory_space=pl.ANY)] * len(earlier),
        out_specs=pl.BlockSpec((weights[0].shape[0], tok), lambda i: (0, half)),
        out_shape=jax.ShapeDtypeStruct((weights[0].shape[0], 2 * tok), BF16),
        input_output_aliases={8: 0} if earlier else {},
        compiler_params=pltpu.CompilerParams(vmem_limit_bytes=MIXED_VMEM),
        cost_estimate=pl.CostEstimate(flops=8 * channels * channels * tok, bytes_accessed=2 << 20, transcendentals=0),
        name="mixed",
    )(*values, *weights, *earlier)


def swapped(block, mask):
    return lax.ppermute(block, "grp", [(i, i ^ mask) for i in range(4)])


def shards(tokens, in_weight, short_weight, filter_bias, spectra, out_weight):
    shard_count = lax.axis_size("seq")
    grp = lax.axis_index("grp")
    channels, tok = tokens.shape
    per_dest = channels // shard_count

    far = swapped(tokens, 2)
    near = swapped(tokens, 1)
    route = [(i, i + 1) for i in range(shard_count - 1)]
    halo = lax.ppermute(tokens[:, -LANES:], "seq", route)
    packed = pack_spectra(spectra, shard_count)
    halo, packed = lax.optimization_barrier((halo, packed))
    halo_far = swapped(halo, 2)
    halo_near = swapped(halo, 1)
    taps = jnp.transpose(short_weight, (2, 0, 1)).reshape(channels, 9)
    far, halo_far, halo_near, near, taps = lax.optimization_barrier((far, halo_far, halo_near, near, taps))
    mains = [tokens, far, near, swapped(far, 1)]
    halos = [halo, halo_far, halo_near, swapped(halo_far, 1)]
    message, gate_stream = project(
        grp.reshape(1).astype(jnp.int32), mains, halos, in_weight.reshape(3 * channels, -1), taps, packed
    )
    message, out_weight, filter_bias, later, gate_stream = lax.optimization_barrier(
        (message, out_weight, filter_bias, grp, gate_stream)
    )
    kept = keep(message, gate_stream, taps)
    received = lax.all_to_all(message, "seq", 0, 0, tiled=True)

    turned = out_weight.T
    parts = [
        lax.dynamic_slice_in_dim(turned, (later ^ mask) * channels, channels, 0) for mask in MASKS
    ]
    weights = [parts[0]] + [swapped(part, mask) for part, mask in zip(parts[1:], MASKS[1:])]
    zero = jnp.minimum(later, 0)
    tables = [t + zero.astype(t.dtype) for t in transform_tables(shard_count, tok // COLS)]
    bias = filter_bias[:, None] + zero.astype(F32)
    received, weights, tables, bias, kept = lax.optimization_barrier((received, weights, tables, bias, kept))

    result = convolve(received, tables)
    back = lax.all_to_all(result, "seq", 0, 0, tiled=True).reshape(channels * 8, LANES)
    early, late = gated(back, kept, bias)
    far_early, far_late = swapped(early, 2), swapped(late, 2)
    near_early, near_late = swapped(early, 1), swapped(late, 1)
    out = mixed((early, far_early, near_early, swapped(far_early, 1)), weights, 0)
    return mixed((late, far_late, near_late, swapped(far_late, 1)), weights, 1, out)


def solution(mesh):
    in_specs = (
        P("grp", "seq"),
        P(None, "grp", None),
        P(None, None, "grp"),
        P("grp"),
        P(None, "grp", "seq", None),
        P("grp", None),
    )
    out_specs = P("grp", "seq")
    return jax.shard_map(shards, mesh=mesh, in_specs=in_specs, out_specs=out_specs, check_vma=False)
```
